128 devices in a mesh: section: 2 (over y_lo), dp: 16 (over x, z), tensor: 4 (over y_hi, core).
Axes of the slice: x: 4, y: 4 (y_hi: 2, y_lo: 2; y = y_hi * 2 + y_lo), z: 4, core: 2. Of those that a mesh axis runs over, the one named last changes fastest.
Arguments:
- embedded: bfloat16 [2, 2, 4096, 1024], P('section', None, ('dp', 'tensor')), may hold values from -6 to 6
- cotangent: bfloat16 [2, 2, 4096, 1024], P('section', None, ('dp', 'tensor')), may hold values from -6 to 6
- lengths: int32 [2, 2, 16, 8], P(None, None, 'dp'), may hold values from 1 to 194, 256 in all within a row
- attn_qkv: bfloat16 [2, 1024, 3072], P('section', 'dp', 'tensor'), may hold values from -0.1875 to 0.1875
- attn_out: bfloat16 [2, 1024, 1024], P('section', 'tensor', 'dp'), may hold values from -0.75 to 0.75
- ffn_up: bfloat16 [2, 1024, 4096], P('section', 'dp', 'tensor'), may hold values from -0.1875 to 0.1875
- ffn_down: bfloat16 [2, 4096, 1024], P('section', 'tensor', 'dp'), may hold values from -0.1875 to 0.1875
- norm_gain: bfloat16 [2, 3, 1024], P('section', None, 'dp'), may hold values from 0.5 to 1.5
- norm_bias: bfloat16 [2, 3, 1024], P('section', None, 'dp'), may hold values from -0.5 to 0.5
- cross_query: bfloat16 [1024, 1024], P(('section', 'dp'), 'tensor'), may hold values from -0.1875 to 0.1875
- cross_kv: bfloat16 [1024, 2048], P(('section', 'dp'), 'tensor'), may hold values from -0.1875 to 0.1875
- cross_out: bfloat16 [1024, 1024], P('tensor', ('section', 'dp')), may hold values from -0.75 to 0.75
Outputs:
- outputs: bfloat16 [2, 2, 4096, 1024], P('section', None, ('dp', 'tensor'))
- g_embedded: float32 [2, 2, 4096, 1024], P('section', None, ('dp', 'tensor'))
- g_attn_qkv: float32 [2, 1024, 3072], P('section', 'dp', 'tensor')
- g_attn_out: float32 [2, 1024, 1024], P('section', 'tensor', 'dp')
- g_ffn_up: float32 [2, 1024, 4096], P('section', 'dp', 'tensor')
- g_ffn_down: float32 [2, 4096, 1024], P('section', 'tensor', 'dp')
- g_norm_gain: float32 [2, 3, 1024], P('section', None, 'dp')
- g_norm_bias: float32 [2, 3, 1024], P('section', None, 'dp')
- g_cross_query: float32 [1024, 1024], P(('section', 'dp'), 'tensor')
- g_cross_kv: float32 [1024, 2048], P(('section', 'dp'), 'tensor')
- g_cross_out: float32 [1024, 1024], P('tensor', ('section', 'dp'))
The draws below stay inside these ranges and needn't reach their ends.
Inputs may be any that keep to these rules, and one draw needn't show every extreme that they name: The 8 pair lengths of each row sum to 256, and every row has one pair of exactly 194 tokens.
All inputs are finite; a program needn't handle non-finite values.
Results may differ from the reference program's by a relative error of at most 0.02.
Values may be sent and summed in bfloat16 or wider, within the bound.
No kernel may reach another device: no remote copies, remote signals or barrier semaphores. Data moves between devices by JAX's collectives and lax.ppermute only.
A program may use at most 128 MiB of HBM per device.

```python
import math
import jax
import jax.numpy as jnp
import numpy as np
from jax import lax

D = 1024
HEADS = 16
HEAD_DIM = 64
FF = 4096
ROW_LEN = 256
MICRO = 2
PAIRS = 8
MOST = 194
TOKENS = 4096
N_DP = 16


def shard_levels(rng, dims, pieces, low, top_value):
    level, own = 1.0, jax.random.fold_in(rng, 6)
    for dim, blocks in pieces:
        steps = jnp.exp(jax.random.uniform(jax.random.fold_in(own, dim), (blocks,), jnp.float32, low / len(pieces), top_value / len(pieces)))
        level = level * jnp.repeat(steps, dims[dim] // blocks).reshape([-1 if axis == dim else 1 for axis in range(len(dims))])
    return level


def length_profile(count, total, limit, skew):
    weights = [(1 << 20) // math.isqrt(grade ** skew) + 1 for grade in range(2, count + 1)]
    spare, counts = total - limit - (count - 1), [1] * (count - 1)
    while spare > 0:
        candidates = [i for i in range(count - 1) if counts[i] < limit]
        pool, remaining = sum([weights[i] for i in candidates]), spare
        for i in candidates:
            more = min(limit - counts[i], max(1, remaining * weights[i] // pool), spare)
            counts[i] = counts[i] + more
            spare = spare - more
    return np.array([limit] + counts)


def ragged_sizes(key, number_of, total, reach, skew):
    if number_of == 2:
        one = jax.random.randint(key, (), max(1, total - reach), min(reach, total - 1) + 1)
        return jnp.stack([one, total - one])
    sizes = jnp.asarray(length_profile(number_of, total, reach, skew), jnp.int32)
    couples = (number_of - 1) // 2
    source_of, receiver = sizes[1:1 + 2 * couples:2], sizes[2:2 + 2 * couples:2]
    margin = jnp.minimum(source_of - 1, reach - receiver)
    shifted = jax.random.randint(jax.random.fold_in(key, 1), (couples,), 0, 1 << 20) % (margin + 1)
    sizes = sizes.at[1:1 + 2 * couples:2].set(source_of - shifted).at[2:2 + 2 * couples:2].set(receiver + shifted)
    return sizes[jax.random.permutation(jax.random.fold_in(key, 2), number_of)]


def gaussian(key, dims, width, reach, cuts=(), kind=jnp.bfloat16):
    values = width * jax.random.normal(key, dims, jnp.float32)
    if cuts:
        values = values * shard_levels(key, dims, cuts, -0.22, 0.18)
    return jnp.clip(values, -reach, reach).astype(kind)


def setup_inputs(seed: int = 0) -> dict:
    seeds = jax.random.split(jax.random.key(seed), 13)
    embedded = gaussian(seeds[0], (2, MICRO, TOKENS, D), 1.0, 6.0, ((0, 2), (2, 64)))
    cotangent = gaussian(seeds[1], (2, MICRO, TOKENS, D), 1.0, 6.0, ((0, 2), (2, 64)))
    lengths = jax.vmap(lambda own: ragged_sizes(own, PAIRS, ROW_LEN, MOST, 2))(jax.random.split(seeds[2], 2 * MICRO * N_DP)).reshape((2, MICRO, N_DP, PAIRS)).astype(jnp.int32)
    attn_qkv = gaussian(seeds[3], (2, D, 3 * D), D ** -0.5, 0.1875, ((0, 2), (1, 16), (2, 4)))
    attn_out = gaussian(seeds[4], (2, D, D), (D // 16) ** -0.5, 0.75, ((0, 2), (1, 4), (2, 16)))
    ffn_up = gaussian(seeds[5], (2, D, FF), D ** -0.5, 0.1875, ((0, 2), (1, 16), (2, 4)))
    ffn_down = gaussian(seeds[6], (2, FF, D), (FF // 4) ** -0.5, 0.1875, ((0, 2), (1, 4), (2, 16)))
    norm_gain = jnp.clip(1.0 + 0.1 * jax.random.normal(seeds[7], (2, 3, D), jnp.float32), 0.5, 1.5).astype(jnp.bfloat16)
    norm_bias = jnp.clip(jax.random.uniform(seeds[8], (2, 3, D), jnp.float32, -0.5, 0.5) * shard_levels(seeds[8], (2, 3, D), ((0, 2), (2, 16)), -0.4, 0.0), -0.5, 0.5).astype(jnp.bfloat16)
    cross_query = gaussian(seeds[9], (D, D), D ** -0.5, 0.1875, ((0, 32), (1, 4)))
    cross_kv = gaussian(seeds[10], (D, 2 * D), D ** -0.5, 0.1875, ((0, 32), (1, 4)))
    cross_out = gaussian(seeds[11], (D, D), (D // 16) ** -0.5, 0.75, ((0, 4), (1, 32)))
    return {"embedded": embedded, "cotangent": cotangent, "lengths": lengths, "attn_qkv": attn_qkv, "attn_out": attn_out, "ffn_up": ffn_up, "ffn_down": ffn_down, "norm_gain": norm_gain, "norm_bias": norm_bias, "cross_query": cross_query, "cross_kv": cross_kv, "cross_out": cross_out}


EPSILON = 1e-05
NEGATIVE = -1000000000.0
SCALING = 0.125
GELU_COEF = 0.7978845608028654
HIGHEST = lax.Precision.HIGHEST

@jax.custom_vjp
def low(v):
    return lax.optimization_barrier(v.astype(jnp.bfloat16)).astype(jnp.float32)

@jax.custom_vjp
def low_back(v):
    return v

def low_keep(v):
    return (low(v), None)

def low_pass(kept, grad):
    return (grad,)

def back_keep(v):
    return (v, None)

def back_low(kept, grad):
    return (low(grad),)
low.defvjp(low_keep, low_pass)
low_back.defvjp(back_keep, back_low)

def gelu_tanh(values):
    return 0.5 * values * (1.0 + jnp.tanh(GELU_COEF * (values + 0.044715 * values * values * values)))

def layer_norm(values, gain, offset):
    centred = values - lax.optimization_barrier(jnp.mean(values, axis=-1, keepdims=True))
    inverse = lax.rsqrt(lax.optimization_barrier(jnp.mean(centred * centred, axis=-1, keepdims=True)) + EPSILON)
    return centred * inverse * gain + offset

def multiply(left, right):
    return jnp.dot(left, right, precision=HIGHEST)

def segment_ids(lengths_row):
    ends = jnp.cumsum(lengths_row)
    positions = jnp.arange(ROW_LEN, dtype=jnp.int32)
    return lax.optimization_barrier(jnp.sum((positions[:, None] >= ends[None, :]).astype(jnp.int32), axis=1))

def attend(query_heads, key_heads, value_heads, allowed):
    raw = jnp.einsum('qhd,khd->hqk', query_heads, key_heads, precision=HIGHEST) * SCALING
    scores = jnp.where(allowed[None], low_back(raw), NEGATIVE)
    highest = lax.optimization_barrier(jnp.max(scores, axis=-1, keepdims=True))
    expo_scores = jnp.exp(scores - highest)
    weights_full = expo_scores / lax.optimization_barrier(jnp.sum(expo_scores, axis=-1, keepdims=True))
    mixed = jnp.einsum('hqk,khd->qhd', low(weights_full), value_heads, precision=HIGHEST)
    return low(low_back(mixed.reshape(mixed.shape[0], -1)))

def encode_decode(weights, source, target, source_pair, target_pair):
    w_qkv, w_out, w_up, w_down, gains, offsets, w_query, w_keyval, w_cross = weights
    positions = jnp.arange(ROW_LEN, dtype=jnp.int32)
    encoder_mask = source_pair[:, None] == source_pair[None, :]
    decoder_mask = (target_pair[:, None] == target_pair[None, :]) & (positions[None, :] <= positions[:, None])
    cross_mask = target_pair[:, None] == source_pair[None, :]

    def self_block(values, section_index, allowed):
        normed = low(layer_norm(values, gains[section_index, 0], offsets[section_index, 0]))
        projected = low(low_back(multiply(normed, w_qkv[section_index])))
        heads = projected.reshape(ROW_LEN, HEADS, 3, HEAD_DIM)
        mixed = attend(heads[:, :, 0], heads[:, :, 1], heads[:, :, 2], allowed)
        return values + low_back(multiply(mixed, w_out[section_index]))

    def ffn_block(values, section_index):
        normed = low(layer_norm(values, gains[section_index, 2], offsets[section_index, 2]))
        hidden = low_back(multiply(normed, w_up[section_index]))
        return values + low_back(multiply(low(gelu_tanh(hidden)), w_down[section_index]))
    encoded = ffn_block(self_block(source, 0, encoder_mask), 0)
    memory = low(layer_norm(encoded, gains[0, 1], offsets[0, 1]))
    decoded = self_block(target, 1, decoder_mask)
    normed = low(layer_norm(decoded, gains[1, 1], offsets[1, 1]))
    queries = low(low_back(multiply(normed, w_query))).reshape(ROW_LEN, HEADS, HEAD_DIM)
    keyvals = low(low_back(multiply(memory, w_keyval))).reshape(ROW_LEN, HEADS, 2, HEAD_DIM)
    mixed = attend(queries, keyvals[:, :, 0], keyvals[:, :, 1], cross_mask)
    decoded = decoded + low_back(multiply(mixed, w_cross))
    decoded = ffn_block(decoded, 1)
    return (memory, decoded)

def forward(weights, embedded, pairs):
    rows_total = MICRO * N_DP
    source = embedded[0].reshape(rows_total, ROW_LEN, D)
    target = embedded[1].reshape(rows_total, ROW_LEN, D)

    def row_step(carry, inputs):
        source_row, target_row, source_pair, target_pair = inputs
        memory, decoded = jax.checkpoint(lambda a_row, b_row, c_row, d_row: encode_decode(weights, a_row, b_row, c_row, d_row))(source_row, target_row, source_pair, target_pair)
        return (carry, (memory, decoded))
    unused, (memories, decodeds) = lax.scan(row_step, jnp.zeros((), jnp.float32), (source, target, pairs[0], pairs[1]))
    return jnp.stack([memories, decodeds]).reshape(2, MICRO, N_DP * ROW_LEN, D)

def reference(embedded, cotangent, lengths, attn_qkv, attn_out, ffn_up, ffn_down, norm_gain, norm_bias, cross_query, cross_kv, cross_out):
    flat_lengths = lengths.reshape(2, MICRO * N_DP, PAIRS)
    pairs = jax.vmap(jax.vmap(segment_ids))(flat_lengths)
    weights = tuple((item_array.astype(jnp.float32) for item_array in (attn_qkv, attn_out, ffn_up, ffn_down, norm_gain, norm_bias, cross_query, cross_kv, cross_out)))
    inputs = embedded.astype(jnp.float32)
    outputs, pullback = jax.vjp(lambda weight_set, input_set: forward(weight_set, input_set, pairs), weights, inputs)
    grad_weights, grad_inputs = pullback(cotangent.astype(jnp.float32))
    return (outputs.astype(jnp.bfloat16), grad_inputs, grad_weights[0], grad_weights[1], grad_weights[2], grad_weights[3], grad_weights[4], grad_weights[5], grad_weights[6], grad_weights[7], grad_weights[8])
```

```python
import jax
import jax.numpy as jnp
import numpy as np
from jax import lax
from jax.sharding import Mesh
from jax.sharding import PartitionSpec as P

HEAD_DIM = 64
ROW_LEN = 256
QUARTER = 64

EPSILON = 1e-05
NEGATIVE = -1000000000.0
SCALING = 0.125
GELU_COEF = 0.7978845608028654
BFLOAT = jnp.bfloat16
FLOAT = jnp.float32
AXES = ("s", "x", "z", "h", "c")
PLANE = ("x", "z")
ORDER = np.concatenate([np.arange(QUARTER) + QUARTER * q for q in (0, 2, 1, 3)]).astype(np.int32)


def swap(block, axis):
    return lax.ppermute(block, axis, [(0, 1), (1, 0)])


def gelu_tanh(values):
    return (
        0.5 * values * (1.0 + jnp.tanh(GELU_COEF * (values + 0.044715 * values * values * values)))
    )


def layer_norm(values, gain, offset):
    centred = values - jnp.mean(values, axis=-1, keepdims=True)
    inverse = lax.rsqrt(jnp.mean(centred * centred, axis=-1, keepdims=True) + EPSILON)
    normed = centred * inverse
    return ((normed * gain + offset).astype(BFLOAT), normed, inverse)


def norm_backward(grad_out, normed, inverse, gain):
    scaled = grad_out * gain
    inner = (
        scaled
        - jnp.mean(scaled, axis=-1, keepdims=True)
        - normed * jnp.mean(scaled * normed, axis=-1, keepdims=True)
    )
    return (inverse * inner, jnp.sum(grad_out * normed, axis=0), jnp.sum(grad_out, axis=0))


def segment_ids(lengths_row):
    ends = jnp.cumsum(lengths_row)
    positions = jnp.asarray(ORDER)
    return jnp.sum((positions[:, None] >= ends[None, :]).astype(jnp.int32), axis=1)


def dot(left, right):
    return jnp.dot(left, right, preferred_element_type=FLOAT)


def dot_left(left, right):
    return lax.dot_general(left, right, (((0,), (0,)), ((), ())), preferred_element_type=FLOAT)


def dot_right(left, right):
    return lax.dot_general(left, right, (((1,), (1,)), ((), ())), preferred_element_type=FLOAT)


def attend_forward(query_heads, key_heads, value_heads, allowed):
    scores = (
        jnp.einsum("qhd,khd->hqk", query_heads, key_heads, preferred_element_type=FLOAT) * SCALING
    )
    scores = jnp.where(allowed[None], scores, NEGATIVE)
    highest = jnp.max(scores, axis=-1, keepdims=True)
    expo_scores = jnp.exp(scores - highest)
    weights = expo_scores / jnp.sum(expo_scores, axis=-1, keepdims=True)
    mixed = jnp.einsum(
        "hqk,khd->qhd", weights.astype(BFLOAT), value_heads, preferred_element_type=FLOAT
    )
    return (mixed.reshape(mixed.shape[0], -1).astype(BFLOAT), weights)


def attend_backward(query_heads, key_heads, value_heads, weights, grad_mixed):
    grad_values = jnp.einsum(
        "hqk,qhd->khd", weights.astype(BFLOAT), grad_mixed, preferred_element_type=FLOAT
    )
    grad_weights = jnp.einsum("qhd,khd->hqk", grad_mixed, value_heads, preferred_element_type=FLOAT)
    grad_scores = weights * (
        grad_weights - jnp.sum(weights * grad_weights, axis=-1, keepdims=True)
    )
    grad_scores = grad_scores.astype(BFLOAT)
    grad_queries = (
        jnp.einsum("hqk,khd->qhd", grad_scores, key_heads, preferred_element_type=FLOAT) * SCALING
    )
    grad_keys = (
        jnp.einsum("hqk,qhd->khd", grad_scores, query_heads, preferred_element_type=FLOAT) * SCALING
    )
    return (grad_queries, grad_keys, grad_values)


def gather_plane(block):
    return lax.all_gather(block, PLANE, axis=0, tiled=True)


def scatter_plane(block):
    return lax.psum_scatter(block, PLANE, scatter_dimension=0, tiled=True)


def core_sum(part):
    return part + swap(part.astype(BFLOAT), "c").astype(FLOAT)


def shards(
    embedded,
    cotangent,
    lengths,
    attn_qkv,
    attn_out,
    ffn_up,
    ffn_down,
    norm_gain,
    norm_bias,
    cross_query,
    cross_kv,
    cross_out,
):
    is_decoder = lax.axis_index("s") == 1
    first_half = lax.axis_index("h") == 0
    core = lax.axis_index("c")

    def pick(flag, yes, no):
        return jnp.where(flag, yes, no)

    def own_row(pair):
        mine = pick(first_half, pair[0], pair[1])
        got = swap(pick(first_half, pair[1], pair[0]), "h")
        half = jnp.concatenate([pick(first_half, mine, got), pick(first_half, got, mine)])
        return lax.all_gather(half, "c", axis=0, tiled=True)

    def to_owners(row):
        half = lax.dynamic_slice_in_dim(row, core * 2 * QUARTER, 2 * QUARTER, 0)
        low, high = half[:QUARTER], half[QUARTER:]
        mine = pick(first_half, low, high)
        got = swap(pick(first_half, high, low), "h")
        return jnp.stack([pick(first_half, mine, got), pick(first_half, got, mine)])

    norms = jnp.concatenate([norm_gain[0], norm_bias[0]]).T
    norms = jnp.pad(norms, ((0, 0), (0, 128 - norms.shape[1])))
    own_attn = jnp.concatenate([attn_qkv[0], attn_out[0].T], axis=1)
    own_ffn = jnp.concatenate([ffn_up[0], ffn_down[0].T], axis=1)
    query_out = jnp.concatenate([cross_query, cross_out.T], axis=1)
    kept = pick(is_decoder, query_out, cross_kv)
    got = swap(pick(is_decoder, cross_kv, query_out), "s")
    own_cross = jnp.concatenate([pick(is_decoder, got, kept), pick(is_decoder, kept, got)])
    other_attn = swap(own_attn, "h")
    other_ffn = swap(own_ffn, "h")
    other_cross = swap(own_cross, "h")
    qkv_width = attn_qkv.shape[2]
    out_width = attn_out.shape[1]
    ff_width = ffn_up.shape[2]
    cross_width = cross_kv.shape[1]
    attn_whole = gather_plane(
        jnp.concatenate(
            [
                own_attn[:, :qkv_width],
                other_attn[:, :qkv_width],
                own_attn[:, qkv_width:],
                other_attn[:, qkv_width:],
                norms,
            ],
            axis=1,
        )
    )
    ffn_whole = gather_plane(
        jnp.concatenate(
            [
                own_ffn[:, :ff_width],
                other_ffn[:, :ff_width],
                own_ffn[:, ff_width:],
                other_ffn[:, ff_width:],
            ],
            axis=1,
        )
    )
    half_cross = cross_width // 2
    key_value_pack = jnp.concatenate([own_cross, other_cross], axis=1)
    query_out_pack = jnp.concatenate(
        [
            own_cross[:, :half_cross],
            other_cross[:, :half_cross],
            own_cross[:, half_cross:],
            other_cross[:, half_cross:],
        ],
        axis=1,
    )
    cross_pack = pick(is_decoder, query_out_pack, key_value_pack)
    cross_whole = gather_plane(cross_pack)
    depth = cross_whole.shape[0]
    cross_whole = (
        cross_whole.reshape(-1, 2, cross_query.shape[0], 2 * cross_width)
        .swapaxes(0, 1)
        .reshape(depth, 2 * cross_width)
    )

    weight_qkv = attn_whole[:, : 2 * qkv_width]
    weight_out = attn_whole[:, 2 * qkv_width : 2 * qkv_width + 2 * out_width]
    norm_rows = attn_whole[:, 2 * qkv_width + 2 * out_width :][:, :6].T.astype(FLOAT)
    gains, offsets = norm_rows[:3], norm_rows[3:]
    weight_up = ffn_whole[:, : 2 * ff_width]
    weight_down = ffn_whole[:, 2 * ff_width :]
    weight_query = cross_whole[:, :cross_width]
    weight_cross = cross_whole[:, cross_width:]
    weight_keyval = cross_whole

    row_lengths = pick(first_half, lengths[:, 0, 0], lengths[:, 1, 0])
    source_pair = segment_ids(row_lengths[0])
    target_pair = segment_ids(row_lengths[1])
    own_pair = pick(is_decoder, target_pair, source_pair)
    positions = jnp.asarray(ORDER)
    ordered = (positions[None, :] <= positions[:, None]) | jnp.logical_not(is_decoder)
    allowed_self = (own_pair[:, None] == own_pair[None, :]) & ordered
    allowed_cross = target_pair[:, None] == source_pair[None, :]

    values = own_row(embedded[0]).astype(FLOAT)
    grad_out = own_row(cotangent[0]).astype(FLOAT)

    def ffn_forward(stream):
        rows, unit, inverse = layer_norm(stream, gains[2], offsets[2])
        hidden = dot(rows, weight_up)
        activated = gelu_tanh(hidden).astype(BFLOAT)
        return (stream + core_sum(dot_right(activated, weight_down)), rows, unit, inverse, hidden, activated)

    def ffn_backward(grad, unit, inverse, hidden):
        low = grad.astype(BFLOAT)
        grad_activated = dot(low, weight_down)
        grad_hidden = jax.vjp(gelu_tanh, hidden)[1](grad_activated)[0].astype(BFLOAT)
        grad_rows = core_sum(dot_right(grad_hidden, weight_up))
        into, gain, offset = norm_backward(grad_rows, unit, inverse, gains[2])
        return (grad + into, low, grad_hidden, gain, offset)

    rows_one, unit_one, inverse_one = layer_norm(values, gains[0], offsets[0])
    heads = dot(rows_one, weight_qkv).astype(BFLOAT).reshape(ROW_LEN, -1, 3, HEAD_DIM)
    mixed_one, weights_one = attend_forward(heads[:, :, 0], heads[:, :, 1], heads[:, :, 2], allowed_self)
    after_self = values + core_sum(dot_right(mixed_one, weight_out))

    encoded, rows_enc, unit_enc, inverse_enc, hidden_enc, activated_enc = ffn_forward(after_self)
    memory, unit_memory, inverse_memory = layer_norm(encoded, gains[1], offsets[1])
    keyvals = lax.ppermute(dot(memory, weight_keyval).astype(BFLOAT), "s", [(0, 1)])

    rows_two, unit_two, inverse_two = layer_norm(after_self, gains[1], offsets[1])
    queries = dot(rows_two, weight_query).astype(BFLOAT).reshape(ROW_LEN, -1, HEAD_DIM)
    pair_heads = keyvals.reshape(ROW_LEN, -1, 2, HEAD_DIM)
    keys, vals = pair_heads[:, :, 0], pair_heads[:, :, 1]
    mixed_two, weights_two = attend_forward(queries, keys, vals, allowed_cross)
    after_cross = after_self + core_sum(dot_right(mixed_two, weight_cross))
    decoded, rows_dec, unit_dec, inverse_dec, hidden_dec, activated_dec = ffn_forward(after_cross)

    outputs = to_owners(pick(is_decoder, decoded.astype(BFLOAT), memory))

    grad_cross_path, low_dec, grad_hidden_dec, gain_dec, offset_dec = ffn_backward(
        grad_out, unit_dec, inverse_dec, hidden_dec
    )
    low_cross = grad_cross_path.astype(BFLOAT)
    grad_mixed_two = dot(low_cross, weight_cross).astype(BFLOAT).reshape(ROW_LEN, -1, HEAD_DIM)
    grad_q, grad_k, grad_v = attend_backward(queries, keys, vals, weights_two, grad_mixed_two)
    grad_keyvals = jnp.stack([grad_k, grad_v], axis=2).reshape(ROW_LEN, -1).astype(BFLOAT)
    grad_keyvals = lax.ppermute(grad_keyvals, "s", [(1, 0)])
    grad_queries = grad_q.reshape(ROW_LEN, -1).astype(BFLOAT)
    into_two, gain_two, offset_two = norm_backward(
        core_sum(dot_right(grad_queries, weight_query)), unit_two, inverse_two, gains[1]
    )
    grad_self_dec = grad_cross_path + into_two

    grad_memory = grad_out + core_sum(dot_right(grad_keyvals, weight_keyval))
    grad_encoded, gain_memory, offset_memory = norm_backward(
        grad_memory, unit_memory, inverse_memory, gains[1]
    )
    grad_self_enc, low_enc, grad_hidden_enc, gain_enc, offset_enc = ffn_backward(
        grad_encoded, unit_enc, inverse_enc, hidden_enc
    )

    grad_up = dot_left(
        pick(is_decoder, rows_dec, rows_enc), pick(is_decoder, grad_hidden_dec, grad_hidden_enc)
    )
    grad_down = dot_left(
        pick(is_decoder, low_dec, low_enc), pick(is_decoder, activated_dec, activated_enc)
    )
    grad_ffn = scatter_plane(jnp.concatenate([grad_up, grad_down], axis=1).astype(BFLOAT))
    grad_cross = pick(
        is_decoder,
        jnp.concatenate([dot_left(rows_two, grad_queries), dot_left(low_cross, mixed_two)], axis=1),
        dot_left(memory, grad_keyvals),
    )
    grad_cross = grad_cross.astype(BFLOAT).reshape(2, -1, cross_query.shape[0], 2 * cross_width)
    grad_cross = scatter_plane(grad_cross.swapaxes(0, 1).reshape(depth, -1))

    grad_self = pick(is_decoder, grad_self_dec, grad_self_enc)
    low_self = grad_self.astype(BFLOAT)
    grad_mixed_one = dot(low_self, weight_out).astype(BFLOAT).reshape(ROW_LEN, -1, HEAD_DIM)
    grad_projected = jnp.stack(
        attend_backward(heads[:, :, 0], heads[:, :, 1], heads[:, :, 2], weights_one, grad_mixed_one),
        axis=2,
    )
    grad_projected = grad_projected.reshape(ROW_LEN, -1).astype(BFLOAT)
    into_one, gain_one, offset_one = norm_backward(
        core_sum(dot_right(grad_projected, weight_qkv)), unit_one, inverse_one, gains[0]
    )
    grad_embedded = to_owners(grad_self + into_one)
    norm_grads = jnp.stack(
        [
            gain_one,
            pick(is_decoder, gain_two, gain_memory),
            pick(is_decoder, gain_dec, gain_enc),
            offset_one,
            pick(is_decoder, offset_two, offset_memory),
            pick(is_decoder, offset_dec, offset_enc),
        ]
    ).T
    grad_attn = jnp.concatenate(
        [
            dot_left(rows_one, grad_projected),
            dot_left(low_self, mixed_one),
            jnp.pad(norm_grads, ((0, 0), (0, 128 - norm_grads.shape[1]))),
        ],
        axis=1,
    )
    grad_attn = scatter_plane(grad_attn.astype(BFLOAT))

    def sum_halves(pairs):
        own = jnp.concatenate([own for own, _ in pairs], axis=1)
        other = jnp.concatenate([other for _, other in pairs], axis=1)
        return own.astype(FLOAT) + swap(other, "h").astype(FLOAT)

    def halves(block, start, width):
        return (block[:, start : start + width], block[:, start + width : start + 2 * width])

    total_ffn = sum_halves([halves(grad_ffn, 0, ff_width), halves(grad_ffn, 2 * ff_width, ff_width)])
    norm_part = grad_attn[:, 2 * qkv_width + 2 * out_width :]
    total_attn = sum_halves(
        [
            halves(grad_attn, 0, qkv_width),
            halves(grad_attn, 2 * qkv_width, out_width),
            (norm_part, norm_part),
        ]
    )
    cross_pairs = [
        (pick(is_decoder, as_dec, as_enc))
        for as_dec, as_enc in zip(
            [
                jnp.concatenate([grad_cross[:, :half_cross], grad_cross[:, cross_width : cross_width + half_cross]], axis=1),
                jnp.concatenate([grad_cross[:, half_cross:cross_width], grad_cross[:, cross_width + half_cross :]], axis=1),
            ],
            halves(grad_cross, 0, cross_width),
        )
    ]
    total_cross = sum_halves([tuple(cross_pairs)])
    rows_cross = cross_query.shape[0]
    low_part, high_part = total_cross[:rows_cross], total_cross[rows_cross:]
    keep_part = pick(is_decoder, high_part, low_part)
    got_part = swap(pick(is_decoder, low_part, high_part).astype(BFLOAT), "s").astype(FLOAT)
    final_query_out = pick(is_decoder, keep_part, got_part)
    final_keyval = pick(is_decoder, got_part, keep_part)

    total_norm = total_attn[:, qkv_width + out_width :][:, :6].T
    return (
        outputs[None],
        grad_embedded[None],
        total_attn[:, :qkv_width][None],
        total_attn[:, qkv_width : qkv_width + out_width].T[None],
        total_ffn[:, :ff_width][None],
        total_ffn[:, ff_width:].T[None],
        total_norm[:3][None],
        total_norm[3:][None],
        final_query_out[:, :half_cross],
        final_keyval,
        final_query_out[:, half_cross:].T,
    )


def solution(mesh):
    fine = Mesh(mesh.devices.reshape(2, 4, 4, 2, 2), AXES)
    tokens = ("x", "z", "h", "c")
    tensor = ("h", "c")
    whole = ("s", "x", "z")
    return jax.shard_map(
        shards,
        mesh=fine,
        in_specs=(
            P("s", None, tokens, None),
            P("s", None, tokens, None),
            P(None, None, PLANE, None),
            P("s", PLANE, tensor),
            P("s", tensor, PLANE),
            P("s", PLANE, tensor),
            P("s", tensor, PLANE),
            P("s", None, PLANE),
            P("s", None, PLANE),
            P(whole, tensor),
            P(whole, tensor),
            P(tensor, whole),
        ),
        out_specs=(
            P("s", None, tokens, None),
            P("s", None, tokens, None),
            P("s", PLANE, tensor),
            P("s", tensor, PLANE),
            P("s", PLANE, tensor),
            P("s", tensor, PLANE),
            P("s", None, PLANE),
            P("s", None, PLANE),
            P(whole, tensor),
            P(whole, tensor),
            P(tensor, whole),
        ),
        check_vma=False,
    )
```

```python
import functools

import jax
import jax.numpy as jnp
import numpy as np
from jax import lax
from jax.experimental import pallas as pl
from jax.experimental.pallas import tpu as pltpu
from jax.sharding import Mesh
from jax.sharding import PartitionSpec as P

HEAD_DIM = 64
ROW_LEN = 256
QUARTER = 64

EPSILON = 1e-05
NEGATIVE = -1000000000.0
SCALING = 0.125
GELU_COEF = 0.7978845608028654
BFLOAT = jnp.bfloat16
FLOAT = jnp.float32
AXES = ("s", "x", "z", "h", "c")
PLANE = ("x", "z")
ORDER = np.concatenate([np.arange(QUARTER) + QUARTER * q for q in (0, 2, 1, 3)]).astype(np.int32)


def swap(block, axis):
    return lax.ppermute(block, axis, [(0, 1), (1, 0)])


def shift(block, axis, distance):
    size = lax.axis_size(axis)
    return lax.ppermute(block, axis, [(i, (i + distance) % size) for i in range(size)])


def place(buffer, block, index, dim):
    return lax.dynamic_update_slice_in_dim(buffer, jnp.expand_dims(block, dim), index, dim)


def take(buffer, index, dim):
    return lax.dynamic_index_in_dim(buffer, index, dim, keepdims=False)


def gather_direct(block, axis):
    here = lax.axis_index(axis)
    blocks = [block, shift(block, axis, -1), shift(block, axis, 2), shift(block, axis, 1)]
    return [((here + k) % 4, block) for k, block in enumerate(blocks)]


def gather_ring(block, axis):
    here = lax.axis_index(axis)
    half = block.shape[0] // 2
    before, after = shift(block, axis, 1), shift(block, axis, -1)
    far = jnp.concatenate([shift(before[:half], axis, 1), shift(after[half:], axis, -1)])
    return [((here + k) % 4, block) for k, block in enumerate([block, after, far, before])]


def gather_ring_plane(block, axes):
    near, far = axes
    rows, columns = block.shape
    first = jnp.zeros((4, rows, columns), block.dtype)
    for index, piece in gather_direct(block, near):
        first = place(first, piece, index, 0)
    whole = jnp.zeros((4, 4, rows, columns), block.dtype)
    dim = PLANE.index(far)
    for index, piece in gather_ring(first, far):
        whole = place(whole, piece, index, dim)
    return whole.reshape(-1, columns)


def scatter_direct(blocks, axis):
    here = lax.axis_index(axis)
    parts = [take(blocks, (here + k) % 4, 0) for k in range(4)]
    total = parts[0].astype(FLOAT)
    for distance in (1, 2, -1):
        total = total + shift(parts[distance % 4].astype(BFLOAT), axis, distance).astype(FLOAT)
    return total


def scatter_ring(blocks, axis, dim):
    here = lax.axis_index(axis)
    own, after, far, before = [take(blocks, (here + k) % 4, dim) for k in range(4)]
    half = own.shape[0] // 2
    far = far.astype(BFLOAT)
    top = shift(far[:half], axis, 1).astype(FLOAT)
    bottom = shift(far[half:], axis, -1).astype(FLOAT)
    after = jnp.concatenate([after[:half].astype(FLOAT) + top, after[half:].astype(FLOAT)])
    before = jnp.concatenate([before[:half].astype(FLOAT), before[half:].astype(FLOAT) + bottom])
    from_before = shift(after.astype(BFLOAT), axis, 1).astype(FLOAT)
    from_after = shift(before.astype(BFLOAT), axis, -1).astype(FLOAT)
    return own.astype(FLOAT) + from_before + from_after


def scatter_ring_plane(block, axes):
    near, far = axes
    rows = block.shape[0] // 16
    blocks = block.reshape(4, 4, rows, -1)
    return scatter_direct(scatter_ring(blocks, far, PLANE.index(far)), near)


def gelu_tanh(values):
    return (
        0.5 * values * (1.0 + jnp.tanh(GELU_COEF * (values + 0.044715 * values * values * values)))
    )


def gelu_slope(values):
    squares = values * values
    curve = jnp.tanh(GELU_COEF * (values + 0.044715 * values * squares))
    return 0.5 * (1.0 + curve) + 0.5 * values * (1.0 - curve * curve) * (
        GELU_COEF * (1.0 + 3.0 * 0.044715 * squares)
    )


def segment_ids(lengths_row):
    ends = jnp.cumsum(lengths_row)
    positions = jnp.asarray(ORDER)
    return jnp.sum((positions[:, None] >= ends[None, :]).astype(jnp.int32), axis=1)


def dot(left, right):
    return jnp.dot(left, right, preferred_element_type=FLOAT)


def dot_left(left, right):
    return lax.dot_general(left, right, (((0,), (0,)), ((), ())), preferred_element_type=FLOAT)


def dot_right(left, right):
    return lax.dot_general(left, right, (((1,), (1,)), ((), ())), preferred_element_type=FLOAT)


def normalize(stream):
    centred = stream - jnp.mean(stream, axis=-1, keepdims=True)
    inverse = lax.rsqrt(jnp.mean(centred * centred, axis=-1, keepdims=True) + EPSILON)
    return centred * inverse, inverse


def layer_norm(stream, norms, index):
    unit, _ = normalize(stream)
    return (unit * norms[index : index + 1] + norms[index + 3 : index + 4]).astype(BFLOAT)


def norm_backward(grad_out, stream, gain):
    unit, inverse = normalize(stream)
    scaled = grad_out * gain
    inner = (
        scaled
        - jnp.mean(scaled, axis=-1, keepdims=True)
        - unit * jnp.mean(scaled * unit, axis=-1, keepdims=True)
    )
    sums = jnp.concatenate(
        [
            jnp.sum(grad_out * unit, axis=0, keepdims=True),
            jnp.sum(grad_out, axis=0, keepdims=True),
            jnp.zeros((6, grad_out.shape[1]), FLOAT),
        ]
    )
    return inverse * inner, sums


def add_parts(own_ref, other_ref):
    return own_ref[...].astype(FLOAT) + other_ref[...].astype(FLOAT)


def softmax(query, key, mask):
    scores = jnp.where(mask, dot_right(query, key) * SCALING, NEGATIVE)
    expo_scores = jnp.exp(scores - jnp.max(scores, axis=-1, keepdims=True))
    return expo_scores / jnp.sum(expo_scores, axis=-1, keepdims=True)


def head_backward(query, key, value, mask, grad_mixed):
    weights = softmax(query, key, mask)
    grad_value = dot_left(weights.astype(BFLOAT), grad_mixed)
    grad_weights = dot_right(grad_mixed, value)
    grad_scores = weights * (
        grad_weights - jnp.sum(weights * grad_weights, axis=-1, keepdims=True)
    )
    grad_scores = grad_scores.astype(BFLOAT)
    grad_query = dot(grad_scores, key) * SCALING
    grad_key = dot_left(grad_scores, query) * SCALING
    return grad_query.astype(BFLOAT), grad_key.astype(BFLOAT), grad_value.astype(BFLOAT)


def head(ref, place):
    return ref[:, place * HEAD_DIM : (place + 1) * HEAD_DIM]


def self_forward_kernel(stream, norms, own, other, mask, rows, qkv, mixed, part):
    allowed = mask[...] > 0.5
    normed = layer_norm(stream[...], norms, 0)
    rows[...] = normed
    quarter = mixed.shape[1] // 2
    width = 3 * quarter
    total = None
    for side, weights in enumerate((own, other)):
        qkv[:, side * width : (side + 1) * width] = dot(normed, weights[:, :width]).astype(BFLOAT)
        first = side * quarter // HEAD_DIM
        for i in range(first, first + quarter // HEAD_DIM):
            weight = softmax(head(qkv, 3 * i), head(qkv, 3 * i + 1), allowed)
            out = dot(weight.astype(BFLOAT), head(qkv, 3 * i + 2))
            mixed[:, i * HEAD_DIM : (i + 1) * HEAD_DIM] = out.astype(BFLOAT)
        term = dot_right(
            mixed[:, side * quarter : (side + 1) * quarter], weights[:, width : width + quarter]
        )
        total = term if total is None else total + term
    part[...] = total.astype(BFLOAT)


def ffn_forward_kernel(
    stream, own, other, norms, up, down, after, rows, hidden, activated, part, total
):
    step = pl.program_id(0)

    @pl.when(step == 0)
    def _():
        after[...] = stream[...] + add_parts(own, other)
        rows[...] = layer_norm(after[...], norms, 2)

    raised = dot(rows[...], up[...])
    hidden[...] = raised
    active = gelu_tanh(raised).astype(BFLOAT)
    activated[...] = active
    term = dot_right(active, down[...])

    @pl.when(step == 0)
    def _():
        total[...] = term

    @pl.when(step > 0)
    def _():
        total[...] += term

    @pl.when(step == pl.num_programs(0) - 1)
    def _():
        part[...] = total[...].astype(BFLOAT)


def memory_kernel(stream, own, other, norms, weights, encoded, memory, keyvals):
    encoded[...] = stream[...] + add_parts(own, other)
    memory[...] = layer_norm(encoded[...], norms, 1)
    keyvals[...] = dot(memory[...], weights[...]).astype(BFLOAT)


def query_kernel(stream, own, other, norms, weights, after, rows, queries):
    after[...] = stream[...] + add_parts(own, other)
    rows[...] = layer_norm(after[...], norms, 1)
    queries[...] = dot(rows[...], weights[:, : queries.shape[1]]).astype(BFLOAT)


def cross_forward_kernel(queries, keyvals, mask, weights, mixed, part):
    allowed = mask[...] > 0.5
    for i in range(queries.shape[1] // HEAD_DIM):
        weight = softmax(head(queries, i), head(keyvals, 2 * i), allowed)
        out = dot(weight.astype(BFLOAT), head(keyvals, 2 * i + 1))
        mixed[:, i * HEAD_DIM : (i + 1) * HEAD_DIM] = out.astype(BFLOAT)
    part[...] = dot_right(mixed[...], weights[:, queries.shape[1] :]).astype(BFLOAT)


def ffn_backward_step(low, hidden, up, down, grad_hidden, part, total):
    step = pl.program_id(0)
    grad_activated = dot(low[...], down[...])
    grad = (grad_activated * gelu_slope(hidden[...])).astype(BFLOAT)
    grad_hidden[...] = grad
    term = dot_right(grad, up[...])

    @pl.when(step == 0)
    def _():
        total[...] = term

    @pl.when(step > 0)
    def _():
        total[...] += term

    @pl.when(step == pl.num_programs(0) - 1)
    def _():
        part[...] = total[...].astype(BFLOAT)


def ffn_backward_kernel(low, hidden, up, down, grad_hidden, part, total):
    ffn_backward_step(low, hidden, up, down, grad_hidden, part, total)


def memory_ffn_backward_kernel(
    cotangent, own, other, stream, norms, hidden, up, down, grad, low, sums, grad_hidden, part, total
):
    @pl.when(pl.program_id(0) == 0)
    def _():
        into, totals = norm_backward(
            cotangent[...].astype(FLOAT) + add_parts(own, other), stream[...], norms[1:2]
        )
        grad[...] = into
        low[...] = into.astype(BFLOAT)
        sums[...] = totals

    ffn_backward_step(low, hidden, up, down, grad_hidden, part, total)


def cross_backward_kernel(
    cotangent, own, other, stream, norms, queries, keyvals, mask, weights,
    grad, low, sums, grad_queries, grad_keyvals, part,
):
    allowed = mask[...] > 0.5
    into, totals = norm_backward(add_parts(own, other), stream[...], norms[2:3])
    grad[...] = cotangent[...].astype(FLOAT) + into
    low[...] = grad[...].astype(BFLOAT)
    sums[...] = totals
    grad_mixed = dot(low[...], weights[:, queries.shape[1] :]).astype(BFLOAT)
    for i in range(queries.shape[1] // HEAD_DIM):
        one, two, three = head_backward(
            head(queries, i),
            head(keyvals, 2 * i),
            head(keyvals, 2 * i + 1),
            allowed,
            grad_mixed[:, i * HEAD_DIM : (i + 1) * HEAD_DIM],
        )
        grad_queries[:, i * HEAD_DIM : (i + 1) * HEAD_DIM] = one
        grad_keyvals[:, 2 * i * HEAD_DIM : (2 * i + 1) * HEAD_DIM] = two
        grad_keyvals[:, (2 * i + 1) * HEAD_DIM : (2 * i + 2) * HEAD_DIM] = three
    part[...] = dot_right(grad_queries[...], weights[:, : queries.shape[1]]).astype(BFLOAT)


def keyval_backward_kernel(grad_keyvals, weights, part):
    part[...] = dot_right(grad_keyvals[...], weights[...]).astype(BFLOAT)


def self_backward_kernel(
    decoder, grad_enc, own_enc, other_enc, grad_dec, own_dec, other_dec, stream, norms, qkv, mask,
    own, other, grad, low, sums, grad_qkv, part,
):
    allowed = mask[...] > 0.5

    @pl.when(decoder[0] == 1)
    def _():
        into, totals = norm_backward(add_parts(own_dec, other_dec), stream[...], norms[1:2])
        grad[...] = grad_dec[...] + into
        sums[...] = totals

    @pl.when(decoder[0] == 0)
    def _():
        into, totals = norm_backward(add_parts(own_enc, other_enc), stream[...], norms[2:3])
        grad[...] = grad_enc[...] + into
        sums[...] = totals

    low[...] = grad[...].astype(BFLOAT)
    quarter = qkv.shape[1] // 6
    width = 3 * quarter
    total = None
    for side, weights in enumerate((own, other)):
        grad_mixed = dot(low[...], weights[:, width : width + quarter]).astype(BFLOAT)
        first = side * quarter // HEAD_DIM
        for j in range(quarter // HEAD_DIM):
            i = first + j
            grads = head_backward(
                head(qkv, 3 * i),
                head(qkv, 3 * i + 1),
                head(qkv, 3 * i + 2),
                allowed,
                grad_mixed[:, j * HEAD_DIM : (j + 1) * HEAD_DIM],
            )
            for k in range(3):
                grad_qkv[:, (3 * i + k) * HEAD_DIM : (3 * i + k + 1) * HEAD_DIM] = grads[k]
        term = dot_right(grad_qkv[:, side * width : (side + 1) * width], weights[:, :width])
        total = term if total is None else total + term
    part[...] = total.astype(BFLOAT)


def input_backward_kernel(grad, own, other, stream, norms, grad_input, sums):
    into, totals = norm_backward(add_parts(own, other), stream[...], norms[0:1])
    grad_input[...] = grad[...] + into
    sums[...] = totals


def early_weights_kernel(
    decoder, rows_enc, rows_dec, hidden_enc, hidden_dec, low_enc, low_dec, active_enc, active_dec,
    rows_two, queries, low_two, mixed, memory, keyvals, out, scratch,
):
    hidden = hidden_enc.shape[1]
    half = queries.shape[1]

    @pl.when(decoder[0] == 1)
    def _():
        out[:, :hidden] = dot_left(rows_dec[...], hidden_dec[...]).astype(BFLOAT)
        out[:, hidden : 2 * hidden] = dot_left(low_dec[...], active_dec[...]).astype(BFLOAT)
        scratch[:, :half] = dot_left(rows_two[...], queries[...])
        scratch[:, half:] = dot_left(low_two[...], mixed[...])

    @pl.when(decoder[0] == 0)
    def _():
        out[:, :hidden] = dot_left(rows_enc[...], hidden_enc[...]).astype(BFLOAT)
        out[:, hidden : 2 * hidden] = dot_left(low_enc[...], active_enc[...]).astype(BFLOAT)
        scratch[...] = dot_left(memory[...], keyvals[...])

    depth = out.shape[0]
    piece = depth // 32
    for i in range(16):
        for j in range(2):
            out[(2 * i + j) * piece : (2 * i + j + 1) * piece, 2 * hidden :] = scratch[
                j * depth // 2 + i * piece : j * depth // 2 + (i + 1) * piece, :
            ].astype(BFLOAT)


def attn_weights_kernel(rows, grad_qkv, low, mixed, norm_grads, own, other):
    quarter = mixed.shape[1] // 2
    width = 3 * quarter
    for side, out in enumerate((own, other)):
        out[:, :width] = dot_left(
            rows[...], grad_qkv[:, side * width : (side + 1) * width]
        ).astype(BFLOAT)
        out[:, width : width + quarter] = dot_left(
            low[...], mixed[:, side * quarter : (side + 1) * quarter]
        ).astype(BFLOAT)
    own[:, width + quarter :] = norm_grads[...]


def gather_plane(block):
    return lax.all_gather(block, PLANE, axis=0, tiled=True)


def scatter_plane(block):
    return lax.psum_scatter(block, PLANE, scatter_dimension=0, tiled=True)


VMEM = pl.BlockSpec(memory_space=pltpu.VMEM)
SMEM = pl.BlockSpec(memory_space=pltpu.SMEM)
LIMIT = pltpu.CompilerParams(vmem_limit_bytes=50 * 1024 * 1024)


def low_of(*dims):
    return jax.ShapeDtypeStruct(dims, BFLOAT)


def full_of(*dims):
    return jax.ShapeDtypeStruct(dims, FLOAT)


def run(kernel, outs, *operands, flops=0, scratch=(), flag=False, specs=None):
    specs = specs or {}
    in_specs = [specs.get(i, VMEM) for i in range(len(operands))]
    if flag:
        in_specs[0] = SMEM
    moved = sum(o.size * o.dtype.itemsize for o in (*operands, *outs))
    return pl.pallas_call(
        kernel,
        out_shape=list(outs),
        in_specs=in_specs,
        out_specs=[VMEM] * len(outs),
        scratch_shapes=list(scratch),
        compiler_params=LIMIT,
        cost_estimate=pl.CostEstimate(flops=flops, bytes_accessed=moved, transcendentals=0),
    )(*operands)


def shards(
    embedded,
    cotangent,
    lengths,
    attn_qkv,
    attn_out,
    ffn_up,
    ffn_down,
    norm_gain,
    norm_bias,
    cross_query,
    cross_kv,
    cross_out,
):
    is_decoder = lax.axis_index("s") == 1
    first_half = lax.axis_index("h") == 0
    core = lax.axis_index("c")

    def pick(flag, yes, no):
        return jnp.where(flag, yes, no)

    def own_row(pair):
        mine = pick(first_half, pair[0], pair[1])
        got = swap(pick(first_half, pair[1], pair[0]), "h")
        half = jnp.concatenate([pick(first_half, mine, got), pick(first_half, got, mine)])
        return lax.all_gather(half, "c", axis=0, tiled=True)

    def to_owners(row):
        half = lax.dynamic_slice_in_dim(row, core * 2 * QUARTER, 2 * QUARTER, 0)
        low, high = half[:QUARTER], half[QUARTER:]
        mine = pick(first_half, low, high)
        got = swap(pick(first_half, high, low), "h")
        return jnp.stack([pick(first_half, mine, got), pick(first_half, got, mine)])

    norms = jnp.concatenate([norm_gain[0], norm_bias[0]]).T
    norms = jnp.pad(norms, ((0, 0), (0, 128 - norms.shape[1])))
    own_attn = jnp.concatenate([attn_qkv[0], attn_out[0].T], axis=1)
    own_ffn = jnp.concatenate([ffn_up[0], ffn_down[0].T], axis=1)
    query_out = jnp.concatenate([cross_query, cross_out.T], axis=1)
    kept = pick(is_decoder, query_out, cross_kv)
    got = swap(pick(is_decoder, cross_kv, query_out), "s")
    own_cross = jnp.concatenate([pick(is_decoder, got, kept), pick(is_decoder, kept, got)])
    other_attn = swap(own_attn, "h")
    other_ffn = swap(own_ffn, "h")
    other_cross = swap(own_cross, "h")
    qkv_width = attn_qkv.shape[2]
    out_width = attn_out.shape[1]
    ff_width = ffn_up.shape[2]
    cross_width = cross_kv.shape[1]
    attn_own = gather_ring_plane(jnp.concatenate([own_attn, norms], axis=1), ("z", "x"))
    attn_other = gather_ring_plane(other_attn, ("x", "z"))
    half_cross = cross_width // 2
    key_value_pack = jnp.concatenate([own_cross, other_cross], axis=1)
    query_out_pack = jnp.concatenate(
        [
            own_cross[:, :half_cross],
            other_cross[:, :half_cross],
            own_cross[:, half_cross:],
            other_cross[:, half_cross:],
        ],
        axis=1,
    )
    cross_pack = pick(is_decoder, query_out_pack, key_value_pack)
    late_whole = gather_plane(
        jnp.concatenate(
            [
                own_ffn[:, :ff_width],
                other_ffn[:, :ff_width],
                own_ffn[:, ff_width:],
                other_ffn[:, ff_width:],
                cross_pack,
            ],
            axis=1,
        )
    )
    attn_width = qkv_width + out_width
    norms = attn_own[:, attn_width:][:, :8].T.astype(FLOAT)
    decoder = lax.axis_index("s").reshape(1).astype(jnp.int32)

    row_lengths = pick(first_half, lengths[:, 0, 0], lengths[:, 1, 0])
    source_pair = segment_ids(row_lengths[0])
    target_pair = segment_ids(row_lengths[1])
    own_pair = pick(is_decoder, target_pair, source_pair)
    positions = jnp.asarray(ORDER)
    ordered = (positions[None, :] <= positions[:, None]) | jnp.logical_not(is_decoder)
    allowed_self = ((own_pair[:, None] == own_pair[None, :]) & ordered).astype(BFLOAT)
    allowed_cross = (target_pair[:, None] == source_pair[None, :]).astype(BFLOAT)

    values = own_row(embedded[0]).astype(FLOAT)
    grad_out = own_row(cotangent[0])
    width = values.shape[1]
    hidden_width = 2 * ff_width
    steps = 4
    block = hidden_width // steps
    row_block = pl.BlockSpec((ROW_LEN, width), lambda i: (0, 0))
    norm_block = pl.BlockSpec((8, width), lambda i: (0, 0))
    up_block = pl.BlockSpec((width, block), lambda i: (0, i))
    down_block = pl.BlockSpec((width, block), lambda i: (0, i + steps))
    hidden_block = pl.BlockSpec((ROW_LEN, block), lambda i: (0, i))
    ffn_flops = 4 * ROW_LEN * width * hidden_width

    cross_whole = (
        late_whole[:, 4 * ff_width :]
        .reshape(-1, 2, cross_query.shape[0], 2 * cross_width)
        .swapaxes(0, 1)
        .reshape(width, 2 * cross_width)
    )

    def ffn_forward(stream, own, other):
        return pl.pallas_call(
            ffn_forward_kernel,
            grid=(steps,),
            out_shape=[
                full_of(ROW_LEN, width),
                low_of(ROW_LEN, width),
                full_of(ROW_LEN, hidden_width),
                low_of(ROW_LEN, hidden_width),
                low_of(ROW_LEN, width),
            ],
            in_specs=[row_block, row_block, row_block, norm_block, up_block, down_block],
            out_specs=[row_block, row_block, hidden_block, hidden_block, row_block],
            scratch_shapes=[pltpu.VMEM((ROW_LEN, width), FLOAT)],
            compiler_params=LIMIT,
            cost_estimate=pl.CostEstimate(
                flops=ffn_flops, bytes_accessed=14 * 1024 * 1024, transcendentals=0
            ),
        )(stream, own, other, norms, late_whole, late_whole)

    rows_one, qkv, mixed_one, part = run(
        self_forward_kernel,
        [
            low_of(ROW_LEN, width),
            low_of(ROW_LEN, 2 * qkv_width),
            low_of(ROW_LEN, 2 * out_width),
            low_of(ROW_LEN, width),
        ],
        values, norms, attn_own, attn_other, allowed_self,
        flops=10 * ROW_LEN * width * out_width * 2,
    )
    got = swap(part, "c")

    after_self, rows_enc, hidden_enc, active_enc, part_enc = ffn_forward(values, part, got)
    encoded, memory, keyvals = run(
        memory_kernel,
        [full_of(ROW_LEN, width), low_of(ROW_LEN, width), low_of(ROW_LEN, 2 * cross_width)],
        after_self, part_enc, swap(part_enc, "c"), norms, cross_whole,
        flops=4 * ROW_LEN * width * cross_width,
    )
    keyvals = lax.ppermute(keyvals, "s", [(0, 1)])

    after_two, rows_two, queries = run(
        query_kernel,
        [full_of(ROW_LEN, width), low_of(ROW_LEN, width), low_of(ROW_LEN, cross_width)],
        values, part, got, norms, cross_whole,
        flops=2 * ROW_LEN * width * cross_width,
    )
    mixed_two, part_two = run(
        cross_forward_kernel,
        [low_of(ROW_LEN, cross_width), low_of(ROW_LEN, width)],
        queries, keyvals, allowed_cross, cross_whole,
        flops=4 * ROW_LEN * width * cross_width,
    )
    after_cross, rows_dec, hidden_dec, active_dec, part_dec = ffn_forward(
        after_two, part_two, swap(part_two, "c")
    )
    decoded = after_cross + part_dec.astype(FLOAT) + swap(part_dec, "c").astype(FLOAT)
    outputs = to_owners(pick(is_decoder, decoded.astype(BFLOAT), memory))

    grad_hidden_dec, part = pl.pallas_call(
        ffn_backward_kernel,
        grid=(steps,),
        out_shape=[low_of(ROW_LEN, hidden_width), low_of(ROW_LEN, width)],
        in_specs=[row_block, hidden_block, up_block, down_block],
        out_specs=[hidden_block, row_block],
        scratch_shapes=[pltpu.VMEM((ROW_LEN, width), FLOAT)],
        compiler_params=LIMIT,
        cost_estimate=pl.CostEstimate(flops=ffn_flops, bytes_accessed=12 * 1024 * 1024, transcendentals=0),
    )(grad_out, hidden_dec, late_whole, late_whole)
    grad_dec, low_two, sums_two_dec, grad_queries, grad_keyvals, part_two = run(
        cross_backward_kernel,
        [
            full_of(ROW_LEN, width),
            low_of(ROW_LEN, width),
            full_of(8, width),
            low_of(ROW_LEN, cross_width),
            low_of(ROW_LEN, 2 * cross_width),
            low_of(ROW_LEN, width),
        ],
        grad_out, part, swap(part, "c"), after_cross, norms, queries, keyvals, allowed_cross,
        cross_whole,
        flops=8 * ROW_LEN * width * cross_width,
    )
    grad_keyvals = lax.ppermute(grad_keyvals, "s", [(1, 0)])
    got_two = swap(part_two, "c")

    (part,) = run(
        keyval_backward_kernel, [low_of(ROW_LEN, width)], grad_keyvals, cross_whole,
        flops=4 * ROW_LEN * width * cross_width,
    )
    grad_enc, low_enc, sums_one_enc, grad_hidden_enc, part_enc = pl.pallas_call(
        memory_ffn_backward_kernel,
        grid=(steps,),
        out_shape=[
            full_of(ROW_LEN, width),
            low_of(ROW_LEN, width),
            full_of(8, width),
            low_of(ROW_LEN, hidden_width),
            low_of(ROW_LEN, width),
        ],
        in_specs=[
            row_block, row_block, row_block, row_block, norm_block, hidden_block, up_block, down_block
        ],
        out_specs=[row_block, row_block, norm_block, hidden_block, row_block],
        scratch_shapes=[pltpu.VMEM((ROW_LEN, width), FLOAT)],
        compiler_params=LIMIT,
        cost_estimate=pl.CostEstimate(flops=ffn_flops, bytes_accessed=15 * 1024 * 1024, transcendentals=0),
    )(grad_out, part, swap(part, "c"), encoded, norms, hidden_enc, late_whole, late_whole)
    got_enc = swap(part_enc, "c")

    (grad_early,) = run(
        early_weights_kernel,
        [low_of(width, 2 * hidden_width + 2 * cross_width)],
        decoder, rows_enc, rows_dec, grad_hidden_enc, grad_hidden_dec, low_enc, grad_out,
        active_enc, active_dec, rows_two, grad_queries, low_two, mixed_two, memory, grad_keyvals,
        flops=2 * ffn_flops, flag=True,
        scratch=[pltpu.VMEM((width, 2 * cross_width), FLOAT)],
    )
    grad_early = scatter_plane(grad_early)
    grad_ffn = grad_early[:, : 2 * hidden_width]
    grad_cross = grad_early[:, 2 * hidden_width :]

    grad_self, low_self, sums_last, grad_qkv, part = run(
        self_backward_kernel,
        [
            full_of(ROW_LEN, width),
            low_of(ROW_LEN, width),
            full_of(8, width),
            low_of(ROW_LEN, 2 * qkv_width),
            low_of(ROW_LEN, width),
        ],
        decoder, grad_enc, part_enc, got_enc, grad_dec, part_two, got_two, after_self, norms, qkv,
        allowed_self, attn_own, attn_other,
        flops=20 * ROW_LEN * width * out_width * 2, flag=True,
    )
    grad_input, sums_zero = run(
        input_backward_kernel,
        [full_of(ROW_LEN, width), full_of(8, width)],
        grad_self, part, swap(part, "c"), values, norms,
    )
    grad_embedded = to_owners(grad_input)
    sums_one = pick(is_decoder, sums_last, sums_one_enc)
    sums_two = pick(is_decoder, sums_two_dec, sums_last)
    norm_grads = jnp.stack(
        [sums_zero[0], sums_one[0], sums_two[0], sums_zero[1], sums_one[1], sums_two[1]]
    ).T
    norm_grads = jnp.pad(norm_grads, ((0, 0), (0, 128 - norm_grads.shape[1]))).astype(BFLOAT)
    attn_own_grad, attn_other_grad = run(
        attn_weights_kernel,
        [low_of(width, attn_width + 128), low_of(width, attn_width)],
        rows_one, grad_qkv, low_self, mixed_one, norm_grads,
        flops=8 * ROW_LEN * width * out_width * 2,
    )
    attn_own_grad = scatter_ring_plane(attn_own_grad, ("z", "x"))
    attn_other_grad = scatter_ring_plane(attn_other_grad, ("x", "z"))

    def sum_halves(pairs):
        own = jnp.concatenate([own for own, _ in pairs], axis=1)
        other = jnp.concatenate([other for _, other in pairs], axis=1)
        return own.astype(FLOAT) + swap(other.astype(BFLOAT), "h").astype(FLOAT)

    def halves(block, start, width):
        return (block[:, start : start + width], block[:, start + width : start + 2 * width])

    total_ffn = sum_halves([halves(grad_ffn, 0, ff_width), halves(grad_ffn, 2 * ff_width, ff_width)])
    total_attn = sum_halves(
        [
            (attn_own_grad[:, :attn_width], attn_other_grad),
            (attn_own_grad[:, attn_width:], attn_own_grad[:, attn_width:]),
        ]
    )
    cross_pairs = [
        (pick(is_decoder, as_dec, as_enc))
        for as_dec, as_enc in zip(
            [
                jnp.concatenate([grad_cross[:, :half_cross], grad_cross[:, cross_width : cross_width + half_cross]], axis=1),
                jnp.concatenate([grad_cross[:, half_cross:cross_width], grad_cross[:, cross_width + half_cross :]], axis=1),
            ],
            halves(grad_cross, 0, cross_width),
        )
    ]
    total_cross = sum_halves([tuple(cross_pairs)])
    rows_cross = cross_query.shape[0]
    low_part, high_part = total_cross[:rows_cross], total_cross[rows_cross:]
    keep_part = pick(is_decoder, high_part, low_part)
    got_part = swap(pick(is_decoder, low_part, high_part).astype(BFLOAT), "s").astype(FLOAT)
    final_query_out = pick(is_decoder, keep_part, got_part)
    final_keyval = pick(is_decoder, got_part, keep_part)

    total_norm = total_attn[:, qkv_width + out_width :][:, :6].T
    return (
        outputs[None],
        grad_embedded[None],
        total_attn[:, :qkv_width][None],
        total_attn[:, qkv_width : qkv_width + out_width].T[None],
        total_ffn[:, :ff_width][None],
        total_ffn[:, ff_width:].T[None],
        total_norm[:3][None],
        total_norm[3:][None],
        final_query_out[:, :half_cross],
        final_keyval,
        final_query_out[:, half_cross:].T,
    )


def solution(mesh):
    fine = Mesh(mesh.devices.reshape(2, 4, 4, 2, 2), AXES)
    tokens = ("x", "z", "h", "c")
    tensor = ("h", "c")
    whole = ("s", "x", "z")
    return jax.shard_map(
        shards,
        mesh=fine,
        in_specs=(
            P("s", None, tokens, None),
            P("s", None, tokens, None),
            P(None, None, PLANE, None),
            P("s", PLANE, tensor),
            P("s", tensor, PLANE),
            P("s", PLANE, tensor),
            P("s", tensor, PLANE),
            P("s", None, PLANE),
            P("s", None, PLANE),
            P(whole, tensor),
            P(whole, tensor),
            P(tensor, whole),
        ),
        out_specs=(
            P("s", None, tokens, None),
            P("s", None, tokens, None),
            P("s", PLANE, tensor),
            P("s", tensor, PLANE),
            P("s", PLANE, tensor),
            P("s", tensor, PLANE),
            P("s", None, PLANE),
            P("s", None, PLANE),
            P(whole, tensor),
            P(whole, tensor),
            P(tensor, whole),
        ),
        check_vma=False,
    )
```

```python
import functools

import jax
import jax.numpy as jnp
import numpy as np
from jax import lax
from jax.experimental import pallas as pl
from jax.experimental.pallas import tpu as pltpu
from jax.sharding import Mesh
from jax.sharding import PartitionSpec as P

HEAD_DIM = 64
ROW_LEN = 256
QUARTER = 64
NORM_COLUMNS = 128

EPSILON = 1e-05
NEGATIVE = -1000000000.0
SCALING = 0.125
GELU_COEF = 0.7978845608028654
BFLOAT = jnp.bfloat16
FLOAT = jnp.float32
AXES = ("s", "x", "z", "h", "c")
PLANE = ("x", "z")
ORDER = np.concatenate([np.arange(QUARTER) + QUARTER * q for q in (0, 2, 1, 3)]).astype(np.int32)


def swap(block, axis):
    return lax.ppermute(block, axis, [(0, 1), (1, 0)])


def shift(block, axis, distance):
    size = lax.axis_size(axis)
    return lax.ppermute(block, axis, [(i, (i + distance) % size) for i in range(size)])


def place(buffer, block, index, dim):
    return lax.dynamic_update_slice_in_dim(buffer, jnp.expand_dims(block, dim), index, dim)


def take(buffer, index, dim):
    return lax.dynamic_index_in_dim(buffer, index, dim, keepdims=False)


def gather_direct(block, axis):
    here = lax.axis_index(axis)
    blocks = [block, shift(block, axis, -1), shift(block, axis, 2), shift(block, axis, 1)]
    return [((here + k) % 4, block) for k, block in enumerate(blocks)]


def gather_ring(block, axis):
    here = lax.axis_index(axis)
    half = block.shape[0] // 2
    before, after = shift(block, axis, 1), shift(block, axis, -1)
    far = jnp.concatenate([shift(before[:half], axis, 1), shift(after[half:], axis, -1)])
    return [((here + k) % 4, block) for k, block in enumerate([block, after, far, before])]


def gather_ring_plane(block, axes):
    near, far = axes
    rows, columns = block.shape
    first = jnp.zeros((4, rows, columns), block.dtype)
    for index, piece in gather_direct(block, near):
        first = place(first, piece, index, 0)
    whole = jnp.zeros((4, 4, rows, columns), block.dtype)
    dim = PLANE.index(far)
    for index, piece in gather_ring(first, far):
        whole = place(whole, piece, index, dim)
    return whole.reshape(-1, columns)


def together(*arrays):
    return lax.optimization_barrier(arrays)


def scatter_direct(blocks, axis):
    here = lax.axis_index(axis)
    parts = [take(blocks, (here + k) % 4, 0) for k in range(4)]
    total = parts[0].astype(FLOAT)
    for distance in (1, 2, -1):
        total = total + shift(parts[distance % 4].astype(BFLOAT), axis, distance).astype(FLOAT)
    return total


def scatter_ring(blocks, axis, dim):
    here = lax.axis_index(axis)
    own, after, far, before = [take(blocks, (here + k) % 4, dim) for k in range(4)]
    half = own.shape[0] // 2
    far = far.astype(BFLOAT)
    top = shift(far[:half], axis, 1).astype(FLOAT)
    bottom = shift(far[half:], axis, -1).astype(FLOAT)
    after = jnp.concatenate([after[:half].astype(FLOAT) + top, after[half:].astype(FLOAT)])
    before = jnp.concatenate([before[:half].astype(FLOAT), before[half:].astype(FLOAT) + bottom])
    from_before = shift(after.astype(BFLOAT), axis, 1).astype(FLOAT)
    from_after = shift(before.astype(BFLOAT), axis, -1).astype(FLOAT)
    return own.astype(FLOAT) + from_before + from_after


def scatter_ring_plane(block, axes):
    near, far = axes
    rows = block.shape[0] // 16
    blocks = block.reshape(4, 4, rows, -1)
    return scatter_direct(scatter_ring(blocks, far, PLANE.index(far)), near)


def swap_across(block):
    return lax.ppermute(block, ("s", "h"), [(0, 3), (3, 0), (1, 2), (2, 1)])


def gelu_tanh(values):
    return (
        0.5 * values * (1.0 + jnp.tanh(GELU_COEF * (values + 0.044715 * values * values * values)))
    )


def gelu_slope(values):
    squares = values * values
    curve = jnp.tanh(GELU_COEF * (values + 0.044715 * values * squares))
    return 0.5 * (1.0 + curve) + 0.5 * values * (1.0 - curve * curve) * (
        GELU_COEF * (1.0 + 3.0 * 0.044715 * squares)
    )


def segment_ids(lengths_row):
    ends = jnp.cumsum(lengths_row)
    positions = jnp.asarray(ORDER)
    return jnp.sum((positions[:, None] >= ends[None, :]).astype(jnp.int32), axis=1)


def dot(left, right):
    return jnp.dot(left, right, preferred_element_type=FLOAT)


def dot_left(left, right):
    return lax.dot_general(left, right, (((0,), (0,)), ((), ())), preferred_element_type=FLOAT)


def dot_right(left, right):
    return lax.dot_general(left, right, (((1,), (1,)), ((), ())), preferred_element_type=FLOAT)


def normalize(stream):
    centred = stream - jnp.mean(stream, axis=-1, keepdims=True)
    inverse = lax.rsqrt(jnp.mean(centred * centred, axis=-1, keepdims=True) + EPSILON)
    return centred * inverse, inverse


def layer_norm(stream, norms, index):
    unit, _ = normalize(stream)
    return (unit * norms[index : index + 1] + norms[index + 3 : index + 4]).astype(BFLOAT)


def norm_backward(grad_out, stream, gain):
    unit, inverse = normalize(stream)
    scaled = grad_out * gain
    inner = (
        scaled
        - jnp.mean(scaled, axis=-1, keepdims=True)
        - unit * jnp.mean(scaled * unit, axis=-1, keepdims=True)
    )
    sums = jnp.concatenate(
        [
            jnp.sum(grad_out * unit, axis=0, keepdims=True),
            jnp.sum(grad_out, axis=0, keepdims=True),
            jnp.zeros((6, grad_out.shape[1]), FLOAT),
        ]
    )
    return inverse * inner, sums


def add_parts(own_ref, other_ref):
    return own_ref[...].astype(FLOAT) + other_ref[...].astype(FLOAT)


def softmax(query, key, mask):
    scores = jnp.where(mask, dot_right(query, key) * SCALING, NEGATIVE)
    expo_scores = jnp.exp(scores - jnp.max(scores, axis=-1, keepdims=True))
    return expo_scores / jnp.sum(expo_scores, axis=-1, keepdims=True)


def head_backward(query, key, value, mask, grad_mixed):
    weights = softmax(query, key, mask)
    grad_value = dot_left(weights.astype(BFLOAT), grad_mixed)
    grad_weights = dot_right(grad_mixed, value)
    grad_scores = weights * (
        grad_weights - jnp.sum(weights * grad_weights, axis=-1, keepdims=True)
    )
    grad_scores = grad_scores.astype(BFLOAT)
    grad_query = dot(grad_scores, key) * SCALING
    grad_key = dot_left(grad_scores, query) * SCALING
    return grad_query.astype(BFLOAT), grad_key.astype(BFLOAT), grad_value.astype(BFLOAT)


def head(ref, place):
    return ref[:, place * HEAD_DIM : (place + 1) * HEAD_DIM]


def self_forward_kernel(stream, norms, own, other, mask, rows, qkv, mixed, part):
    allowed = mask[...] > 0.5
    normed = layer_norm(stream[...], norms, 0)
    rows[...] = normed
    quarter = mixed.shape[1] // 2
    width = 3 * quarter
    total = None
    for side, weights in enumerate((own, other)):
        qkv[:, side * width : (side + 1) * width] = dot(normed, weights[:, :width]).astype(BFLOAT)
        first = side * quarter // HEAD_DIM
        for i in range(first, first + quarter // HEAD_DIM):
            weight = softmax(head(qkv, 3 * i), head(qkv, 3 * i + 1), allowed)
            out = dot(weight.astype(BFLOAT), head(qkv, 3 * i + 2))
            mixed[:, i * HEAD_DIM : (i + 1) * HEAD_DIM] = out.astype(BFLOAT)
        term = dot_right(
            mixed[:, side * quarter : (side + 1) * quarter], weights[:, width : width + quarter]
        )
        total = term if total is None else total + term
    part[...] = total.astype(BFLOAT)


def accumulate(total, term, part):
    step = pl.program_id(0)

    @pl.when(step == 0)
    def _():
        total[...] = term

    @pl.when(step > 0)
    def _():
        total[...] += term

    @pl.when(step == pl.num_programs(0) - 1)
    def _():
        part[...] = total[...].astype(BFLOAT)


def ffn_forward_kernel(
    decoder, stream, own, other, norms, up_own, up_other, down_own, down_other,
    after, rows, hidden_own, hidden_other, active_own, active_other, part, total,
):
    @pl.when(pl.program_id(0) == 0)
    def _():
        after[...] = stream[...] + add_parts(own, other)
        rows[...] = layer_norm(after[...], norms, 2)

    @pl.when(decoder[0] == 0)
    def _():
        term = None
        for up, down, hidden, active in (
            (up_own, down_own, hidden_own, active_own),
            (up_other, down_other, hidden_other, active_other),
        ):
            raised = dot(rows[...], up[...])
            hidden[...] = raised
            active[...] = gelu_tanh(raised).astype(BFLOAT)
            piece = dot_right(active[...], down[...])
            term = piece if term is None else term + piece
        accumulate(total, term, part)


def ffn_both_kernel(
    decoder, stream, own, other, norms, cotangent, up_own, up_other, down_own, down_other,
    after, rows, active_own, active_other, grad_own, grad_other, part, total,
):
    @pl.when(decoder[0] == 1)
    def _():
        @pl.when(pl.program_id(0) == 0)
        def _():
            after[...] = stream[...] + add_parts(own, other)
            rows[...] = layer_norm(after[...], norms, 2)

        term = None
        for up, down, active, grad in (
            (up_own, down_own, active_own, grad_own),
            (up_other, down_other, active_other, grad_other),
        ):
            raised = dot(rows[...], up[...])
            active[...] = gelu_tanh(raised).astype(BFLOAT)
            grad[...] = (dot(cotangent[...], down[...]) * gelu_slope(raised)).astype(BFLOAT)
            piece = dot_right(grad[...], up[...])
            term = piece if term is None else term + piece
        accumulate(total, term, part)


def ffn_down_kernel(decoder, after_this, active_own, active_other, down_own, down_other, part, total):
    @pl.when(decoder[0] == 1)
    def _():
        term = dot_right(active_own[...], down_own[...]) + dot_right(active_other[...], down_other[...])
        accumulate(total, term, part)


def sort_rows(gathered, ordered, columns):
    depth = ordered.shape[0]
    piece = depth // 32
    first, to = columns
    wide = to.stop - to.start
    for i in range(16):
        for j in range(2):
            start = j * depth // 2 + i * piece
            ordered[start : start + piece, to] = gathered[
                (2 * i + j) * piece : (2 * i + j + 1) * piece, first : first + wide
            ]


def memory_kernel(
    decoder, stream, own, other, norms, late, encoded, memory, keyvals, weights
):
    wide = weights.shape[1] // 2
    half = wide // 2
    base = late.shape[1] - 2 * wide

    @pl.when(decoder[0] == 1)
    def _():
        for side in range(2):
            for part in range(2):
                start = part * wide + side * half
                sort_rows(late, weights, (base + side * wide + part * half, slice(start, start + half)))

    @pl.when(decoder[0] == 0)
    def _():
        sort_rows(late, weights, (base, slice(0, 2 * wide)))
        encoded[...] = stream[...] + add_parts(own, other)
        memory[...] = layer_norm(encoded[...], norms, 1)
        keyvals[...] = dot(memory[...], weights[...]).astype(BFLOAT)


def query_kernel(decoder, stream, own, other, norms, weights, after, rows, queries):
    @pl.when(decoder[0] == 1)
    def _():
        after[...] = stream[...] + add_parts(own, other)
        rows[...] = layer_norm(after[...], norms, 1)
        queries[...] = dot(rows[...], weights[:, : queries.shape[1]]).astype(BFLOAT)


def cross_forward_kernel(decoder, queries, keyvals, mask, weights, mixed, part):
    @pl.when(decoder[0] == 1)
    def _():
        allowed = mask[...] > 0.5
        for i in range(queries.shape[1] // HEAD_DIM):
            weight = softmax(head(queries, i), head(keyvals, 2 * i), allowed)
            out = dot(weight.astype(BFLOAT), head(keyvals, 2 * i + 1))
            mixed[:, i * HEAD_DIM : (i + 1) * HEAD_DIM] = out.astype(BFLOAT)
        part[...] = dot_right(mixed[...], weights[:, queries.shape[1] :]).astype(BFLOAT)


def memory_ffn_backward_kernel(
    decoder, cotangent, own, other, stream, norms, hidden_own, hidden_other, down_own, down_other,
    grad, low, sums, grad_own, grad_other, unused,
):
    @pl.when(decoder[0] == 0)
    def _():
        @pl.when(pl.program_id(0) == 0)
        def _():
            into, totals = norm_backward(
                cotangent[...].astype(FLOAT) + add_parts(own, other), stream[...], norms[1:2]
            )
            grad[...] = into
            low[...] = into.astype(BFLOAT)
            sums[...] = totals

        for down, hidden, out in ((down_own, hidden_own, grad_own), (down_other, hidden_other, grad_other)):
            out[...] = (dot(low[...], down[...]) * gelu_slope(hidden[...])).astype(BFLOAT)


def ffn_up_kernel(decoder, after_this, grad_own, grad_other, up_own, up_other, part, total):
    @pl.when(decoder[0] == 0)
    def _():
        term = dot_right(grad_own[...], up_own[...]) + dot_right(grad_other[...], up_other[...])
        accumulate(total, term, part)


def cross_backward_kernel(
    decoder, cotangent, own, other, stream, norms, queries, keyvals, mask, weights,
    grad, low, sums, grad_queries, grad_keyvals, part,
):
    @pl.when(decoder[0] == 1)
    def _():
        allowed = mask[...] > 0.5
        into, totals = norm_backward(add_parts(own, other), stream[...], norms[2:3])
        grad[...] = cotangent[...].astype(FLOAT) + into
        low[...] = grad[...].astype(BFLOAT)
        sums[...] = totals
        grad_mixed = dot(low[...], weights[:, queries.shape[1] :]).astype(BFLOAT)
        for i in range(queries.shape[1] // HEAD_DIM):
            one, two, three = head_backward(
                head(queries, i),
                head(keyvals, 2 * i),
                head(keyvals, 2 * i + 1),
                allowed,
                grad_mixed[:, i * HEAD_DIM : (i + 1) * HEAD_DIM],
            )
            grad_queries[:, i * HEAD_DIM : (i + 1) * HEAD_DIM] = one
            grad_keyvals[:, 2 * i * HEAD_DIM : (2 * i + 1) * HEAD_DIM] = two
            grad_keyvals[:, (2 * i + 1) * HEAD_DIM : (2 * i + 2) * HEAD_DIM] = three
        part[...] = dot_right(grad_queries[...], weights[:, : queries.shape[1]]).astype(BFLOAT)


def keyval_backward_kernel(decoder, grad_keyvals, weights, after_this, part):
    @pl.when(decoder[0] == 0)
    def _():
        part[...] = dot_right(grad_keyvals[...], weights[...]).astype(BFLOAT)


def self_gradient_kernel(
    decoder, grad_enc, own_enc, other_enc, grad_dec, own_dec, other_dec, stream, norms, grad, low, sums
):
    @pl.when(decoder[0] == 1)
    def _():
        into, totals = norm_backward(add_parts(own_dec, other_dec), stream[...], norms[1:2])
        grad[...] = grad_dec[...] + into
        sums[...] = totals

    @pl.when(decoder[0] == 0)
    def _():
        into, totals = norm_backward(add_parts(own_enc, other_enc), stream[...], norms[2:3])
        grad[...] = grad_enc[...] + into
        sums[...] = totals

    low[...] = grad[...].astype(BFLOAT)


def self_backward_kernel(low, qkv, mask, own, other, grad_qkv, part):
    allowed = mask[...] > 0.5
    quarter = qkv.shape[1] // 6
    width = 3 * quarter
    total = None
    for side, weights in enumerate((own, other)):
        grad_mixed = dot(low[...], weights[:, width : width + quarter]).astype(BFLOAT)
        first = side * quarter // HEAD_DIM
        for j in range(quarter // HEAD_DIM):
            i = first + j
            grads = head_backward(
                head(qkv, 3 * i),
                head(qkv, 3 * i + 1),
                head(qkv, 3 * i + 2),
                allowed,
                grad_mixed[:, j * HEAD_DIM : (j + 1) * HEAD_DIM],
            )
            for k in range(3):
                grad_qkv[:, (3 * i + k) * HEAD_DIM : (3 * i + k + 1) * HEAD_DIM] = grads[k]
        term = dot_right(grad_qkv[:, side * width : (side + 1) * width], weights[:, :width])
        total = term if total is None else total + term
    part[...] = total.astype(BFLOAT)


def input_backward_kernel(
    decoder, grad, own, other, stream, norms, last, one_enc, two_dec, grad_input, sums
):
    into, zero = norm_backward(add_parts(own, other), stream[...], norms[0:1])
    grad_input[...] = grad[...] + into
    is_decoder = decoder[0] == 1
    one = jnp.where(is_decoder, last[...], one_enc[...])
    two = jnp.where(is_decoder, two_dec[...], last[...])
    sums[...] = jnp.concatenate(
        [zero[0:1], one[0:1], two[0:1], zero[1:2], one[1:2], two[1:2], jnp.zeros((2, zero.shape[1]), FLOAT)]
    )


def early_weights_kernel(
    decoder, rows_enc, rows_dec, low_enc, low_dec, rows_two_low, rows_two_high, low_two_low, low_two_high,
    memory_low, memory_high, hidden_enc_own, hidden_enc_other, hidden_dec_own, hidden_dec_other,
    active_enc_own, active_enc_other, active_dec_own, active_dec_other, queries, mixed, keyvals, whole, token, slots, sems,
):
    token[...] = jnp.zeros_like(token)
    step = pl.program_id(0)
    slot = lax.rem(step, 2)
    out = slots.at[slot]
    rows = slots.shape[1]

    def copy_of(step, slot):
        start = pl.multiple_of(step * rows, rows)
        return pltpu.make_async_copy(slots.at[slot], whole.at[pl.ds(start, rows), :], sems.at[slot])

    @pl.when(step >= 2)
    def _():
        copy_of(step - 2, slot).wait()

    hidden = hidden_enc_own.shape[1]
    half = queries.shape[1]
    piece = rows_two_low.shape[1] // 4

    def put(start, value):
        out[:, start : start + value.shape[1]] = value.astype(BFLOAT)

    def put_cross(start, low, high):
        for i in range(4):
            for j, value in enumerate((low, high)):
                out[
                    (2 * i + j) * piece : (2 * i + j + 1) * piece, start : start + value.shape[1]
                ] = value[i * piece : (i + 1) * piece].astype(BFLOAT)

    @pl.when(decoder[0] == 1)
    def _():
        put(0, dot_left(rows_dec[...], hidden_dec_own[...]))
        put(hidden, dot_left(rows_dec[...], hidden_dec_other[...]))
        put(2 * hidden, dot_left(low_dec[...], active_dec_own[...]))
        put(3 * hidden, dot_left(low_dec[...], active_dec_other[...]))
        put_cross(4 * hidden, dot_left(rows_two_low[...], queries[...]), dot_left(rows_two_high[...], queries[...]))
        put_cross(4 * hidden + half, dot_left(low_two_low[...], mixed[...]), dot_left(low_two_high[...], mixed[...]))

    @pl.when(decoder[0] == 0)
    def _():
        put(0, dot_left(rows_enc[...], hidden_enc_own[...]))
        put(hidden, dot_left(rows_enc[...], hidden_enc_other[...]))
        put(2 * hidden, dot_left(low_enc[...], active_enc_own[...]))
        put(3 * hidden, dot_left(low_enc[...], active_enc_other[...]))
        put_cross(4 * hidden, dot_left(memory_low[...], keyvals[...]), dot_left(memory_high[...], keyvals[...]))

    copy_of(step, slot).start()

    @pl.when(step == pl.num_programs(0) - 1)
    def _():
        copy_of(step - 1, 1 - slot).wait()
        copy_of(step, slot).wait()


def attn_weights_kernel(
    core, rows, rows_got, rows_core, grad_qkv, grad_got, low, low_got, low_core, mixed, mixed_got, sums, sums_got,
    out, rows_all, low_all, grad_all, mixed_all,
):
    length = rows.shape[0]
    half = length // 2
    quarter = mixed_got.shape[1]
    width = 3 * quarter
    near = pl.multiple_of(length + core[0] * half, half)
    away = pl.multiple_of(length + (1 - core[0]) * half, half)
    for whole, mine, got, other in ((rows_all, rows, rows_got, rows_core), (low_all, low, low_got, low_core)):
        whole[:length, :] = mine[...]
        whole[pl.ds(near, half), :] = got[...]
        whole[pl.ds(away, half), :] = other[...]
    grad_all[:length, :] = grad_qkv[:, :width]
    grad_all[length:, :] = grad_got[...]
    mixed_all[:length, :] = mixed[:, :quarter]
    mixed_all[length:, :] = mixed_got[...]
    out[:, :width] = dot_left(rows_all[...], grad_all[...]).astype(BFLOAT)
    out[:, width : width + quarter] = dot_left(low_all[...], mixed_all[...]).astype(BFLOAT)
    totals = jnp.concatenate(
        [sums[...] + sums_got[...], jnp.zeros((NORM_COLUMNS - sums.shape[0], sums.shape[1]), FLOAT)]
    )
    out[:, width + quarter :] = totals.T.astype(BFLOAT)


def gather_plane(block):
    return lax.all_gather(block, PLANE, axis=0, tiled=True)


def scatter_plane(block):
    return lax.psum_scatter(block, PLANE, scatter_dimension=0, tiled=True)


def send_home_kernel(decoder, early, send_h, send_s, send_across):
    rows = send_s.shape[0]
    wide = send_s.shape[1]
    hidden = (early.shape[1] - 2 * wide) // 4
    half = wide // 2
    send_h[:, :hidden] = early[:, hidden : 2 * hidden]
    send_h[:, hidden : 2 * hidden] = early[:, 3 * hidden : 4 * hidden]
    start = 4 * hidden

    @pl.when(decoder[0] == 1)
    def _():
        send_h[:rows, 2 * hidden :] = early[rows:, start + half : start + 2 * half]
        send_h[rows:, 2 * hidden :] = early[rows:, start + 3 * half : start + 4 * half]
        send_s[:, :half] = early[:rows, start : start + half]
        send_s[:, half:] = early[:rows, start + 2 * half : start + 3 * half]
        send_across[:, :half] = early[:rows, start + half : start + 2 * half]
        send_across[:, half:] = early[:rows, start + 3 * half : start + 4 * half]

    @pl.when(decoder[0] == 0)
    def _():
        send_h[:rows, 2 * hidden :] = early[:rows, start + 2 * half : start + 3 * half]
        send_h[rows:, 2 * hidden :] = early[:rows, start + 3 * half : start + 4 * half]
        send_s[...] = early[rows:, start : start + 2 * half]
        send_across[...] = early[rows:, start + 2 * half :]


def bring_home_kernel(decoder, early, got_h, got_s, got_across, up, down, query, keyval, out):
    rows = got_s.shape[0]
    wide = got_s.shape[1]
    hidden = (early.shape[1] - 2 * wide) // 4
    half = wide // 2
    start = 4 * hidden
    up[0] = early[:, :hidden].astype(FLOAT) + got_h[:, :hidden].astype(FLOAT)
    down[0] = (
        early[:, 2 * hidden : 3 * hidden].astype(FLOAT) + got_h[:, hidden : 2 * hidden].astype(FLOAT)
    ).T
    far = got_s[...].astype(FLOAT) + got_across[...].astype(FLOAT)
    near_left = got_h[:rows, 2 * hidden :].astype(FLOAT)
    near_right = got_h[rows:, 2 * hidden :].astype(FLOAT)

    @pl.when(decoder[0] == 1)
    def _():
        query[...] = early[rows:, start : start + half].astype(FLOAT) + near_left
        out[...] = (early[rows:, start + 2 * half : start + 3 * half].astype(FLOAT) + near_right).T
        keyval[...] = far

    @pl.when(decoder[0] == 0)
    def _():
        keyval[:, :half] = early[:rows, start : start + half].astype(FLOAT) + near_left
        keyval[:, half:] = early[:rows, start + half : start + 2 * half].astype(FLOAT) + near_right
        query[...] = far[:, :half]
        out[...] = far[:, half:].T


def attn_home_kernel(own, qkv, out, gain, offset):
    width = qkv.shape[2]
    quarter = out.shape[1]
    qkv[0] = own[:, :width]
    out[0] = own[:, width : width + quarter].T
    sums = own[:, width + quarter :].T
    gain[0] = sums[:3]
    offset[0] = sums[3:6]


VMEM = pl.BlockSpec(memory_space=pltpu.VMEM)
SMEM = pl.BlockSpec(memory_space=pltpu.SMEM)
LIMIT = pltpu.CompilerParams(vmem_limit_bytes=28 * 1024 * 1024)
WIDE_LIMIT = pltpu.CompilerParams(vmem_limit_bytes=56 * 1024 * 1024)


def low_of(*dims):
    return jax.ShapeDtypeStruct(dims, BFLOAT)


def full_of(*dims):
    return jax.ShapeDtypeStruct(dims, FLOAT)


def run(kernel, outs, *operands, flops=0, scratch=(), flag=False, specs=None, limit=LIMIT):
    specs = specs or {}
    whole = lambda o: pl.BlockSpec(o.shape, lambda i: (0,) * len(o.shape)) if specs else VMEM
    in_specs = [specs.get(i, whole(o)) for i, o in enumerate(operands)]
    if flag:
        in_specs[0] = SMEM
    moved = sum(o.size * o.dtype.itemsize for o in (*operands, *outs))
    return pl.pallas_call(
        kernel,
        grid=(1,) if specs else (),
        out_shape=list(outs),
        in_specs=in_specs,
        out_specs=[whole(o) for o in outs],
        scratch_shapes=list(scratch),
        compiler_params=limit,
        cost_estimate=pl.CostEstimate(flops=flops, bytes_accessed=moved, transcendentals=0),
    )(*operands)


def shards(
    embedded,
    cotangent,
    lengths,
    attn_qkv,
    attn_out,
    ffn_up,
    ffn_down,
    norm_gain,
    norm_bias,
    cross_query,
    cross_kv,
    cross_out,
):
    is_decoder = lax.axis_index("s") == 1
    first_half = lax.axis_index("h") == 0
    core = lax.axis_index("c")

    def pick(flag, yes, no):
        return jnp.where(flag, yes, no)

    def own_rows(pairs):
        mine = [pick(first_half, pair[0], pair[1]) for pair in pairs]
        got = swap(jnp.concatenate([pick(first_half, pair[1], pair[0]) for pair in pairs], axis=1), "h")
        mine = jnp.concatenate(mine, axis=1)
        half = jnp.concatenate([pick(first_half, mine, got), pick(first_half, got, mine)])
        got = swap(half, "c")
        whole = jnp.concatenate([pick(core == 0, half, got), pick(core == 0, got, half)])
        return jnp.split(whole, len(pairs), axis=1)

    def to_owners(row):
        half = lax.dynamic_slice_in_dim(row, core * 2 * QUARTER, 2 * QUARTER, 0)
        low, high = half[:QUARTER], half[QUARTER:]
        mine = pick(first_half, low, high)
        got = swap(pick(first_half, high, low), "h")
        return jnp.stack([pick(first_half, mine, got), pick(first_half, got, mine)])

    qkv_width = attn_qkv.shape[2]
    out_width = attn_out.shape[1]
    attn_width = qkv_width + out_width
    ff_width = ffn_up.shape[2]
    cross_width = cross_kv.shape[1]
    half_cross = cross_width // 2
    depth = embedded.shape[-1]

    own_ffn = jnp.concatenate([ffn_up[0], ffn_down[0].T], axis=1)
    query_out = jnp.concatenate([cross_query, cross_out.T], axis=1)
    kept = pick(is_decoder, query_out, cross_kv)
    give = pick(is_decoder, cross_kv, query_out)
    own_ffn, kept, give = together(own_ffn, kept, give)
    other_ffn = swap(own_ffn, "h")
    cross = [
        jnp.concatenate([pick(is_decoder, far, near), pick(is_decoder, near, far)])
        for near, far in ((kept, swap(give, "s")), (swap(kept, "h"), swap_across(give)))
    ]
    late_pack = jnp.concatenate(
        [
            own_ffn[:, :ff_width], other_ffn[:, :ff_width], own_ffn[:, ff_width:], other_ffn[:, ff_width:],
            *cross,
        ],
        axis=1,
    )
    late_pack, attn_qkv, attn_out, norm_gain, norm_bias, embedded, cotangent = together(
        late_pack, attn_qkv, attn_out, norm_gain, norm_bias, embedded, cotangent
    )
    late_whole = gather_plane(late_pack)

    norms = jnp.concatenate([norm_gain[0], norm_bias[0]]).T
    norms = jnp.pad(norms, ((0, 0), (0, NORM_COLUMNS - norms.shape[1])))
    own_attn = jnp.concatenate([attn_qkv[0], attn_out[0].T], axis=1)
    attn_own = gather_ring_plane(jnp.concatenate([own_attn, norms], axis=1), ("z", "x"))
    attn_other = gather_ring_plane(swap(own_attn, "h"), ("x", "z"))
    values, grad_out = own_rows((embedded[0], cotangent[0]))
    values = values.astype(FLOAT)

    norms = attn_own[:, attn_width : attn_width + 8].T.astype(FLOAT)
    decoder = lax.axis_index("s").reshape(1).astype(jnp.int32)

    row_lengths = pick(first_half, lengths[:, 0, 0], lengths[:, 1, 0])
    source_pair = segment_ids(row_lengths[0])
    target_pair = segment_ids(row_lengths[1])
    own_pair = pick(is_decoder, target_pair, source_pair)
    positions = jnp.asarray(ORDER)
    ordered = (positions[None, :] <= positions[:, None]) | jnp.logical_not(is_decoder)
    allowed_self = ((own_pair[:, None] == own_pair[None, :]) & ordered).astype(BFLOAT)
    allowed_cross = (target_pair[:, None] == source_pair[None, :]).astype(BFLOAT)

    width = values.shape[1]
    steps = 2
    block = ff_width // steps
    row_block = pl.BlockSpec((ROW_LEN, width), lambda i: (0, 0))
    norm_block = pl.BlockSpec((8, width), lambda i: (0, 0))
    weight_blocks = [
        pl.BlockSpec((width, block), functools.partial(lambda start, i: (0, start * steps + i), start))
        for start in range(4)
    ]
    hidden_block = pl.BlockSpec((ROW_LEN, block), lambda i: (0, i))
    ffn_flops = 8 * ROW_LEN * width * ff_width
    hidden_full, hidden_low = full_of(ROW_LEN, ff_width), low_of(ROW_LEN, ff_width)
    row_full, row_low = full_of(ROW_LEN, width), low_of(ROW_LEN, width)

    def run_ffn(kernel, outs, out_specs, operands, in_specs, flops, weights, limit=LIMIT):
        moved = sum(o.size * o.dtype.itemsize for o in (*operands, *outs))
        moved = moved + len(weights) * 2 * width * ff_width
        return pl.pallas_call(
            kernel,
            grid=(steps,),
            out_shape=outs,
            in_specs=[*in_specs, *[weight_blocks[i] for i in weights]],
            out_specs=out_specs,
            scratch_shapes=[pltpu.VMEM((ROW_LEN, width), FLOAT)],
            compiler_params=limit,
            cost_estimate=pl.CostEstimate(flops=flops, bytes_accessed=moved, transcendentals=0),
        )(*operands, *[late_whole for i in weights])

    rows_one, qkv, mixed_one, part = run(
        self_forward_kernel,
        [
            low_of(ROW_LEN, width),
            low_of(ROW_LEN, 2 * qkv_width),
            low_of(ROW_LEN, 2 * out_width),
            low_of(ROW_LEN, width),
        ],
        values, norms, attn_own, attn_other, allowed_self,
        flops=10 * ROW_LEN * width * out_width * 2,
    )
    got = swap(part, "c")

    def rows_across(block):
        half = lax.dynamic_slice_in_dim(block, core * 2 * QUARTER, 2 * QUARTER, 0)
        got = swap(half, "h")
        return got, swap(got, "c")

    after_self, rows_enc, hidden_own, hidden_other, active_enc_own, active_enc_other, part_enc = run_ffn(
        ffn_forward_kernel,
        [row_full, row_low, hidden_full, hidden_full, hidden_low, hidden_low, row_low],
        [row_block, row_block, hidden_block, hidden_block, hidden_block, hidden_block, row_block],
        (decoder, values, part, got, norms),
        [SMEM, row_block, row_block, row_block, norm_block],
        ffn_flops,
        (0, 1, 2, 3),
    )
    encoded, memory, keyvals, cross_whole = run(
        memory_kernel,
        [row_full, row_low, low_of(ROW_LEN, 2 * cross_width), low_of(width, 2 * cross_width)],
        decoder, after_self, part_enc, swap(part_enc, "c"), norms, late_whole,
        flops=4 * ROW_LEN * width * cross_width, flag=True,
    )
    keyvals = lax.ppermute(keyvals, "s", [(0, 1)])


    after_two, rows_two, queries = run(
        query_kernel,
        [full_of(ROW_LEN, width), low_of(ROW_LEN, width), low_of(ROW_LEN, cross_width)],
        decoder, values, part, got, norms, cross_whole,
        flops=2 * ROW_LEN * width * cross_width, flag=True,
    )
    mixed_two, part_two = run(
        cross_forward_kernel,
        [low_of(ROW_LEN, cross_width), low_of(ROW_LEN, width)],
        decoder, queries, keyvals, allowed_cross, cross_whole,
        flops=4 * ROW_LEN * width * cross_width, flag=True,
    )
    after_cross, rows_dec, active_dec_own, active_dec_other, grad_dec_own, grad_dec_other, part = run_ffn(
        ffn_both_kernel,
        [row_full, row_low, hidden_low, hidden_low, hidden_low, hidden_low, row_low],
        [row_block, row_block, hidden_block, hidden_block, hidden_block, hidden_block, row_block],
        (decoder, after_two, part_two, swap(part_two, "c"), norms, grad_out),
        [SMEM, row_block, row_block, row_block, norm_block, row_block],
        ffn_flops * 3 // 2,
        (0, 1, 2, 3),
    )
    grad_dec, low_two, sums_two_dec, grad_queries, grad_keyvals, part_two = run(
        cross_backward_kernel,
        [
            full_of(ROW_LEN, width),
            low_of(ROW_LEN, width),
            full_of(8, width),
            low_of(ROW_LEN, cross_width),
            low_of(ROW_LEN, 2 * cross_width),
            low_of(ROW_LEN, width),
        ],
        decoder, grad_out, part, swap(part, "c"), after_cross, norms, queries, keyvals, allowed_cross,
        cross_whole,
        flops=8 * ROW_LEN * width * cross_width, flag=True,
    )
    (part_dec,) = run_ffn(
        ffn_down_kernel,
        [row_low],
        [row_block],
        (decoder, sums_two_dec, active_dec_own, active_dec_other),
        [SMEM, norm_block, hidden_block, hidden_block],
        ffn_flops // 2,
        (2, 3),
    )
    decoded = after_cross + part_dec.astype(FLOAT) + swap(part_dec, "c").astype(FLOAT)
    grad_keyvals = lax.ppermute(grad_keyvals, "s", [(1, 0)])
    got_two = swap(part_two, "c")

    rows_sent, mixed_sent, grad_keyvals = together(rows_one, mixed_one, grad_keyvals)
    rows_got = rows_across(rows_sent)
    mixed_got = swap(mixed_sent[:, out_width:], "h")

    (part,) = run(
        keyval_backward_kernel, [row_low], decoder, grad_keyvals, cross_whole, part_dec,
        flops=4 * ROW_LEN * width * cross_width, flag=True,
    )
    grad_enc, low_enc, sums_one_enc, grad_enc_own, grad_enc_other = run_ffn(
        memory_ffn_backward_kernel,
        [row_full, row_low, full_of(8, width), hidden_low, hidden_low],
        [row_block, row_block, norm_block, hidden_block, hidden_block],
        (decoder, grad_out, part, swap(part, "c"), encoded, norms, hidden_own, hidden_other),
        [SMEM, row_block, row_block, row_block, row_block, norm_block, hidden_block, hidden_block],
        ffn_flops // 2,
        (2, 3),
    )

    early_width = 4 * ff_width + 2 * cross_width
    row_part = pl.BlockSpec((ROW_LEN, width // 4), lambda i: (0, i))
    low_part = pl.BlockSpec((ROW_LEN, width // 8), lambda i: (0, i))
    high_part = pl.BlockSpec((ROW_LEN, width // 8), lambda i: (0, i + 4))
    whole_block = lambda columns: pl.BlockSpec((ROW_LEN, columns), lambda i: (0, 0))
    operands = (
        decoder, rows_enc, rows_dec, low_enc, grad_out, rows_two, rows_two, low_two, low_two, memory, memory,
        grad_enc_own, grad_enc_other, grad_dec_own, grad_dec_other,
        active_enc_own, active_enc_other, active_dec_own, active_dec_other,
        grad_queries, mixed_two, grad_keyvals,
    )
    grad_early, token = pl.pallas_call(
        early_weights_kernel,
        grid=(4,),
        out_shape=[pltpu.HBM((width, early_width), BFLOAT), full_of(8, 128)],
        in_specs=[
            SMEM, *[row_part] * 4, *[low_part, high_part] * 3, *[whole_block(ff_width)] * 8,
            whole_block(cross_width), whole_block(cross_width), whole_block(2 * cross_width),
        ],
        out_specs=[
            pl.BlockSpec(memory_space=pltpu.HBM),
            pl.BlockSpec((8, 128), lambda i: (0, 0)),
        ],
        scratch_shapes=[
            pltpu.VMEM((2, width // 4, early_width), BFLOAT),
            pltpu.SemaphoreType.DMA((2,)),
        ],
        compiler_params=LIMIT,
        cost_estimate=pl.CostEstimate(
            flops=2 * ROW_LEN * width * early_width, bytes_accessed=20 * 1024 * 1024, transcendentals=0
        ),
    )(*operands)
    (part_enc,) = run_ffn(
        ffn_up_kernel,
        [row_low],
        [row_block],
        (decoder, token, grad_enc_own, grad_enc_other),
        [SMEM, pl.BlockSpec((8, 128), lambda i: (0, 0)), hidden_block, hidden_block],
        ffn_flops // 2,
        (0, 1),
        WIDE_LIMIT,
    )
    got_enc = swap(part_enc, "c")
    grad_early = scatter_plane(grad_early)

    grad_self, low_self, sums_last = run(
        self_gradient_kernel,
        [row_full, row_low, full_of(8, width)],
        decoder, grad_enc, part_enc, got_enc, grad_dec, part_two, got_two, after_self, norms, flag=True,
        limit=WIDE_LIMIT,
    )
    low_got = rows_across(low_self)
    grad_qkv, part = run(
        self_backward_kernel,
        [low_of(ROW_LEN, 2 * qkv_width), row_low],
        low_self, qkv, allowed_self, attn_own, attn_other,
        flops=20 * ROW_LEN * width * out_width * 2, limit=WIDE_LIMIT,
    )
    grad_got = swap(grad_qkv[:, qkv_width:], "h")
    grad_input, sums = run(
        input_backward_kernel,
        [row_full, full_of(8, width)],
        decoder, grad_self, part, swap(part, "c"), values, norms, sums_last, sums_one_enc, sums_two_dec,
        flag=True,
    )
    core_index = core.reshape(1).astype(jnp.int32)
    (attn_grad,) = run(
        attn_weights_kernel,
        [low_of(width, attn_width + NORM_COLUMNS)],
        core_index, rows_one, *rows_got, grad_qkv, grad_got, low_self, *low_got, mixed_one, mixed_got,
        sums, swap(sums, "h"),
        flops=8 * ROW_LEN * width * out_width, flag=True,
        scratch=[
            pltpu.VMEM((2 * ROW_LEN, width), BFLOAT),
            pltpu.VMEM((2 * ROW_LEN, width), BFLOAT),
            pltpu.VMEM((2 * ROW_LEN, qkv_width), BFLOAT),
            pltpu.VMEM((2 * ROW_LEN, out_width), BFLOAT),
        ],
    )
    decoded, memory, grad_input, attn_grad = together(decoded, memory, grad_input, attn_grad)
    outputs = to_owners(pick(is_decoder, decoded.astype(BFLOAT), memory))
    grad_embedded = to_owners(grad_input)
    attn_grad = scatter_ring_plane(attn_grad, ("z", "x"))

    rows_cross = cross_query.shape[0]
    send_h, send_s, send_across = run(
        send_home_kernel,
        [
            low_of(2 * rows_cross, 2 * ff_width + half_cross),
            low_of(rows_cross, cross_width),
            low_of(rows_cross, cross_width),
        ],
        decoder, grad_early, flag=True,
    )
    total_up, total_down, total_query, total_keyval, total_cross_out = run(
        bring_home_kernel,
        [
            full_of(1, 2 * rows_cross, ff_width),
            full_of(1, ff_width, 2 * rows_cross),
            full_of(rows_cross, half_cross),
            full_of(rows_cross, cross_width),
            full_of(half_cross, rows_cross),
        ],
        decoder, grad_early, swap(send_h, "h"), swap(send_s, "s"), swap_across(send_across), flag=True,
    )
    total_qkv, total_out, total_gain, total_offset = run(
        attn_home_kernel,
        [
            full_of(1, 2 * rows_cross, qkv_width),
            full_of(1, out_width, 2 * rows_cross),
            full_of(1, 3, 2 * rows_cross),
            full_of(1, 3, 2 * rows_cross),
        ],
        attn_grad,
    )
    return (
        outputs[None],
        grad_embedded[None],
        total_qkv,
        total_out,
        total_up,
        total_down,
        total_gain,
        total_offset,
        total_query,
        total_keyval,
        total_cross_out,
    )


def solution(mesh):
    fine = Mesh(mesh.devices.reshape(2, 4, 4, 2, 2), AXES)
    tokens = ("x", "z", "h", "c")
    tensor = ("h", "c")
    whole = ("s", "x", "z")
    return jax.shard_map(
        shards,
        mesh=fine,
        in_specs=(
            P("s", None, tokens, None),
            P("s", None, tokens, None),
            P(None, None, PLANE, None),
            P("s", PLANE, tensor),
            P("s", tensor, PLANE),
            P("s", PLANE, tensor),
            P("s", tensor, PLANE),
            P("s", None, PLANE),
            P("s", None, PLANE),
            P(whole, tensor),
            P(whole, tensor),
            P(tensor, whole),
        ),
        out_specs=(
            P("s", None, tokens, None),
            P("s", None, tokens, None),
            P("s", PLANE, tensor),
            P("s", tensor, PLANE),
            P("s", PLANE, tensor),
            P("s", tensor, PLANE),
            P("s", None, PLANE),
            P("s", None, PLANE),
            P(whole, tensor),
            P(whole, tensor),
            P(tensor, whole),
        ),
        check_vma=False,
    )
```

```python
import functools

import jax
import jax.numpy as jnp
import numpy as np
from jax import lax
from jax.experimental import pallas as pl
from jax.experimental.pallas import tpu as pltpu
from jax.sharding import Mesh
from jax.sharding import PartitionSpec as P

HEAD_DIM = 64
ROW_LEN = 256
QUARTER = 64
NORM_COLUMNS = 128

EPSILON = 1e-05
NEGATIVE = -1000000000.0
SCALING = 0.125
GELU_COEF = 0.7978845608028654
BFLOAT = jnp.bfloat16
FLOAT = jnp.float32
AXES = ("s", "x", "z", "h", "c")
PLANE = ("x", "z")
ORDER = np.concatenate([np.arange(QUARTER) + QUARTER * q for q in (0, 2, 1, 3)]).astype(np.int32)


def swap(block, axis):
    return lax.ppermute(block, axis, [(0, 1), (1, 0)])


def shift(block, axis, distance):
    size = lax.axis_size(axis)
    return lax.ppermute(block, axis, [(i, (i + distance) % size) for i in range(size)])


def place(buffer, block, index, dim):
    return lax.dynamic_update_slice_in_dim(buffer, jnp.expand_dims(block, dim), index, dim)


def take(buffer, index, dim):
    return lax.dynamic_index_in_dim(buffer, index, dim, keepdims=False)


def gather_direct(block, axis):
    here = lax.axis_index(axis)
    blocks = [block, shift(block, axis, -1), shift(block, axis, 2), shift(block, axis, 1)]
    return [((here + k) % 4, block) for k, block in enumerate(blocks)]


def gather_ring(block, axis):
    here = lax.axis_index(axis)
    half = block.shape[0] // 2
    before, after = shift(block, axis, 1), shift(block, axis, -1)
    far = jnp.concatenate([shift(before[:half], axis, 1), shift(after[half:], axis, -1)])
    return [((here + k) % 4, block) for k, block in enumerate([block, after, far, before])]


def gather_ring_plane(block, axes):
    near, far = axes
    rows, columns = block.shape
    first = jnp.zeros((4, rows, columns), block.dtype)
    for index, piece in gather_direct(block, near):
        first = place(first, piece, index, 0)
    whole = jnp.zeros((4, 4, rows, columns), block.dtype)
    dim = PLANE.index(far)
    for index, piece in gather_ring(first, far):
        whole = place(whole, piece, index, dim)
    return whole.reshape(-1, columns)


def together(*arrays):
    return lax.optimization_barrier(arrays)


def scatter_direct(blocks, axis):
    here = lax.axis_index(axis)
    parts = [take(blocks, (here + k) % 4, 0) for k in range(4)]
    total = parts[0].astype(FLOAT)
    for distance in (1, 2, -1):
        total = total + shift(parts[distance % 4].astype(BFLOAT), axis, distance).astype(FLOAT)
    return total


def scatter_ring(blocks, axis, dim):
    here = lax.axis_index(axis)
    own, after, far, before = [take(blocks, (here + k) % 4, dim) for k in range(4)]
    half = own.shape[0] // 2
    far = far.astype(BFLOAT)
    top = shift(far[:half], axis, 1).astype(FLOAT)
    bottom = shift(far[half:], axis, -1).astype(FLOAT)
    after = jnp.concatenate([after[:half].astype(FLOAT) + top, after[half:].astype(FLOAT)])
    before = jnp.concatenate([before[:half].astype(FLOAT), before[half:].astype(FLOAT) + bottom])
    from_before = shift(after.astype(BFLOAT), axis, 1).astype(FLOAT)
    from_after = shift(before.astype(BFLOAT), axis, -1).astype(FLOAT)
    return own.astype(FLOAT) + from_before + from_after


def scatter_ring_plane(block, axes):
    near, far = axes
    rows = block.shape[0] // 16
    blocks = block.reshape(4, 4, rows, -1)
    return scatter_direct(scatter_ring(blocks, far, PLANE.index(far)), near)


def swap_across(block):
    return lax.ppermute(block, ("s", "h"), [(0, 3), (3, 0), (1, 2), (2, 1)])


def gelu_tanh(values):
    return (
        0.5 * values * (1.0 + jnp.tanh(GELU_COEF * (values + 0.044715 * values * values * values)))
    )


def gelu_slope(values):
    squares = values * values
    curve = jnp.tanh(GELU_COEF * (values + 0.044715 * values * squares))
    return 0.5 * (1.0 + curve) + 0.5 * values * (1.0 - curve * curve) * (
        GELU_COEF * (1.0 + 3.0 * 0.044715 * squares)
    )


def segment_ids(lengths_row):
    ends = jnp.cumsum(lengths_row)
    positions = jnp.asarray(ORDER)
    return jnp.sum((positions[:, None] >= ends[None, :]).astype(jnp.int32), axis=1)


def dot(left, right):
    return jnp.dot(left, right, preferred_element_type=FLOAT)


def dot_left(left, right):
    return lax.dot_general(left, right, (((0,), (0,)), ((), ())), preferred_element_type=FLOAT)


def dot_right(left, right):
    return lax.dot_general(left, right, (((1,), (1,)), ((), ())), preferred_element_type=FLOAT)


def normalize(stream):
    centred = stream - jnp.mean(stream, axis=-1, keepdims=True)
    inverse = lax.rsqrt(jnp.mean(centred * centred, axis=-1, keepdims=True) + EPSILON)
    return centred * inverse, inverse


def layer_norm(stream, norms, index):
    unit, _ = normalize(stream)
    return (unit * norms[index : index + 1] + norms[index + 3 : index + 4]).astype(BFLOAT)


def norm_backward(grad_out, stream, gain):
    unit, inverse = normalize(stream)
    scaled = grad_out * gain
    inner = (
        scaled
        - jnp.mean(scaled, axis=-1, keepdims=True)
        - unit * jnp.mean(scaled * unit, axis=-1, keepdims=True)
    )
    sums = jnp.concatenate(
        [
            jnp.sum(grad_out * unit, axis=0, keepdims=True),
            jnp.sum(grad_out, axis=0, keepdims=True),
            jnp.zeros((6, grad_out.shape[1]), FLOAT),
        ]
    )
    return inverse * inner, sums


def add_parts(own_ref, other_ref):
    return own_ref[...].astype(FLOAT) + other_ref[...].astype(FLOAT)


def softmax(query, key, mask):
    scores = jnp.where(mask, dot_right(query, key) * SCALING, NEGATIVE)
    expo_scores = jnp.exp(scores - jnp.max(scores, axis=-1, keepdims=True))
    return expo_scores / jnp.sum(expo_scores, axis=-1, keepdims=True)


def head_backward(query, key, value, mask, grad_mixed):
    weights = softmax(query, key, mask)
    grad_value = dot_left(weights.astype(BFLOAT), grad_mixed)
    grad_weights = dot_right(grad_mixed, value)
    grad_scores = weights * (
        grad_weights - jnp.sum(weights * grad_weights, axis=-1, keepdims=True)
    )
    grad_scores = grad_scores.astype(BFLOAT)
    grad_query = dot(grad_scores, key) * SCALING
    grad_key = dot_left(grad_scores, query) * SCALING
    return grad_query.astype(BFLOAT), grad_key.astype(BFLOAT), grad_value.astype(BFLOAT)


def head(ref, place):
    return ref[:, place * HEAD_DIM : (place + 1) * HEAD_DIM]


def put_halves(place, whole, mine, others):
    length = mine.shape[0]
    whole[pl.ds(pl.multiple_of(place[1] * length, length), length), :] = mine[...].astype(whole.dtype)
    whole[pl.ds(pl.multiple_of((1 - place[1]) * length, length), length), :] = others[...].astype(
        whole.dtype
    )


def take_halves(place, whole, keep, send):
    length = keep.shape[0]
    keep[...] = whole[pl.ds(pl.multiple_of(place[1] * length, length), length), :]
    send[...] = whole[pl.ds(pl.multiple_of((1 - place[1]) * length, length), length), :].astype(BFLOAT)


def self_forward_kernel(
    place, stream, partner, norms, weights, mask, mask_partner,
    rows, rows_partner, qkv, qkv_partner, mixed, mixed_partner, part, keep, send, total,
):
    quarter = mixed.shape[1]
    width = 3 * quarter
    rows[...] = layer_norm(stream[...], norms, 0)
    rows_partner[...] = layer_norm(partner[...].astype(FLOAT), norms, 0)
    for row, heads, mixes, allow in (
        (rows, qkv, mixed, mask), (rows_partner, qkv_partner, mixed_partner, mask_partner)
    ):
        allowed = allow[...] > 0.5
        heads[...] = dot(row[...], weights[:, :width]).astype(BFLOAT)
        for i in range(quarter // HEAD_DIM):
            weight = softmax(head(heads, 3 * i), head(heads, 3 * i + 1), allowed)
            out = dot(weight.astype(BFLOAT), head(heads, 3 * i + 2))
            mixes[:, i * HEAD_DIM : (i + 1) * HEAD_DIM] = out.astype(BFLOAT)
    part[...] = dot_right(mixed[...], weights[:, width : width + quarter]).astype(BFLOAT)
    total[...] = dot_right(mixed_partner[...], weights[:, width : width + quarter])
    take_halves(place, total, keep, send)


def combine_kernel(place, stream, own, other, got, got_core, after):
    put_halves(place, after, got, got_core)
    after[...] += stream[...] + add_parts(own, other)


def accumulate(total, term, part):
    step = pl.program_id(0)

    @pl.when(step == 0)
    def _():
        total[...] = term

    @pl.when(step > 0)
    def _():
        total[...] += term

    @pl.when(step == pl.num_programs(0) - 1)
    def _():
        part[...] = total[...].astype(BFLOAT)


def ffn_forward_kernel(
    decoder, stream, norms, up_own, up_other, down_own, down_other,
    rows, hidden_own, hidden_other, active_own, active_other, part, total,
):
    @pl.when(pl.program_id(0) == 0)
    def _():
        rows[...] = layer_norm(stream[...], norms, 2)

    @pl.when(decoder[0] == 0)
    def _():
        term = None
        for up, down, hidden, active in (
            (up_own, down_own, hidden_own, active_own),
            (up_other, down_other, hidden_other, active_other),
        ):
            raised = dot(rows[...], up[...])
            hidden[...] = raised
            active[...] = gelu_tanh(raised).astype(BFLOAT)
            piece = dot_right(active[...], down[...])
            term = piece if term is None else term + piece
        accumulate(total, term, part)


def ffn_both_kernel(
    decoder, stream, own, other, norms, cotangent, up_own, up_other, down_own, down_other,
    after, rows, active_own, active_other, grad_own, grad_other, part, total,
):
    @pl.when(decoder[0] == 1)
    def _():
        @pl.when(pl.program_id(0) == 0)
        def _():
            after[...] = stream[...] + add_parts(own, other)
            rows[...] = layer_norm(after[...], norms, 2)

        term = None
        for up, down, active, grad in (
            (up_own, down_own, active_own, grad_own),
            (up_other, down_other, active_other, grad_other),
        ):
            raised = dot(rows[...], up[...])
            active[...] = gelu_tanh(raised).astype(BFLOAT)
            grad[...] = (dot(cotangent[...], down[...]) * gelu_slope(raised)).astype(BFLOAT)
            piece = dot_right(grad[...], up[...])
            term = piece if term is None else term + piece
        accumulate(total, term, part)


def ffn_down_kernel(decoder, after_this, active_own, active_other, down_own, down_other, part, total):
    @pl.when(decoder[0] == 1)
    def _():
        term = dot_right(active_own[...], down_own[...]) + dot_right(active_other[...], down_other[...])
        accumulate(total, term, part)


def sort_rows(gathered, ordered, columns):
    depth = ordered.shape[0]
    piece = depth // 32
    first, to = columns
    wide = to.stop - to.start
    for i in range(16):
        for j in range(2):
            start = j * depth // 2 + i * piece
            ordered[start : start + piece, to] = gathered[
                (2 * i + j) * piece : (2 * i + j + 1) * piece, first : first + wide
            ]


def memory_kernel(
    decoder, stream, own, other, norms, late, encoded, memory, keyvals, weights
):
    wide = weights.shape[1] // 2
    half = wide // 2
    base = late.shape[1] - 2 * wide

    @pl.when(decoder[0] == 1)
    def _():
        for side in range(2):
            for part in range(2):
                start = part * wide + side * half
                sort_rows(late, weights, (base + side * wide + part * half, slice(start, start + half)))

    @pl.when(decoder[0] == 0)
    def _():
        sort_rows(late, weights, (base, slice(0, 2 * wide)))
        encoded[...] = stream[...] + add_parts(own, other)
        memory[...] = layer_norm(encoded[...], norms, 1)
        keyvals[...] = dot(memory[...], weights[...]).astype(BFLOAT)


def query_kernel(decoder, stream, norms, weights, rows, queries):
    @pl.when(decoder[0] == 1)
    def _():
        rows[...] = layer_norm(stream[...], norms, 1)
        queries[...] = dot(rows[...], weights[:, : queries.shape[1]]).astype(BFLOAT)


def cross_forward_kernel(decoder, queries, keyvals, mask, weights, mixed, part):
    @pl.when(decoder[0] == 1)
    def _():
        allowed = mask[...] > 0.5
        for i in range(queries.shape[1] // HEAD_DIM):
            weight = softmax(head(queries, i), head(keyvals, 2 * i), allowed)
            out = dot(weight.astype(BFLOAT), head(keyvals, 2 * i + 1))
            mixed[:, i * HEAD_DIM : (i + 1) * HEAD_DIM] = out.astype(BFLOAT)
        part[...] = dot_right(mixed[...], weights[:, queries.shape[1] :]).astype(BFLOAT)


def memory_ffn_backward_kernel(
    decoder, cotangent, own, other, stream, norms, hidden_own, hidden_other, down_own, down_other,
    grad, low, sums, grad_own, grad_other, unused,
):
    @pl.when(decoder[0] == 0)
    def _():
        @pl.when(pl.program_id(0) == 0)
        def _():
            into, totals = norm_backward(
                cotangent[...].astype(FLOAT) + add_parts(own, other), stream[...], norms[1:2]
            )
            grad[...] = into
            low[...] = into.astype(BFLOAT)
            sums[...] = totals

        for down, hidden, out in ((down_own, hidden_own, grad_own), (down_other, hidden_other, grad_other)):
            out[...] = (dot(low[...], down[...]) * gelu_slope(hidden[...])).astype(BFLOAT)


def ffn_up_kernel(decoder, after_this, grad_own, grad_other, up_own, up_other, part, total):
    @pl.when(decoder[0] == 0)
    def _():
        term = dot_right(grad_own[...], up_own[...]) + dot_right(grad_other[...], up_other[...])
        accumulate(total, term, part)


def cross_backward_kernel(
    decoder, cotangent, own, other, stream, norms, queries, keyvals, mask, weights,
    grad, low, sums, grad_queries, grad_keyvals, part,
):
    @pl.when(decoder[0] == 1)
    def _():
        allowed = mask[...] > 0.5
        into, totals = norm_backward(add_parts(own, other), stream[...], norms[2:3])
        grad[...] = cotangent[...].astype(FLOAT) + into
        low[...] = grad[...].astype(BFLOAT)
        sums[...] = totals
        grad_mixed = dot(low[...], weights[:, queries.shape[1] :]).astype(BFLOAT)
        for i in range(queries.shape[1] // HEAD_DIM):
            one, two, three = head_backward(
                head(queries, i),
                head(keyvals, 2 * i),
                head(keyvals, 2 * i + 1),
                allowed,
                grad_mixed[:, i * HEAD_DIM : (i + 1) * HEAD_DIM],
            )
            grad_queries[:, i * HEAD_DIM : (i + 1) * HEAD_DIM] = one
            grad_keyvals[:, 2 * i * HEAD_DIM : (2 * i + 1) * HEAD_DIM] = two
            grad_keyvals[:, (2 * i + 1) * HEAD_DIM : (2 * i + 2) * HEAD_DIM] = three
        part[...] = dot_right(grad_queries[...], weights[:, : queries.shape[1]]).astype(BFLOAT)


def keyval_backward_kernel(decoder, grad_keyvals, weights, after_this, part):
    @pl.when(decoder[0] == 0)
    def _():
        part[...] = dot_right(grad_keyvals[...], weights[...]).astype(BFLOAT)


def self_gradient_kernel(
    place, grad_enc, own_enc, other_enc, grad_dec, own_dec, other_dec, stream, norms, grad, low, low_half, sums
):
    @pl.when(place[0] == 1)
    def _():
        into, totals = norm_backward(add_parts(own_dec, other_dec), stream[...], norms[1:2])
        grad[...] = grad_dec[...] + into
        sums[...] = totals

    @pl.when(place[0] == 0)
    def _():
        into, totals = norm_backward(add_parts(own_enc, other_enc), stream[...], norms[2:3])
        grad[...] = grad_enc[...] + into
        sums[...] = totals

    low[...] = grad[...].astype(BFLOAT)
    half = low_half.shape[0]
    low_half[...] = low[pl.ds(pl.multiple_of(place[1] * half, half), half), :]


def row_backward(low, qkv, mask, weights, grad_qkv):
    allowed = mask[...] > 0.5
    quarter = qkv.shape[1] // 3
    width = 3 * quarter
    grad_mixed = dot(low[...], weights[:, width : width + quarter]).astype(BFLOAT)
    for i in range(quarter // HEAD_DIM):
        grads = head_backward(
            head(qkv, 3 * i),
            head(qkv, 3 * i + 1),
            head(qkv, 3 * i + 2),
            allowed,
            grad_mixed[:, i * HEAD_DIM : (i + 1) * HEAD_DIM],
        )
        for k in range(3):
            grad_qkv[:, (3 * i + k) * HEAD_DIM : (3 * i + k + 1) * HEAD_DIM] = grads[k]
    return dot_right(grad_qkv[...], weights[:, :width])


def self_backward_kernel(low, qkv, mask, weights, grad_qkv, part):
    part[...] = row_backward(low, qkv, mask, weights, grad_qkv).astype(BFLOAT)


def partner_backward_kernel(
    place, low_got, low_core, qkv, mask, weights, low, grad_qkv, keep, send, total
):
    put_halves(place, low, low_got, low_core)
    total[...] = row_backward(low, qkv, mask, weights, grad_qkv)
    take_halves(place, total, keep, send)


def input_backward_kernel(
    place, grad, own, other, got, got_core, stream, norms, last, one_enc, two_dec, grad_input, sums, total
):
    put_halves(place, total, got, got_core)
    into, zero = norm_backward(total[...] + add_parts(own, other), stream[...], norms[0:1])
    grad_input[...] = grad[...] + into
    is_decoder = place[0] == 1
    one = jnp.where(is_decoder, last[...], one_enc[...])
    two = jnp.where(is_decoder, two_dec[...], last[...])
    sums[...] = jnp.concatenate(
        [zero[0:1], one[0:1], two[0:1], zero[1:2], one[1:2], two[1:2], jnp.zeros((2, zero.shape[1]), FLOAT)]
    )


def early_weights_kernel(
    decoder, rows_enc, rows_dec, low_enc, low_dec, rows_two_low, rows_two_high, low_two_low, low_two_high,
    memory_low, memory_high, hidden_enc_own, hidden_enc_other, hidden_dec_own, hidden_dec_other,
    active_enc_own, active_enc_other, active_dec_own, active_dec_other, queries, mixed, keyvals, whole, token, slots, sems,
):
    token[...] = jnp.zeros_like(token)
    step = pl.program_id(0)
    slot = lax.rem(step, 2)
    out = slots.at[slot]
    rows = slots.shape[1]

    def copy_of(step, slot):
        start = pl.multiple_of(step * rows, rows)
        return pltpu.make_async_copy(slots.at[slot], whole.at[pl.ds(start, rows), :], sems.at[slot])

    @pl.when(step >= 2)
    def _():
        copy_of(step - 2, slot).wait()

    hidden = hidden_enc_own.shape[1]
    half = queries.shape[1]
    piece = rows_two_low.shape[1] // 4

    def put(start, value):
        out[:, start : start + value.shape[1]] = value.astype(BFLOAT)

    def put_cross(start, low, high):
        for i in range(4):
            for j, value in enumerate((low, high)):
                out[
                    (2 * i + j) * piece : (2 * i + j + 1) * piece, start : start + value.shape[1]
                ] = value[i * piece : (i + 1) * piece].astype(BFLOAT)

    @pl.when(decoder[0] == 1)
    def _():
        put(0, dot_left(rows_dec[...], hidden_dec_own[...]))
        put(hidden, dot_left(rows_dec[...], hidden_dec_other[...]))
        put(2 * hidden, dot_left(low_dec[...], active_dec_own[...]))
        put(3 * hidden, dot_left(low_dec[...], active_dec_other[...]))
        put_cross(4 * hidden, dot_left(rows_two_low[...], queries[...]), dot_left(rows_two_high[...], queries[...]))
        put_cross(4 * hidden + half, dot_left(low_two_low[...], mixed[...]), dot_left(low_two_high[...], mixed[...]))

    @pl.when(decoder[0] == 0)
    def _():
        put(0, dot_left(rows_enc[...], hidden_enc_own[...]))
        put(hidden, dot_left(rows_enc[...], hidden_enc_other[...]))
        put(2 * hidden, dot_left(low_enc[...], active_enc_own[...]))
        put(3 * hidden, dot_left(low_enc[...], active_enc_other[...]))
        put_cross(4 * hidden, dot_left(memory_low[...], keyvals[...]), dot_left(memory_high[...], keyvals[...]))

    copy_of(step, slot).start()

    @pl.when(step == pl.num_programs(0) - 1)
    def _():
        copy_of(step - 1, 1 - slot).wait()
        copy_of(step, slot).wait()


def attn_weights_kernel(
    rows, rows_partner, grad_qkv, grad_qkv_partner, low, low_partner, mixed, mixed_partner, out
):
    width = grad_qkv.shape[1]
    out[:, :width] = (
        dot_left(rows[...], grad_qkv[...]) + dot_left(rows_partner[...], grad_qkv_partner[...])
    ).astype(BFLOAT)
    out[:, width:] = (
        dot_left(low[...], mixed[...]) + dot_left(low_partner[...], mixed_partner[...])
    ).astype(BFLOAT)


def gather_plane(block):
    return lax.all_gather(block, PLANE, axis=0, tiled=True)


def scatter_plane(block):
    return lax.psum_scatter(block, PLANE, scatter_dimension=0, tiled=True)


def send_home_kernel(decoder, early, send_h, send_s, send_across):
    rows = send_s.shape[0]
    wide = send_s.shape[1]
    hidden = (early.shape[1] - 2 * wide) // 4
    half = wide // 2
    send_h[:, :hidden] = early[:, hidden : 2 * hidden]
    send_h[:, hidden : 2 * hidden] = early[:, 3 * hidden : 4 * hidden]
    start = 4 * hidden

    @pl.when(decoder[0] == 1)
    def _():
        send_h[:rows, 2 * hidden :] = early[rows:, start + half : start + 2 * half]
        send_h[rows:, 2 * hidden :] = early[rows:, start + 3 * half : start + 4 * half]
        send_s[:, :half] = early[:rows, start : start + half]
        send_s[:, half:] = early[:rows, start + 2 * half : start + 3 * half]
        send_across[:, :half] = early[:rows, start + half : start + 2 * half]
        send_across[:, half:] = early[:rows, start + 3 * half : start + 4 * half]

    @pl.when(decoder[0] == 0)
    def _():
        send_h[:rows, 2 * hidden :] = early[:rows, start + 2 * half : start + 3 * half]
        send_h[rows:, 2 * hidden :] = early[:rows, start + 3 * half : start + 4 * half]
        send_s[...] = early[rows:, start : start + 2 * half]
        send_across[...] = early[rows:, start + 2 * half :]


def bring_home_kernel(decoder, early, got_h, got_s, got_across, up, down, query, keyval, out):
    rows = got_s.shape[0]
    wide = got_s.shape[1]
    hidden = (early.shape[1] - 2 * wide) // 4
    half = wide // 2
    start = 4 * hidden
    up[0] = early[:, :hidden].astype(FLOAT) + got_h[:, :hidden].astype(FLOAT)
    down[0] = early[:, 2 * hidden : 3 * hidden].astype(FLOAT) + got_h[:, hidden : 2 * hidden].astype(FLOAT)
    far = got_s[...].astype(FLOAT) + got_across[...].astype(FLOAT)
    near_left = got_h[:rows, 2 * hidden :].astype(FLOAT)
    near_right = got_h[rows:, 2 * hidden :].astype(FLOAT)

    @pl.when(decoder[0] == 1)
    def _():
        query[...] = early[rows:, start : start + half].astype(FLOAT) + near_left
        out[...] = early[rows:, start + 2 * half : start + 3 * half].astype(FLOAT) + near_right
        keyval[...] = far

    @pl.when(decoder[0] == 0)
    def _():
        keyval[:, :half] = early[:rows, start : start + half].astype(FLOAT) + near_left
        keyval[:, half:] = early[:rows, start + half : start + 2 * half].astype(FLOAT) + near_right
        query[...] = far[:, :half]
        out[...] = far[:, half:]


def attn_home_kernel(own, norms, qkv, out, gain, offset):
    width = qkv.shape[2]
    qkv[0] = own[:, :width]
    out[0] = own[:, width:]
    sums = norms[...].T
    gain[0] = sums[:3]
    offset[0] = sums[3:6]


VMEM = pl.BlockSpec(memory_space=pltpu.VMEM)
SMEM = pl.BlockSpec(memory_space=pltpu.SMEM)
LIMIT = pltpu.CompilerParams(vmem_limit_bytes=28 * 1024 * 1024)
WIDE_LIMIT = pltpu.CompilerParams(vmem_limit_bytes=56 * 1024 * 1024)


def low_of(*dims):
    return jax.ShapeDtypeStruct(dims, BFLOAT)


def full_of(*dims):
    return jax.ShapeDtypeStruct(dims, FLOAT)


def run(kernel, outs, *operands, flops=0, scratch=(), flag=False, specs=None, limit=LIMIT):
    specs = specs or {}
    whole = lambda o: pl.BlockSpec(o.shape, lambda i: (0,) * len(o.shape)) if specs else VMEM
    in_specs = [specs.get(i, whole(o)) for i, o in enumerate(operands)]
    if flag:
        in_specs[0] = SMEM
    moved = sum(o.size * o.dtype.itemsize for o in (*operands, *outs))
    return pl.pallas_call(
        kernel,
        grid=(1,) if specs else (),
        out_shape=list(outs),
        in_specs=in_specs,
        out_specs=[whole(o) for o in outs],
        scratch_shapes=list(scratch),
        compiler_params=limit,
        cost_estimate=pl.CostEstimate(flops=flops, bytes_accessed=moved, transcendentals=0),
    )(*operands)


def shards(
    embedded,
    cotangent,
    lengths,
    attn_qkv,
    attn_out,
    ffn_up,
    ffn_down,
    norm_gain,
    norm_bias,
    cross_query,
    cross_kv,
    cross_out,
):
    is_decoder = lax.axis_index("s") == 1
    first_half = lax.axis_index("h") == 0
    core = lax.axis_index("c")

    def pick(flag, yes, no):
        return jnp.where(flag, yes, no)

    def own_rows(pairs):
        mine = [pick(first_half, pair[0], pair[1]) for pair in pairs]
        got = swap(jnp.concatenate([pick(first_half, pair[1], pair[0]) for pair in pairs], axis=1), "h")
        mine = jnp.concatenate(mine, axis=1)
        half = jnp.concatenate([pick(first_half, mine, got), pick(first_half, got, mine)])
        got = swap(half, "c")
        whole = jnp.concatenate([pick(core == 0, half, got), pick(core == 0, got, half)])
        return jnp.split(whole, len(pairs), axis=1)

    def to_owners(row):
        half = lax.dynamic_slice_in_dim(row, core * 2 * QUARTER, 2 * QUARTER, 0)
        low, high = half[:QUARTER], half[QUARTER:]
        mine = pick(first_half, low, high)
        got = swap(pick(first_half, high, low), "h")
        return jnp.stack([pick(first_half, mine, got), pick(first_half, got, mine)])

    qkv_width = attn_qkv.shape[2]
    out_width = attn_out.shape[1]
    attn_width = qkv_width + out_width
    ff_width = ffn_up.shape[2]
    cross_width = cross_kv.shape[1]
    half_cross = cross_width // 2
    depth = embedded.shape[-1]

    own_ffn = jnp.concatenate([ffn_up[0], ffn_down[0].T], axis=1)
    query_out = jnp.concatenate([cross_query, cross_out.T], axis=1)
    kept = pick(is_decoder, query_out, cross_kv)
    give = pick(is_decoder, cross_kv, query_out)
    rows_cross = cross_query.shape[0]
    packed = jnp.concatenate([kept[:, :half_cross], kept[:, half_cross:]])
    packed, give = together(jnp.concatenate([own_ffn, packed], axis=1), give)
    other = swap(packed, "h")
    other_ffn, kept_other = other[:, : 2 * ff_width], other[:, 2 * ff_width :]
    kept_other = jnp.concatenate([kept_other[:rows_cross], kept_other[rows_cross:]], axis=1)
    cross = [
        jnp.concatenate([pick(is_decoder, far, near), pick(is_decoder, near, far)])
        for near, far in ((kept, swap(give, "s")), (kept_other, swap_across(give)))
    ]
    late_pack = jnp.concatenate(
        [
            own_ffn[:, :ff_width], other_ffn[:, :ff_width], own_ffn[:, ff_width:], other_ffn[:, ff_width:],
            *cross,
        ],
        axis=1,
    )
    late_pack, attn_qkv, attn_out, norm_gain, norm_bias, embedded, cotangent = together(
        late_pack, attn_qkv, attn_out, norm_gain, norm_bias, embedded, cotangent
    )
    late_whole = gather_plane(late_pack)

    norms = jnp.concatenate([norm_gain[0], norm_bias[0]]).T
    norms = jnp.pad(norms, ((0, 0), (0, NORM_COLUMNS - norms.shape[1])))
    attn_own = gather_ring_plane(
        jnp.concatenate([attn_qkv[0], attn_out[0].T, norms], axis=1), ("z", "x")
    )

    inputs, grads = embedded[0], cotangent[0]
    mine = jnp.concatenate([inputs[0], inputs[1], pick(first_half, grads[0], grads[1])])
    got = swap(jnp.concatenate([inputs[0], inputs[1], pick(first_half, grads[1], grads[0])]), "h")
    mine, got = (block.reshape(3, 1, QUARTER, depth) for block in (mine, got))
    half = jnp.concatenate([pick(first_half, mine, got), pick(first_half, got, mine)], axis=1)
    half = half.reshape(3, 2 * QUARTER, depth)
    got = swap(half, "c")
    whole = jnp.concatenate([pick(core == 0, half, got), pick(core == 0, got, half)], axis=1)
    values = pick(first_half, whole[0], whole[1]).astype(FLOAT)
    partner = pick(first_half, whole[1], whole[0])
    grad_out = whole[2]

    norms = attn_own[:, attn_width : attn_width + 8].T.astype(FLOAT)
    decoder = jnp.stack([lax.axis_index("s"), core]).astype(jnp.int32)

    positions = jnp.asarray(ORDER)
    ordered = (positions[None, :] <= positions[:, None]) | jnp.logical_not(is_decoder)
    masks = []
    for row_lengths in (
        pick(first_half, lengths[:, 0, 0], lengths[:, 1, 0]),
        pick(first_half, lengths[:, 1, 0], lengths[:, 0, 0]),
    ):
        source_pair = segment_ids(row_lengths[0])
        target_pair = segment_ids(row_lengths[1])
        own_pair = pick(is_decoder, target_pair, source_pair)
        masks.append(((own_pair[:, None] == own_pair[None, :]) & ordered).astype(BFLOAT))
        if len(masks) == 1:
            allowed_cross = (target_pair[:, None] == source_pair[None, :]).astype(BFLOAT)
    allowed_self, allowed_partner = masks

    width = values.shape[1]
    steps = 2
    block = ff_width // steps
    row_block = pl.BlockSpec((ROW_LEN, width), lambda i: (0, 0))
    norm_block = pl.BlockSpec((8, width), lambda i: (0, 0))
    weight_blocks = [
        pl.BlockSpec((width, block), functools.partial(lambda start, i: (0, start * steps + i), start))
        for start in range(4)
    ]
    hidden_block = pl.BlockSpec((ROW_LEN, block), lambda i: (0, i))
    ffn_flops = 8 * ROW_LEN * width * ff_width
    hidden_full, hidden_low = full_of(ROW_LEN, ff_width), low_of(ROW_LEN, ff_width)
    row_full, row_low = full_of(ROW_LEN, width), low_of(ROW_LEN, width)
    half_full, half_low = full_of(ROW_LEN // 2, width), low_of(ROW_LEN // 2, width)
    heads_low, mixed_low = low_of(ROW_LEN, qkv_width), low_of(ROW_LEN, out_width)
    row_scratch = [pltpu.VMEM((ROW_LEN, width), FLOAT)]

    def run_ffn(kernel, outs, out_specs, operands, in_specs, flops, weights, limit=LIMIT):
        moved = sum(o.size * o.dtype.itemsize for o in (*operands, *outs))
        moved = moved + len(weights) * 2 * width * ff_width
        return pl.pallas_call(
            kernel,
            grid=(steps,),
            out_shape=outs,
            in_specs=[*in_specs, *[weight_blocks[i] for i in weights]],
            out_specs=out_specs,
            scratch_shapes=[pltpu.VMEM((ROW_LEN, width), FLOAT)],
            compiler_params=limit,
            cost_estimate=pl.CostEstimate(flops=flops, bytes_accessed=moved, transcendentals=0),
        )(*operands, *[late_whole for i in weights])

    rows_one, rows_partner, qkv, qkv_partner, mixed_one, mixed_partner, part, keep, send = run(
        self_forward_kernel,
        [
            row_low, row_low, heads_low, heads_low, mixed_low, mixed_low, row_low, half_full, half_low,
        ],
        decoder, values, partner, norms, attn_own, allowed_self, allowed_partner,
        flops=10 * ROW_LEN * width * out_width * 2, flag=True, scratch=row_scratch,
    )

    def from_partner(keep, send):
        got = swap((keep + swap(send, "c").astype(FLOAT)).astype(BFLOAT), "h")
        return got, swap(got, "c")

    (after_self,) = run(
        combine_kernel, [row_full],
        decoder, values, part, swap(part, "c"), *from_partner(keep, send), flag=True,
    )

    rows_enc, hidden_own, hidden_other, active_enc_own, active_enc_other, part_enc = run_ffn(
        ffn_forward_kernel,
        [row_low, hidden_full, hidden_full, hidden_low, hidden_low, row_low],
        [row_block, hidden_block, hidden_block, hidden_block, hidden_block, row_block],
        (decoder, after_self, norms),
        [SMEM, row_block, norm_block],
        ffn_flops,
        (0, 1, 2, 3),
    )
    encoded, memory, keyvals, cross_whole = run(
        memory_kernel,
        [row_full, row_low, low_of(ROW_LEN, 2 * cross_width), low_of(width, 2 * cross_width)],
        decoder, after_self, part_enc, swap(part_enc, "c"), norms, late_whole,
        flops=4 * ROW_LEN * width * cross_width, flag=True,
    )
    keyvals = lax.ppermute(keyvals, "s", [(0, 1)])


    rows_two, queries = run(
        query_kernel,
        [row_low, low_of(ROW_LEN, cross_width)],
        decoder, after_self, norms, cross_whole,
        flops=2 * ROW_LEN * width * cross_width, flag=True,
    )
    mixed_two, part_two = run(
        cross_forward_kernel,
        [low_of(ROW_LEN, cross_width), low_of(ROW_LEN, width)],
        decoder, queries, keyvals, allowed_cross, cross_whole,
        flops=4 * ROW_LEN * width * cross_width, flag=True,
    )
    after_cross, rows_dec, active_dec_own, active_dec_other, grad_dec_own, grad_dec_other, part = run_ffn(
        ffn_both_kernel,
        [row_full, row_low, hidden_low, hidden_low, hidden_low, hidden_low, row_low],
        [row_block, row_block, hidden_block, hidden_block, hidden_block, hidden_block, row_block],
        (decoder, after_self, part_two, swap(part_two, "c"), norms, grad_out),
        [SMEM, row_block, row_block, row_block, norm_block, row_block],
        ffn_flops * 3 // 2,
        (0, 1, 2, 3),
    )
    grad_dec, low_two, sums_two_dec, grad_queries, grad_keyvals, part_two = run(
        cross_backward_kernel,
        [
            full_of(ROW_LEN, width),
            low_of(ROW_LEN, width),
            full_of(8, width),
            low_of(ROW_LEN, cross_width),
            low_of(ROW_LEN, 2 * cross_width),
            low_of(ROW_LEN, width),
        ],
        decoder, grad_out, part, swap(part, "c"), after_cross, norms, queries, keyvals, allowed_cross,
        cross_whole,
        flops=8 * ROW_LEN * width * cross_width, flag=True,
    )
    (part_dec,) = run_ffn(
        ffn_down_kernel,
        [row_low],
        [row_block],
        (decoder, sums_two_dec, active_dec_own, active_dec_other),
        [SMEM, norm_block, hidden_block, hidden_block],
        ffn_flops // 2,
        (2, 3),
    )
    decoded = after_cross + part_dec.astype(FLOAT) + swap(part_dec, "c").astype(FLOAT)
    grad_keyvals = lax.ppermute(grad_keyvals, "s", [(1, 0)])
    got_two = swap(part_two, "c")

    (part,) = run(
        keyval_backward_kernel, [row_low], decoder, grad_keyvals, cross_whole, part_dec,
        flops=4 * ROW_LEN * width * cross_width, flag=True,
    )
    grad_enc, low_enc, sums_one_enc, grad_enc_own, grad_enc_other = run_ffn(
        memory_ffn_backward_kernel,
        [row_full, row_low, full_of(8, width), hidden_low, hidden_low],
        [row_block, row_block, norm_block, hidden_block, hidden_block],
        (decoder, grad_out, part, swap(part, "c"), encoded, norms, hidden_own, hidden_other),
        [SMEM, row_block, row_block, row_block, row_block, norm_block, hidden_block, hidden_block],
        ffn_flops // 2,
        (2, 3),
    )

    early_width = 4 * ff_width + 2 * cross_width
    row_part = pl.BlockSpec((ROW_LEN, width // 4), lambda i: (0, i))
    low_part = pl.BlockSpec((ROW_LEN, width // 8), lambda i: (0, i))
    high_part = pl.BlockSpec((ROW_LEN, width // 8), lambda i: (0, i + 4))
    whole_block = lambda columns: pl.BlockSpec((ROW_LEN, columns), lambda i: (0, 0))
    operands = (
        decoder, rows_enc, rows_dec, low_enc, grad_out, rows_two, rows_two, low_two, low_two, memory, memory,
        grad_enc_own, grad_enc_other, grad_dec_own, grad_dec_other,
        active_enc_own, active_enc_other, active_dec_own, active_dec_other,
        grad_queries, mixed_two, grad_keyvals,
    )
    grad_early, token = pl.pallas_call(
        early_weights_kernel,
        grid=(4,),
        out_shape=[pltpu.HBM((width, early_width), BFLOAT), full_of(8, 128)],
        in_specs=[
            SMEM, *[row_part] * 4, *[low_part, high_part] * 3, *[whole_block(ff_width)] * 8,
            whole_block(cross_width), whole_block(cross_width), whole_block(2 * cross_width),
        ],
        out_specs=[
            pl.BlockSpec(memory_space=pltpu.HBM),
            pl.BlockSpec((8, 128), lambda i: (0, 0)),
        ],
        scratch_shapes=[
            pltpu.VMEM((2, width // 4, early_width), BFLOAT),
            pltpu.SemaphoreType.DMA((2,)),
        ],
        compiler_params=LIMIT,
        cost_estimate=pl.CostEstimate(
            flops=2 * ROW_LEN * width * early_width, bytes_accessed=20 * 1024 * 1024, transcendentals=0
        ),
    )(*operands)
    (part_enc,) = run_ffn(
        ffn_up_kernel,
        [row_low],
        [row_block],
        (decoder, token, grad_enc_own, grad_enc_other),
        [SMEM, pl.BlockSpec((8, 128), lambda i: (0, 0)), hidden_block, hidden_block],
        ffn_flops // 2,
        (0, 1),
        WIDE_LIMIT,
    )
    got_enc = swap(part_enc, "c")
    grad_early = scatter_plane(grad_early)

    grad_self, low_self, low_half, sums_last = run(
        self_gradient_kernel,
        [row_full, row_low, half_low, full_of(8, width)],
        decoder, grad_enc, part_enc, got_enc, grad_dec, part_two, got_two, after_self, norms, flag=True,
        limit=WIDE_LIMIT,
    )
    low_got = swap(low_half, "h")
    low_core = swap(low_got, "c")
    grad_qkv, part = run(
        self_backward_kernel,
        [heads_low, row_low],
        low_self, qkv, allowed_self, attn_own,
        flops=10 * ROW_LEN * width * out_width * 2, limit=WIDE_LIMIT,
    )
    low_partner, grad_qkv_partner, keep, send = run(
        partner_backward_kernel,
        [row_low, heads_low, half_full, half_low],
        decoder, low_got, low_core, qkv_partner, allowed_partner, attn_own,
        flops=10 * ROW_LEN * width * out_width * 2, flag=True, limit=WIDE_LIMIT, scratch=row_scratch,
    )
    (attn_grad,) = run(
        attn_weights_kernel,
        [low_of(width, attn_width)],
        rows_one, rows_partner, grad_qkv, grad_qkv_partner, low_self, low_partner, mixed_one, mixed_partner,
        flops=8 * ROW_LEN * width * out_width, limit=WIDE_LIMIT,
    )
    attn_grad = scatter_ring_plane(attn_grad, ("z", "x"))
    grad_input, sums = run(
        input_backward_kernel,
        [row_full, full_of(8, width)],
        decoder, grad_self, part, swap(part, "c"), *from_partner(keep, send), values, norms,
        sums_last, sums_one_enc, sums_two_dec, flag=True, scratch=row_scratch, limit=WIDE_LIMIT,
    )
    sums = jnp.pad(sums.T, ((0, 0), (0, NORM_COLUMNS - sums.shape[0]))).astype(BFLOAT)
    sums = lax.all_to_all(sums, PLANE, split_axis=0, concat_axis=0, tiled=True)
    sums = jnp.sum(sums.reshape(16, -1, NORM_COLUMNS).astype(FLOAT), axis=0)
    sums = sums + swap(sums, "h")
    decoded, memory, grad_input = together(decoded, memory, grad_input)
    outputs = to_owners(pick(is_decoder, decoded.astype(BFLOAT), memory))
    grad_embedded = to_owners(grad_input)

    send_h, send_s, send_across = run(
        send_home_kernel,
        [
            low_of(2 * rows_cross, 2 * ff_width + half_cross),
            low_of(rows_cross, cross_width),
            low_of(rows_cross, cross_width),
        ],
        decoder, grad_early, flag=True,
    )
    total_up, total_down, total_query, total_keyval, total_cross_out = run(
        bring_home_kernel,
        [
            full_of(1, 2 * rows_cross, ff_width),
            full_of(1, 2 * rows_cross, ff_width),
            full_of(rows_cross, half_cross),
            full_of(rows_cross, cross_width),
            full_of(rows_cross, half_cross),
        ],
        decoder, grad_early, swap(send_h, "h"), swap(send_s, "s"), swap_across(send_across), flag=True,
    )
    total_qkv, total_out, total_gain, total_offset = run(
        attn_home_kernel,
        [
            full_of(1, 2 * rows_cross, qkv_width),
            full_of(1, 2 * rows_cross, out_width),
            full_of(1, 3, 2 * rows_cross),
            full_of(1, 3, 2 * rows_cross),
        ],
        attn_grad, sums,
    )
    return (
        outputs[None],
        grad_embedded[None],
        total_qkv,
        total_out.swapaxes(1, 2),
        total_up,
        total_down.swapaxes(1, 2),
        total_gain,
        total_offset,
        total_query,
        total_keyval,
        total_cross_out.T,
    )


def solution(mesh):
    fine = Mesh(mesh.devices.reshape(2, 4, 4, 2, 2), AXES)
    tokens = ("x", "z", "h", "c")
    tensor = ("h", "c")
    whole = ("s", "x", "z")
    return jax.shard_map(
        shards,
        mesh=fine,
        in_specs=(
            P("s", None, tokens, None),
            P("s", None, tokens, None),
            P(None, None, PLANE, None),
            P("s", PLANE, tensor),
            P("s", tensor, PLANE),
            P("s", PLANE, tensor),
            P("s", tensor, PLANE),
            P("s", None, PLANE),
            P("s", None, PLANE),
            P(whole, tensor),
            P(whole, tensor),
            P(tensor, whole),
        ),
        out_specs=(
            P("s", None, tokens, None),
            P("s", None, tokens, None),
            P("s", PLANE, tensor),
            P("s", tensor, PLANE),
            P("s", PLANE, tensor),
            P("s", tensor, PLANE),
            P("s", None, PLANE),
            P("s", None, PLANE),
            P(whole, tensor),
            P(whole, tensor),
            P(tensor, whole),
        ),
        check_vma=False,
    )
```

```python
import functools

import jax
import jax.numpy as jnp
import numpy as np
from jax import lax
from jax.experimental import pallas as pl
from jax.experimental.pallas import tpu as pltpu
from jax.sharding import Mesh
from jax.sharding import PartitionSpec as P

HEAD_DIM = 64
ROW_LEN = 256
QUARTER = 64
NORM_COLUMNS = 128

EPSILON = 1e-05
NEGATIVE = -1000000000.0
SCALING = 0.125
GELU_COEF = 0.7978845608028654
BFLOAT = jnp.bfloat16
FLOAT = jnp.float32
AXES = ("s", "x", "z", "h", "c")
PLANE = ("x", "z")
ORDER = np.concatenate([np.arange(QUARTER) + QUARTER * q for q in (0, 2, 1, 3)]).astype(np.int32)


def swap(block, axis):
    return lax.ppermute(block, axis, [(0, 1), (1, 0)])


def shift(block, axis, distance):
    size = lax.axis_size(axis)
    return lax.ppermute(block, axis, [(i, (i + distance) % size) for i in range(size)])


def place(buffer, block, index, dim):
    return lax.dynamic_update_slice_in_dim(buffer, jnp.expand_dims(block, dim), index, dim)


def take(buffer, index, dim):
    return lax.dynamic_index_in_dim(buffer, index, dim, keepdims=False)


def gather_direct(block, axis):
    here = lax.axis_index(axis)
    blocks = [block, shift(block, axis, -1), shift(block, axis, 2), shift(block, axis, 1)]
    return [((here + k) % 4, block) for k, block in enumerate(blocks)]


def gather_ring(block, axis):
    here = lax.axis_index(axis)
    half = block.shape[0] // 2
    before, after = shift(block, axis, 1), shift(block, axis, -1)
    far = jnp.concatenate([shift(before[:half], axis, 1), shift(after[half:], axis, -1)])
    return [((here + k) % 4, block) for k, block in enumerate([block, after, far, before])]


def gather_ring_plane(block, axes):
    near, far = axes
    rows, columns = block.shape
    first = jnp.zeros((4, rows, columns), block.dtype)
    for index, piece in gather_direct(block, near):
        first = place(first, piece, index, 0)
    whole = jnp.zeros((4, 4, rows, columns), block.dtype)
    dim = PLANE.index(far)
    for index, piece in gather_ring(first, far):
        whole = place(whole, piece, index, dim)
    return whole.reshape(-1, columns)


def together(*arrays):
    return lax.optimization_barrier(arrays)


def scatter_direct(blocks, axis):
    here = lax.axis_index(axis)
    parts = [take(blocks, (here + k) % 4, 0) for k in range(4)]
    total = parts[0].astype(FLOAT)
    for distance in (1, 2, -1):
        total = total + shift(parts[distance % 4].astype(BFLOAT), axis, distance).astype(FLOAT)
    return total


def scatter_ring(blocks, axis, dim):
    here = lax.axis_index(axis)
    own, after, far, before = [take(blocks, (here + k) % 4, dim) for k in range(4)]
    half = own.shape[0] // 2
    far = far.astype(BFLOAT)
    top = shift(far[:half], axis, 1).astype(FLOAT)
    bottom = shift(far[half:], axis, -1).astype(FLOAT)
    after = jnp.concatenate([after[:half].astype(FLOAT) + top, after[half:].astype(FLOAT)])
    before = jnp.concatenate([before[:half].astype(FLOAT), before[half:].astype(FLOAT) + bottom])
    from_before = shift(after.astype(BFLOAT), axis, 1).astype(FLOAT)
    from_after = shift(before.astype(BFLOAT), axis, -1).astype(FLOAT)
    return own.astype(FLOAT) + from_before + from_after


def scatter_ring_plane(block, axes):
    near, far = axes
    rows = block.shape[0] // 16
    blocks = block.reshape(4, 4, rows, -1)
    return scatter_direct(scatter_ring(blocks, far, PLANE.index(far)), near)


def swap_across(block):
    return lax.ppermute(block, ("s", "h"), [(0, 3), (3, 0), (1, 2), (2, 1)])


def gelu_tanh(values):
    return (
        0.5 * values * (1.0 + jnp.tanh(GELU_COEF * (values + 0.044715 * values * values * values)))
    )


def gelu_slope(values):
    squares = values * values
    curve = jnp.tanh(GELU_COEF * (values + 0.044715 * values * squares))
    return 0.5 * (1.0 + curve) + 0.5 * values * (1.0 - curve * curve) * (
        GELU_COEF * (1.0 + 3.0 * 0.044715 * squares)
    )


def segment_ids(lengths_row):
    ends = jnp.cumsum(lengths_row)
    positions = jnp.asarray(ORDER)
    return jnp.sum((positions[:, None] >= ends[None, :]).astype(jnp.int32), axis=1)


def dot(left, right):
    return jnp.dot(left, right, preferred_element_type=FLOAT)


def dot_left(left, right):
    return lax.dot_general(left, right, (((0,), (0,)), ((), ())), preferred_element_type=FLOAT)


def dot_right(left, right):
    return lax.dot_general(left, right, (((1,), (1,)), ((), ())), preferred_element_type=FLOAT)


def normalize(stream):
    centred = stream - jnp.mean(stream, axis=-1, keepdims=True)
    inverse = lax.rsqrt(jnp.mean(centred * centred, axis=-1, keepdims=True) + EPSILON)
    return centred * inverse, inverse


def layer_norm(stream, norms, index):
    unit, _ = normalize(stream)
    return (unit * norms[index : index + 1] + norms[index + 3 : index + 4]).astype(BFLOAT)


def norm_backward(grad_out, stream, gain):
    unit, inverse = normalize(stream)
    scaled = grad_out * gain
    inner = (
        scaled
        - jnp.mean(scaled, axis=-1, keepdims=True)
        - unit * jnp.mean(scaled * unit, axis=-1, keepdims=True)
    )
    sums = jnp.concatenate(
        [
            jnp.sum(grad_out * unit, axis=0, keepdims=True),
            jnp.sum(grad_out, axis=0, keepdims=True),
            jnp.zeros((6, grad_out.shape[1]), FLOAT),
        ]
    )
    return inverse * inner, sums


def add_parts(own_ref, other_ref):
    return own_ref[...].astype(FLOAT) + other_ref[...].astype(FLOAT)


def softmax(query, key, mask):
    scores = jnp.where(mask, dot_right(query, key) * SCALING, NEGATIVE)
    expo_scores = jnp.exp(scores - jnp.max(scores, axis=-1, keepdims=True))
    return expo_scores / jnp.sum(expo_scores, axis=-1, keepdims=True)


def head_backward(query, key, value, mask, grad_mixed):
    weights = softmax(query, key, mask)
    grad_value = dot_left(weights.astype(BFLOAT), grad_mixed)
    grad_weights = dot_right(grad_mixed, value)
    grad_scores = weights * (
        grad_weights - jnp.sum(weights * grad_weights, axis=-1, keepdims=True)
    )
    grad_scores = grad_scores.astype(BFLOAT)
    grad_query = dot(grad_scores, key) * SCALING
    grad_key = dot_left(grad_scores, query) * SCALING
    return grad_query.astype(BFLOAT), grad_key.astype(BFLOAT), grad_value.astype(BFLOAT)


def head(ref, place):
    return ref[:, place * HEAD_DIM : (place + 1) * HEAD_DIM]


def put_halves(place, whole, mine, others):
    length = mine.shape[0]
    whole[pl.ds(pl.multiple_of(place[1] * length, length), length), :] = mine[...].astype(whole.dtype)
    whole[pl.ds(pl.multiple_of((1 - place[1]) * length, length), length), :] = others[...].astype(
        whole.dtype
    )


def take_halves(place, whole, keep, send):
    length = keep.shape[0]
    keep[...] = whole[pl.ds(pl.multiple_of(place[1] * length, length), length), :]
    send[...] = whole[pl.ds(pl.multiple_of((1 - place[1]) * length, length), length), :].astype(BFLOAT)


def self_forward_kernel(
    place, stream, partner, norms, weights, mask, mask_partner,
    rows, rows_partner, qkv, qkv_partner, mixed, mixed_partner, part, keep, send, total,
):
    quarter = mixed.shape[1]
    width = 3 * quarter
    rows[...] = layer_norm(stream[...], norms, 0)
    rows_partner[...] = layer_norm(partner[...].astype(FLOAT), norms, 0)
    for row, heads, mixes, allow in (
        (rows, qkv, mixed, mask), (rows_partner, qkv_partner, mixed_partner, mask_partner)
    ):
        allowed = allow[...] > 0.5
        heads[...] = dot(row[...], weights[:, :width]).astype(BFLOAT)
        for i in range(quarter // HEAD_DIM):
            weight = softmax(head(heads, 3 * i), head(heads, 3 * i + 1), allowed)
            out = dot(weight.astype(BFLOAT), head(heads, 3 * i + 2))
            mixes[:, i * HEAD_DIM : (i + 1) * HEAD_DIM] = out.astype(BFLOAT)
    part[...] = dot_right(mixed[...], weights[:, width : width + quarter]).astype(BFLOAT)
    total[...] = dot_right(mixed_partner[...], weights[:, width : width + quarter])
    take_halves(place, total, keep, send)


def combine_kernel(place, stream, own, other, got, got_core, after):
    put_halves(place, after, got, got_core)
    after[...] += stream[...] + add_parts(own, other)


def ffn_forward_kernel(
    decoder, stream, norms, up_own, up_other, down_own, down_other,
    rows, hidden_own, hidden_other, active_own, active_other, part,
):
    rows[...] = layer_norm(stream[...], norms, 2)

    @pl.when(decoder[0] == 0)
    def _():
        term = None
        for up, down, hidden, active in (
            (up_own, down_own, hidden_own, active_own),
            (up_other, down_other, hidden_other, active_other),
        ):
            raised = dot(rows[...], up[...])
            hidden[...] = raised
            active[...] = gelu_tanh(raised).astype(BFLOAT)
            piece = dot_right(active[...], down[...])
            term = piece if term is None else term + piece
        part[...] = term.astype(BFLOAT)


def ffn_both_kernel(
    decoder, stream, own, other, norms, cotangent, up_own, up_other, down_own, down_other,
    after, rows, active_own, active_other, grad_own, grad_other, part,
):
    @pl.when(decoder[0] == 1)
    def _():
        after[...] = stream[...] + add_parts(own, other)
        rows[...] = layer_norm(after[...], norms, 2)
        term = None
        for up, down, active, grad in (
            (up_own, down_own, active_own, grad_own),
            (up_other, down_other, active_other, grad_other),
        ):
            raised = dot(rows[...], up[...])
            active[...] = gelu_tanh(raised).astype(BFLOAT)
            grad[...] = (dot(cotangent[...], down[...]) * gelu_slope(raised)).astype(BFLOAT)
            piece = dot_right(grad[...], up[...])
            term = piece if term is None else term + piece
        part[...] = term.astype(BFLOAT)


def ffn_down_kernel(decoder, after_this, active_own, active_other, down_own, down_other, part):
    @pl.when(decoder[0] == 1)
    def _():
        term = dot_right(active_own[...], down_own[...]) + dot_right(active_other[...], down_other[...])
        part[...] = term.astype(BFLOAT)


def sort_rows(gathered, ordered, columns):
    depth = ordered.shape[0]
    piece = depth // 32
    first, to = columns
    wide = to.stop - to.start
    for i in range(16):
        for j in range(2):
            start = j * depth // 2 + i * piece
            ordered[start : start + piece, to] = gathered[
                (2 * i + j) * piece : (2 * i + j + 1) * piece, first : first + wide
            ]


def memory_kernel(
    decoder, stream, own, other, norms, late, encoded, memory, keyvals, weights
):
    wide = weights.shape[1] // 2
    half = wide // 2
    base = late.shape[1] - 2 * wide

    @pl.when(decoder[0] == 1)
    def _():
        for side in range(2):
            for part in range(2):
                start = part * wide + side * half
                sort_rows(late, weights, (base + side * wide + part * half, slice(start, start + half)))

    @pl.when(decoder[0] == 0)
    def _():
        sort_rows(late, weights, (base, slice(0, 2 * wide)))
        encoded[...] = stream[...] + add_parts(own, other)
        memory[...] = layer_norm(encoded[...], norms, 1)
        keyvals[...] = dot(memory[...], weights[...]).astype(BFLOAT)


def query_kernel(decoder, stream, norms, weights, rows, queries):
    @pl.when(decoder[0] == 1)
    def _():
        rows[...] = layer_norm(stream[...], norms, 1)
        queries[...] = dot(rows[...], weights[:, : queries.shape[1]]).astype(BFLOAT)


def cross_forward_kernel(decoder, queries, keyvals, mask, weights, mixed, part):
    @pl.when(decoder[0] == 1)
    def _():
        allowed = mask[...] > 0.5
        for i in range(queries.shape[1] // HEAD_DIM):
            weight = softmax(head(queries, i), head(keyvals, 2 * i), allowed)
            out = dot(weight.astype(BFLOAT), head(keyvals, 2 * i + 1))
            mixed[:, i * HEAD_DIM : (i + 1) * HEAD_DIM] = out.astype(BFLOAT)
        part[...] = dot_right(mixed[...], weights[:, queries.shape[1] :]).astype(BFLOAT)


def memory_ffn_backward_kernel(
    decoder, cotangent, own, other, stream, norms, hidden_own, hidden_other, down_own, down_other,
    grad, low, sums, grad_own, grad_other,
):
    @pl.when(decoder[0] == 0)
    def _():
        into, totals = norm_backward(
            cotangent[...].astype(FLOAT) + add_parts(own, other), stream[...], norms[1:2]
        )
        grad[...] = into
        low[...] = into.astype(BFLOAT)
        sums[...] = totals
        for down, hidden, out in ((down_own, hidden_own, grad_own), (down_other, hidden_other, grad_other)):
            out[...] = (dot(low[...], down[...]) * gelu_slope(hidden[...])).astype(BFLOAT)


def ffn_up_kernel(decoder, after_this, grad_own, grad_other, up_own, up_other, part):
    @pl.when(decoder[0] == 0)
    def _():
        term = dot_right(grad_own[...], up_own[...]) + dot_right(grad_other[...], up_other[...])
        part[...] = term.astype(BFLOAT)


def cross_backward_kernel(
    decoder, cotangent, own, other, stream, norms, queries, keyvals, mask, weights,
    grad, low, sums, grad_queries, grad_keyvals, part,
):
    @pl.when(decoder[0] == 1)
    def _():
        allowed = mask[...] > 0.5
        into, totals = norm_backward(add_parts(own, other), stream[...], norms[2:3])
        grad[...] = cotangent[...].astype(FLOAT) + into
        low[...] = grad[...].astype(BFLOAT)
        sums[...] = totals
        grad_mixed = dot(low[...], weights[:, queries.shape[1] :]).astype(BFLOAT)
        for i in range(queries.shape[1] // HEAD_DIM):
            one, two, three = head_backward(
                head(queries, i),
                head(keyvals, 2 * i),
                head(keyvals, 2 * i + 1),
                allowed,
                grad_mixed[:, i * HEAD_DIM : (i + 1) * HEAD_DIM],
            )
            grad_queries[:, i * HEAD_DIM : (i + 1) * HEAD_DIM] = one
            grad_keyvals[:, 2 * i * HEAD_DIM : (2 * i + 1) * HEAD_DIM] = two
            grad_keyvals[:, (2 * i + 1) * HEAD_DIM : (2 * i + 2) * HEAD_DIM] = three
        part[...] = dot_right(grad_queries[...], weights[:, : queries.shape[1]]).astype(BFLOAT)


def keyval_backward_kernel(decoder, grad_keyvals, weights, after_this, part):
    @pl.when(decoder[0] == 0)
    def _():
        part[...] = dot_right(grad_keyvals[...], weights[...]).astype(BFLOAT)


def self_gradient_kernel(
    place, grad_enc, own_enc, other_enc, grad_dec, own_dec, other_dec, stream, norms, grad, low, low_half, sums
):
    @pl.when(place[0] == 1)
    def _():
        into, totals = norm_backward(add_parts(own_dec, other_dec), stream[...], norms[1:2])
        grad[...] = grad_dec[...] + into
        sums[...] = totals

    @pl.when(place[0] == 0)
    def _():
        into, totals = norm_backward(add_parts(own_enc, other_enc), stream[...], norms[2:3])
        grad[...] = grad_enc[...] + into
        sums[...] = totals

    low[...] = grad[...].astype(BFLOAT)
    half = low_half.shape[0]
    low_half[...] = low[pl.ds(pl.multiple_of(place[1] * half, half), half), :]


def row_backward(low, qkv, mask, weights, grad_qkv):
    allowed = mask[...] > 0.5
    quarter = qkv.shape[1] // 3
    width = 3 * quarter
    grad_mixed = dot(low[...], weights[:, width : width + quarter]).astype(BFLOAT)
    for i in range(quarter // HEAD_DIM):
        grads = head_backward(
            head(qkv, 3 * i),
            head(qkv, 3 * i + 1),
            head(qkv, 3 * i + 2),
            allowed,
            grad_mixed[:, i * HEAD_DIM : (i + 1) * HEAD_DIM],
        )
        for k in range(3):
            grad_qkv[:, (3 * i + k) * HEAD_DIM : (3 * i + k + 1) * HEAD_DIM] = grads[k]
    return dot_right(grad_qkv[...], weights[:, :width])


def self_backward_kernel(low, qkv, mask, weights, grad_qkv, part):
    part[...] = row_backward(low, qkv, mask, weights, grad_qkv).astype(BFLOAT)


def partner_backward_kernel(
    place, low_got, low_core, qkv, mask, weights, low, grad_qkv, keep, send, total
):
    put_halves(place, low, low_got, low_core)
    total[...] = row_backward(low, qkv, mask, weights, grad_qkv)
    take_halves(place, total, keep, send)


def input_backward_kernel(
    place, grad, own, other, got, got_core, stream, norms, last, one_enc, two_dec, grad_input, sums, total
):
    put_halves(place, total, got, got_core)
    into, zero = norm_backward(total[...] + add_parts(own, other), stream[...], norms[0:1])
    grad_input[...] = grad[...] + into
    is_decoder = place[0] == 1
    one = jnp.where(is_decoder, last[...], one_enc[...])
    two = jnp.where(is_decoder, two_dec[...], last[...])
    sums[...] = jnp.concatenate(
        [zero[0:1], one[0:1], two[0:1], zero[1:2], one[1:2], two[1:2], jnp.zeros((2, zero.shape[1]), FLOAT)]
    )


def early_weights_kernel(
    decoder, rows_enc, rows_dec, low_enc, low_dec, rows_two_low, rows_two_high, low_two_low, low_two_high,
    memory_low, memory_high, hidden_enc_own, hidden_enc_other, hidden_dec_own, hidden_dec_other,
    active_enc_own, active_enc_other, active_dec_own, active_dec_other, queries, mixed, keyvals, whole, token, slots, sems,
):
    token[...] = jnp.zeros_like(token)
    step = pl.program_id(0)
    slot = lax.rem(step, 2)
    out = slots.at[slot]
    rows = slots.shape[1]

    def copy_of(step, slot):
        start = pl.multiple_of(step * rows, rows)
        return pltpu.make_async_copy(slots.at[slot], whole.at[pl.ds(start, rows), :], sems.at[slot])

    @pl.when(step >= 2)
    def _():
        copy_of(step - 2, slot).wait()

    hidden = hidden_enc_own.shape[1]
    half = queries.shape[1]
    piece = rows_two_low.shape[1] // 4

    def put(start, value):
        out[:, start : start + value.shape[1]] = value.astype(BFLOAT)

    def put_cross(start, low, high):
        for i in range(4):
            for j, value in enumerate((low, high)):
                out[
                    (2 * i + j) * piece : (2 * i + j + 1) * piece, start : start + value.shape[1]
                ] = value[i * piece : (i + 1) * piece].astype(BFLOAT)

    @pl.when(decoder[0] == 1)
    def _():
        put(0, dot_left(rows_dec[...], hidden_dec_own[...]))
        put(hidden, dot_left(rows_dec[...], hidden_dec_other[...]))
        put(2 * hidden, dot_left(low_dec[...], active_dec_own[...]))
        put(3 * hidden, dot_left(low_dec[...], active_dec_other[...]))
        put_cross(4 * hidden, dot_left(rows_two_low[...], queries[...]), dot_left(rows_two_high[...], queries[...]))
        put_cross(4 * hidden + half, dot_left(low_two_low[...], mixed[...]), dot_left(low_two_high[...], mixed[...]))

    @pl.when(decoder[0] == 0)
    def _():
        put(0, dot_left(rows_enc[...], hidden_enc_own[...]))
        put(hidden, dot_left(rows_enc[...], hidden_enc_other[...]))
        put(2 * hidden, dot_left(low_enc[...], active_enc_own[...]))
        put(3 * hidden, dot_left(low_enc[...], active_enc_other[...]))
        put_cross(4 * hidden, dot_left(memory_low[...], keyvals[...]), dot_left(memory_high[...], keyvals[...]))

    copy_of(step, slot).start()

    @pl.when(step == pl.num_programs(0) - 1)
    def _():
        copy_of(step - 1, 1 - slot).wait()
        copy_of(step, slot).wait()


def attn_weights_kernel(
    rows, rows_partner, grad_qkv, grad_qkv_partner, low, low_partner, mixed, mixed_partner, out
):
    width = grad_qkv.shape[1]
    out[:, :width] = (
        dot_left(rows[...], grad_qkv[...]) + dot_left(rows_partner[...], grad_qkv_partner[...])
    ).astype(BFLOAT)
    out[:, width:] = (
        dot_left(low[...], mixed[...]) + dot_left(low_partner[...], mixed_partner[...])
    ).astype(BFLOAT)


def gather_plane(block):
    return lax.all_gather(block, PLANE, axis=0, tiled=True)


def scatter_plane(block):
    return lax.psum_scatter(block, PLANE, scatter_dimension=0, tiled=True)


def send_home_kernel(decoder, early, send_h, send_s, send_across):
    rows = send_s.shape[0]
    wide = send_s.shape[1]
    hidden = (early.shape[1] - 2 * wide) // 4
    half = wide // 2
    send_h[:, :hidden] = early[:, hidden : 2 * hidden]
    send_h[:, hidden : 2 * hidden] = early[:, 3 * hidden : 4 * hidden]
    start = 4 * hidden

    @pl.when(decoder[0] == 1)
    def _():
        send_h[:rows, 2 * hidden :] = early[rows:, start + half : start + 2 * half]
        send_h[rows:, 2 * hidden :] = early[rows:, start + 3 * half : start + 4 * half]
        send_s[:, :half] = early[:rows, start : start + half]
        send_s[:, half:] = early[:rows, start + 2 * half : start + 3 * half]
        send_across[:, :half] = early[:rows, start + half : start + 2 * half]
        send_across[:, half:] = early[:rows, start + 3 * half : start + 4 * half]

    @pl.when(decoder[0] == 0)
    def _():
        send_h[:rows, 2 * hidden :] = early[:rows, start + 2 * half : start + 3 * half]
        send_h[rows:, 2 * hidden :] = early[:rows, start + 3 * half : start + 4 * half]
        send_s[...] = early[rows:, start : start + 2 * half]
        send_across[...] = early[rows:, start + 2 * half :]


def bring_home_kernel(decoder, early, got_h, got_s, got_across, up, down, query, keyval, out):
    rows = got_s.shape[0]
    wide = got_s.shape[1]
    hidden = (early.shape[1] - 2 * wide) // 4
    half = wide // 2
    start = 4 * hidden
    up[0] = early[:, :hidden].astype(FLOAT) + got_h[:, :hidden].astype(FLOAT)
    down[0] = early[:, 2 * hidden : 3 * hidden].astype(FLOAT) + got_h[:, hidden : 2 * hidden].astype(FLOAT)
    far = got_s[...].astype(FLOAT) + got_across[...].astype(FLOAT)
    near_left = got_h[:rows, 2 * hidden :].astype(FLOAT)
    near_right = got_h[rows:, 2 * hidden :].astype(FLOAT)

    @pl.when(decoder[0] == 1)
    def _():
        query[...] = early[rows:, start : start + half].astype(FLOAT) + near_left
        out[...] = early[rows:, start + 2 * half : start + 3 * half].astype(FLOAT) + near_right
        keyval[...] = far

    @pl.when(decoder[0] == 0)
    def _():
        keyval[:, :half] = early[:rows, start : start + half].astype(FLOAT) + near_left
        keyval[:, half:] = early[:rows, start + half : start + 2 * half].astype(FLOAT) + near_right
        query[...] = far[:, :half]
        out[...] = far[:, half:]


def attn_home_kernel(own, norms, qkv, out, gain, offset):
    width = qkv.shape[2]
    qkv[0] = own[:, :width]
    out[0] = own[:, width:]
    sums = norms[...].T
    gain[0] = sums[:3]
    offset[0] = sums[3:6]


VMEM = pl.BlockSpec(memory_space=pltpu.VMEM)
SMEM = pl.BlockSpec(memory_space=pltpu.SMEM)
LIMIT = pltpu.CompilerParams(vmem_limit_bytes=28 * 1024 * 1024)
WIDE_LIMIT = pltpu.CompilerParams(vmem_limit_bytes=56 * 1024 * 1024)


def low_of(*dims):
    return jax.ShapeDtypeStruct(dims, BFLOAT)


def full_of(*dims):
    return jax.ShapeDtypeStruct(dims, FLOAT)


def run(kernel, outs, *operands, flops=0, scratch=(), flag=False, specs=None, limit=LIMIT):
    specs = specs or {}
    whole = lambda o: pl.BlockSpec(o.shape, lambda i: (0,) * len(o.shape)) if specs else VMEM
    in_specs = [specs.get(i, whole(o)) for i, o in enumerate(operands)]
    if flag:
        in_specs[0] = SMEM
    moved = sum(o.size * o.dtype.itemsize for o in (*operands, *outs))
    return pl.pallas_call(
        kernel,
        grid=(1,) if specs else (),
        out_shape=list(outs),
        in_specs=in_specs,
        out_specs=[whole(o) for o in outs],
        scratch_shapes=list(scratch),
        compiler_params=limit,
        cost_estimate=pl.CostEstimate(flops=flops, bytes_accessed=moved, transcendentals=0),
    )(*operands)


def shards(
    embedded,
    cotangent,
    lengths,
    attn_qkv,
    attn_out,
    ffn_up,
    ffn_down,
    norm_gain,
    norm_bias,
    cross_query,
    cross_kv,
    cross_out,
):
    is_decoder = lax.axis_index("s") == 1
    first_half = lax.axis_index("h") == 0
    core = lax.axis_index("c")

    def pick(flag, yes, no):
        return jnp.where(flag, yes, no)

    def own_rows(pairs):
        mine = [pick(first_half, pair[0], pair[1]) for pair in pairs]
        got = swap(jnp.concatenate([pick(first_half, pair[1], pair[0]) for pair in pairs], axis=1), "h")
        mine = jnp.concatenate(mine, axis=1)
        half = jnp.concatenate([pick(first_half, mine, got), pick(first_half, got, mine)])
        got = swap(half, "c")
        whole = jnp.concatenate([pick(core == 0, half, got), pick(core == 0, got, half)])
        return jnp.split(whole, len(pairs), axis=1)

    def to_owners(row):
        half = lax.dynamic_slice_in_dim(row, core * 2 * QUARTER, 2 * QUARTER, 0)
        low, high = half[:QUARTER], half[QUARTER:]
        mine = pick(first_half, low, high)
        got = swap(pick(first_half, high, low), "h")
        return jnp.stack([pick(first_half, mine, got), pick(first_half, got, mine)])

    qkv_width = attn_qkv.shape[2]
    out_width = attn_out.shape[1]
    attn_width = qkv_width + out_width
    ff_width = ffn_up.shape[2]
    cross_width = cross_kv.shape[1]
    half_cross = cross_width // 2
    depth = embedded.shape[-1]

    own_ffn = jnp.concatenate([ffn_up[0], ffn_down[0].T], axis=1)
    query_out = jnp.concatenate([cross_query, cross_out.T], axis=1)
    kept = pick(is_decoder, query_out, cross_kv)
    give = pick(is_decoder, cross_kv, query_out)
    own_ffn, kept, give = together(own_ffn, kept, give)
    other_ffn = swap(own_ffn, "h")
    cross = [
        jnp.concatenate([pick(is_decoder, far, near), pick(is_decoder, near, far)])
        for near, far in ((kept, swap(give, "s")), (swap(kept, "h"), swap_across(give)))
    ]
    late_pack = jnp.concatenate(
        [
            own_ffn[:, :ff_width], other_ffn[:, :ff_width], own_ffn[:, ff_width:], other_ffn[:, ff_width:],
            *cross,
        ],
        axis=1,
    )
    late_pack, attn_qkv, attn_out, norm_gain, norm_bias, embedded, cotangent = together(
        late_pack, attn_qkv, attn_out, norm_gain, norm_bias, embedded, cotangent
    )
    late_whole = gather_plane(late_pack)

    norms = jnp.concatenate([norm_gain[0], norm_bias[0]]).T
    norms = jnp.pad(norms, ((0, 0), (0, NORM_COLUMNS - norms.shape[1])))
    attn_own = gather_ring_plane(
        jnp.concatenate([attn_qkv[0], attn_out[0].T, norms], axis=1), ("z", "x")
    )

    inputs, grads = embedded[0], cotangent[0]
    mine = jnp.concatenate([inputs[0], inputs[1], pick(first_half, grads[0], grads[1])])
    got = swap(jnp.concatenate([inputs[0], inputs[1], pick(first_half, grads[1], grads[0])]), "h")
    mine, got = (block.reshape(3, 1, QUARTER, depth) for block in (mine, got))
    half = jnp.concatenate([pick(first_half, mine, got), pick(first_half, got, mine)], axis=1)
    half = half.reshape(3, 2 * QUARTER, depth)
    got = swap(half, "c")
    whole = jnp.concatenate([pick(core == 0, half, got), pick(core == 0, got, half)], axis=1)
    values = pick(first_half, whole[0], whole[1]).astype(FLOAT)
    partner = pick(first_half, whole[1], whole[0])
    grad_out = whole[2]

    norms = attn_own[:, attn_width : attn_width + 8].T.astype(FLOAT)
    decoder = jnp.stack([lax.axis_index("s"), core]).astype(jnp.int32)

    positions = jnp.asarray(ORDER)
    ordered = (positions[None, :] <= positions[:, None]) | jnp.logical_not(is_decoder)
    masks = []
    for row_lengths in (
        pick(first_half, lengths[:, 0, 0], lengths[:, 1, 0]),
        pick(first_half, lengths[:, 1, 0], lengths[:, 0, 0]),
    ):
        source_pair = segment_ids(row_lengths[0])
        target_pair = segment_ids(row_lengths[1])
        own_pair = pick(is_decoder, target_pair, source_pair)
        masks.append(((own_pair[:, None] == own_pair[None, :]) & ordered).astype(BFLOAT))
        if len(masks) == 1:
            allowed_cross = (target_pair[:, None] == source_pair[None, :]).astype(BFLOAT)
    allowed_self, allowed_partner = masks

    width = values.shape[1]
    steps = 2
    block = ff_width // steps
    row_block = pl.BlockSpec((ROW_LEN, width), lambda i: (0, 0))
    norm_block = pl.BlockSpec((8, width), lambda i: (0, 0))
    weight_blocks = [
        pl.BlockSpec((width, block), functools.partial(lambda start, i: (0, start * steps + i), start))
        for start in range(4)
    ]
    hidden_block = pl.BlockSpec((ROW_LEN, block), lambda i: (0, i))
    ffn_flops = 8 * ROW_LEN * width * ff_width
    hidden_full, hidden_low = full_of(ROW_LEN, ff_width), low_of(ROW_LEN, ff_width)
    row_full, row_low = full_of(ROW_LEN, width), low_of(ROW_LEN, width)
    half_full, half_low = full_of(ROW_LEN // 2, width), low_of(ROW_LEN // 2, width)
    heads_low, mixed_low = low_of(ROW_LEN, qkv_width), low_of(ROW_LEN, out_width)
    row_scratch = [pltpu.VMEM((ROW_LEN, width), FLOAT)]

    def run_ffn(kernel, outs, operands, flops, weights):
        count = len(operands)

        def on_columns(*refs):
            late = refs[count]
            views = [late.at[:, pl.ds(i * ff_width, ff_width)] for i in weights]
            kernel(*refs[:count], *views, *refs[count + 1 :])

        return run(on_columns, outs, *operands, late_whole, flops=flops, flag=True)

    rows_one, rows_partner, qkv, qkv_partner, mixed_one, mixed_partner, part, keep, send = run(
        self_forward_kernel,
        [
            row_low, row_low, heads_low, heads_low, mixed_low, mixed_low, row_low, half_full, half_low,
        ],
        decoder, values, partner, norms, attn_own, allowed_self, allowed_partner,
        flops=10 * ROW_LEN * width * out_width * 2, flag=True, scratch=row_scratch,
    )

    def from_partner(keep, send):
        got = swap((keep + swap(send, "c").astype(FLOAT)).astype(BFLOAT), "h")
        return got, swap(got, "c")

    (after_self,) = run(
        combine_kernel, [row_full],
        decoder, values, part, swap(part, "c"), *from_partner(keep, send), flag=True,
    )

    rows_enc, hidden_own, hidden_other, active_enc_own, active_enc_other, part_enc = run_ffn(
        ffn_forward_kernel,
        [row_low, hidden_full, hidden_full, hidden_low, hidden_low, row_low],
        (decoder, after_self, norms),
        ffn_flops,
        (0, 1, 2, 3),
    )
    encoded, memory, keyvals, cross_whole = run(
        memory_kernel,
        [row_full, row_low, low_of(ROW_LEN, 2 * cross_width), low_of(width, 2 * cross_width)],
        decoder, after_self, part_enc, swap(part_enc, "c"), norms, late_whole,
        flops=4 * ROW_LEN * width * cross_width, flag=True,
    )
    keyvals = lax.ppermute(keyvals, "s", [(0, 1)])


    rows_two, queries = run(
        query_kernel,
        [row_low, low_of(ROW_LEN, cross_width)],
        decoder, after_self, norms, cross_whole,
        flops=2 * ROW_LEN * width * cross_width, flag=True,
    )
    mixed_two, part_two = run(
        cross_forward_kernel,
        [low_of(ROW_LEN, cross_width), low_of(ROW_LEN, width)],
        decoder, queries, keyvals, allowed_cross, cross_whole,
        flops=4 * ROW_LEN * width * cross_width, flag=True,
    )
    after_cross, rows_dec, active_dec_own, active_dec_other, grad_dec_own, grad_dec_other, part = run_ffn(
        ffn_both_kernel,
        [row_full, row_low, hidden_low, hidden_low, hidden_low, hidden_low, row_low],
        (decoder, after_self, part_two, swap(part_two, "c"), norms, grad_out),
        ffn_flops * 3 // 2,
        (0, 1, 2, 3),
    )
    grad_dec, low_two, sums_two_dec, grad_queries, grad_keyvals, part_two = run(
        cross_backward_kernel,
        [
            full_of(ROW_LEN, width),
            low_of(ROW_LEN, width),
            full_of(8, width),
            low_of(ROW_LEN, cross_width),
            low_of(ROW_LEN, 2 * cross_width),
            low_of(ROW_LEN, width),
        ],
        decoder, grad_out, part, swap(part, "c"), after_cross, norms, queries, keyvals, allowed_cross,
        cross_whole,
        flops=8 * ROW_LEN * width * cross_width, flag=True,
    )
    (part_dec,) = run_ffn(
        ffn_down_kernel,
        [row_low],
        (decoder, sums_two_dec, active_dec_own, active_dec_other),
        ffn_flops // 2,
        (2, 3),
    )
    decoded = after_cross + part_dec.astype(FLOAT) + swap(part_dec, "c").astype(FLOAT)
    grad_keyvals = lax.ppermute(grad_keyvals, "s", [(1, 0)])
    got_two = swap(part_two, "c")

    (part,) = run(
        keyval_backward_kernel, [row_low], decoder, grad_keyvals, cross_whole, part_dec,
        flops=4 * ROW_LEN * width * cross_width, flag=True,
    )
    grad_enc, low_enc, sums_one_enc, grad_enc_own, grad_enc_other = run_ffn(
        memory_ffn_backward_kernel,
        [row_full, row_low, full_of(8, width), hidden_low, hidden_low],
        (decoder, grad_out, part, swap(part, "c"), encoded, norms, hidden_own, hidden_other),
        ffn_flops // 2,
        (2, 3),
    )

    early_width = 4 * ff_width + 2 * cross_width
    row_part = pl.BlockSpec((ROW_LEN, width // 4), lambda i: (0, i))
    low_part = pl.BlockSpec((ROW_LEN, width // 8), lambda i: (0, i))
    high_part = pl.BlockSpec((ROW_LEN, width // 8), lambda i: (0, i + 4))
    whole_block = lambda columns: pl.BlockSpec((ROW_LEN, columns), lambda i: (0, 0))
    operands = (
        decoder, rows_enc, rows_dec, low_enc, grad_out, rows_two, rows_two, low_two, low_two, memory, memory,
        grad_enc_own, grad_enc_other, grad_dec_own, grad_dec_other,
        active_enc_own, active_enc_other, active_dec_own, active_dec_other,
        grad_queries, mixed_two, grad_keyvals,
    )
    grad_early, token = pl.pallas_call(
        early_weights_kernel,
        grid=(4,),
        out_shape=[pltpu.HBM((width, early_width), BFLOAT), full_of(8, 128)],
        in_specs=[
            SMEM, *[row_part] * 4, *[low_part, high_part] * 3, *[whole_block(ff_width)] * 8,
            whole_block(cross_width), whole_block(cross_width), whole_block(2 * cross_width),
        ],
        out_specs=[
            pl.BlockSpec(memory_space=pltpu.HBM),
            pl.BlockSpec((8, 128), lambda i: (0, 0)),
        ],
        scratch_shapes=[
            pltpu.VMEM((2, width // 4, early_width), BFLOAT),
            pltpu.SemaphoreType.DMA((2,)),
        ],
        compiler_params=LIMIT,
        cost_estimate=pl.CostEstimate(
            flops=2 * ROW_LEN * width * early_width, bytes_accessed=20 * 1024 * 1024, transcendentals=0
        ),
    )(*operands)
    (part_enc,) = run_ffn(
        ffn_up_kernel,
        [row_low],
        (decoder, token, grad_enc_own, grad_enc_other),
        ffn_flops // 2,
        (0, 1),
    )
    got_enc = swap(part_enc, "c")
    grad_early = scatter_plane(grad_early)

    grad_self, low_self, low_half, sums_last = run(
        self_gradient_kernel,
        [row_full, row_low, half_low, full_of(8, width)],
        decoder, grad_enc, part_enc, got_enc, grad_dec, part_two, got_two, after_self, norms, flag=True,
        limit=WIDE_LIMIT,
    )
    low_got = swap(low_half, "h")
    low_core = swap(low_got, "c")
    grad_qkv, part = run(
        self_backward_kernel,
        [heads_low, row_low],
        low_self, qkv, allowed_self, attn_own,
        flops=10 * ROW_LEN * width * out_width * 2, limit=WIDE_LIMIT,
    )
    part, low_got, low_core = together(part, low_got, low_core)
    low_partner, grad_qkv_partner, keep, send = run(
        partner_backward_kernel,
        [row_low, heads_low, half_full, half_low],
        decoder, low_got, low_core, qkv_partner, allowed_partner, attn_own,
        flops=10 * ROW_LEN * width * out_width * 2, flag=True, limit=WIDE_LIMIT, scratch=row_scratch,
    )
    (attn_grad,) = run(
        attn_weights_kernel,
        [low_of(width, attn_width)],
        rows_one, rows_partner, grad_qkv, grad_qkv_partner, low_self, low_partner, mixed_one, mixed_partner,
        flops=8 * ROW_LEN * width * out_width, limit=WIDE_LIMIT,
    )
    attn_grad = scatter_ring_plane(attn_grad, ("z", "x"))
    grad_input, sums = run(
        input_backward_kernel,
        [row_full, full_of(8, width)],
        decoder, grad_self, part, swap(part, "c"), *from_partner(keep, send), values, norms,
        sums_last, sums_one_enc, sums_two_dec, flag=True, scratch=row_scratch, limit=WIDE_LIMIT,
    )
    sums = jnp.pad(sums.T, ((0, 0), (0, NORM_COLUMNS - sums.shape[0]))).astype(BFLOAT)
    sums = lax.all_to_all(sums, PLANE, split_axis=0, concat_axis=0, tiled=True)
    sums = jnp.sum(sums.reshape(16, -1, NORM_COLUMNS).astype(FLOAT), axis=0)
    sums = sums + swap(sums, "h")
    decoded, memory, grad_input = together(decoded, memory, grad_input)
    outputs = to_owners(pick(is_decoder, decoded.astype(BFLOAT), memory))
    grad_embedded = to_owners(grad_input)

    rows_cross = cross_query.shape[0]
    send_h, send_s, send_across = run(
        send_home_kernel,
        [
            low_of(2 * rows_cross, 2 * ff_width + half_cross),
            low_of(rows_cross, cross_width),
            low_of(rows_cross, cross_width),
        ],
        decoder, grad_early, flag=True,
    )
    total_up, total_down, total_query, total_keyval, total_cross_out = run(
        bring_home_kernel,
        [
            full_of(1, 2 * rows_cross, ff_width),
            full_of(1, 2 * rows_cross, ff_width),
            full_of(rows_cross, half_cross),
            full_of(rows_cross, cross_width),
            full_of(rows_cross, half_cross),
        ],
        decoder, grad_early, swap(send_h, "h"), swap(send_s, "s"), swap_across(send_across), flag=True,
    )
    total_qkv, total_out, total_gain, total_offset = run(
        attn_home_kernel,
        [
            full_of(1, 2 * rows_cross, qkv_width),
            full_of(1, 2 * rows_cross, out_width),
            full_of(1, 3, 2 * rows_cross),
            full_of(1, 3, 2 * rows_cross),
        ],
        attn_grad, sums,
    )
    return (
        outputs[None],
        grad_embedded[None],
        total_qkv,
        total_out.swapaxes(1, 2),
        total_up,
        total_down.swapaxes(1, 2),
        total_gain,
        total_offset,
        total_query,
        total_keyval,
        total_cross_out.T,
    )


def solution(mesh):
    fine = Mesh(mesh.devices.reshape(2, 4, 4, 2, 2), AXES)
    tokens = ("x", "z", "h", "c")
    tensor = ("h", "c")
    whole = ("s", "x", "z")
    return jax.shard_map(
        shards,
        mesh=fine,
        in_specs=(
            P("s", None, tokens, None),
            P("s", None, tokens, None),
            P(None, None, PLANE, None),
            P("s", PLANE, tensor),
            P("s", tensor, PLANE),
            P("s", PLANE, tensor),
            P("s", tensor, PLANE),
            P("s", None, PLANE),
            P("s", None, PLANE),
            P(whole, tensor),
            P(whole, tensor),
            P(tensor, whole),
        ),
        out_specs=(
            P("s", None, tokens, None),
            P("s", None, tokens, None),
            P("s", PLANE, tensor),
            P("s", tensor, PLANE),
            P("s", PLANE, tensor),
            P("s", tensor, PLANE),
            P("s", None, PLANE),
            P("s", None, PLANE),
            P(whole, tensor),
            P(whole, tensor),
            P(tensor, whole),
        ),
        check_vma=False,
    )
```

```python
import functools

import jax
import jax.numpy as jnp
import numpy as np
from jax import lax
from jax.experimental import pallas as pl
from jax.experimental.pallas import tpu as pltpu
from jax.sharding import Mesh
from jax.sharding import PartitionSpec as P

HEAD_DIM = 64
ROW_LEN = 256
QUARTER = 64
NORM_COLUMNS = 128

EPSILON = 1e-05
NEGATIVE = -1000000000.0
SCALING = 0.125
GELU_COEF = 0.7978845608028654
BFLOAT = jnp.bfloat16
FLOAT = jnp.float32
AXES = ("s", "x", "z", "h", "c")
PLANE = ("x", "z")
ORDER = np.concatenate([np.arange(QUARTER) + QUARTER * q for q in (0, 2, 1, 3)]).astype(np.int32)


def swap(block, axis):
    return lax.ppermute(block, axis, [(0, 1), (1, 0)])


def shift(block, axis, distance):
    size = lax.axis_size(axis)
    return lax.ppermute(block, axis, [(i, (i + distance) % size) for i in range(size)])


def place(buffer, block, index, dim):
    return lax.dynamic_update_slice_in_dim(buffer, jnp.expand_dims(block, dim), index, dim)


def take(buffer, index, dim):
    return lax.dynamic_index_in_dim(buffer, index, dim, keepdims=False)


def gather_direct(block, axis):
    here = lax.axis_index(axis)
    blocks = [block, shift(block, axis, -1), shift(block, axis, 2), shift(block, axis, 1)]
    return [((here + k) % 4, block) for k, block in enumerate(blocks)]


def gather_ring(block, axis):
    here = lax.axis_index(axis)
    half = block.shape[0] // 2
    before, after = shift(block, axis, 1), shift(block, axis, -1)
    far = jnp.concatenate([shift(before[:half], axis, 1), shift(after[half:], axis, -1)])
    return [((here + k) % 4, block) for k, block in enumerate([block, after, far, before])]


def gather_ring_plane(block, axes):
    near, far = axes
    rows, columns = block.shape
    first = jnp.zeros((4, rows, columns), block.dtype)
    for index, piece in gather_direct(block, near):
        first = place(first, piece, index, 0)
    whole = jnp.zeros((4, 4, rows, columns), block.dtype)
    dim = PLANE.index(far)
    for index, piece in gather_ring(first, far):
        whole = place(whole, piece, index, dim)
    return whole.reshape(-1, columns)


def together(*arrays):
    return lax.optimization_barrier(arrays)


def scatter_direct(blocks, axis):
    here = lax.axis_index(axis)
    parts = [take(blocks, (here + k) % 4, 0) for k in range(4)]
    total = parts[0].astype(FLOAT)
    for distance in (1, 2, -1):
        total = total + shift(parts[distance % 4].astype(BFLOAT), axis, distance).astype(FLOAT)
    return total


def scatter_ring(blocks, axis, dim):
    here = lax.axis_index(axis)
    own, after, far, before = [take(blocks, (here + k) % 4, dim) for k in range(4)]
    half = own.shape[0] // 2
    far = far.astype(BFLOAT)
    top = shift(far[:half], axis, 1).astype(FLOAT)
    bottom = shift(far[half:], axis, -1).astype(FLOAT)
    after = jnp.concatenate([after[:half].astype(FLOAT) + top, after[half:].astype(FLOAT)])
    before = jnp.concatenate([before[:half].astype(FLOAT), before[half:].astype(FLOAT) + bottom])
    from_before = shift(after.astype(BFLOAT), axis, 1).astype(FLOAT)
    from_after = shift(before.astype(BFLOAT), axis, -1).astype(FLOAT)
    return own.astype(FLOAT) + from_before + from_after


def scatter_ring_plane(block, axes):
    near, far = axes
    rows = block.shape[0] // 16
    blocks = block.reshape(4, 4, rows, -1)
    return scatter_direct(scatter_ring(blocks, far, PLANE.index(far)), near)


def swap_across(block):
    return lax.ppermute(block, ("s", "h"), [(0, 3), (3, 0), (1, 2), (2, 1)])


def gelu_tanh(values):
    return (
        0.5 * values * (1.0 + jnp.tanh(GELU_COEF * (values + 0.044715 * values * values * values)))
    )


def gelu_slope(values):
    squares = values * values
    curve = jnp.tanh(GELU_COEF * (values + 0.044715 * values * squares))
    return 0.5 * (1.0 + curve) + 0.5 * values * (1.0 - curve * curve) * (
        GELU_COEF * (1.0 + 3.0 * 0.044715 * squares)
    )


def segment_ids(lengths_row):
    ends = jnp.cumsum(lengths_row)
    positions = jnp.asarray(ORDER)
    return jnp.sum((positions[:, None] >= ends[None, :]).astype(jnp.int32), axis=1)


def dot(left, right):
    return jnp.dot(left, right, preferred_element_type=FLOAT)


def dot_left(left, right):
    return lax.dot_general(left, right, (((0,), (0,)), ((), ())), preferred_element_type=FLOAT)


def dot_right(left, right):
    return lax.dot_general(left, right, (((1,), (1,)), ((), ())), preferred_element_type=FLOAT)


def normalize(stream):
    centred = stream - jnp.mean(stream, axis=-1, keepdims=True)
    inverse = lax.rsqrt(jnp.mean(centred * centred, axis=-1, keepdims=True) + EPSILON)
    return centred * inverse, inverse


def layer_norm(stream, norms, index):
    unit, _ = normalize(stream)
    return (unit * norms[index : index + 1] + norms[index + 3 : index + 4]).astype(BFLOAT)


def norm_backward(grad_out, stream, gain):
    unit, inverse = normalize(stream)
    scaled = grad_out * gain
    inner = (
        scaled
        - jnp.mean(scaled, axis=-1, keepdims=True)
        - unit * jnp.mean(scaled * unit, axis=-1, keepdims=True)
    )
    sums = jnp.concatenate(
        [
            jnp.sum(grad_out * unit, axis=0, keepdims=True),
            jnp.sum(grad_out, axis=0, keepdims=True),
            jnp.zeros((6, grad_out.shape[1]), FLOAT),
        ]
    )
    return inverse * inner, sums


def add_parts(own_ref, other_ref):
    return own_ref[...].astype(FLOAT) + other_ref[...].astype(FLOAT)


def softmax(query, key, mask):
    scores = jnp.where(mask, dot_right(query, key) * SCALING, NEGATIVE)
    expo_scores = jnp.exp(scores - jnp.max(scores, axis=-1, keepdims=True))
    return expo_scores / jnp.sum(expo_scores, axis=-1, keepdims=True)


def head_backward(query, key, value, mask, grad_mixed):
    weights = softmax(query, key, mask)
    grad_value = dot_left(weights.astype(BFLOAT), grad_mixed)
    grad_weights = dot_right(grad_mixed, value)
    grad_scores = weights * (
        grad_weights - jnp.sum(weights * grad_weights, axis=-1, keepdims=True)
    )
    grad_scores = grad_scores.astype(BFLOAT)
    grad_query = dot(grad_scores, key) * SCALING
    grad_key = dot_left(grad_scores, query) * SCALING
    return grad_query.astype(BFLOAT), grad_key.astype(BFLOAT), grad_value.astype(BFLOAT)


def head(ref, place):
    return ref[:, place * HEAD_DIM : (place + 1) * HEAD_DIM]


def put_halves(place, whole, mine, others):
    length = mine.shape[0]
    whole[pl.ds(pl.multiple_of(place[1] * length, length), length), :] = mine[...].astype(whole.dtype)
    whole[pl.ds(pl.multiple_of((1 - place[1]) * length, length), length), :] = others[...].astype(
        whole.dtype
    )


def take_halves(place, whole, keep, send):
    length = keep.shape[0]
    keep[...] = whole[pl.ds(pl.multiple_of(place[1] * length, length), length), :]
    send[...] = whole[pl.ds(pl.multiple_of((1 - place[1]) * length, length), length), :].astype(BFLOAT)


def self_forward_kernel(
    place, stream, partner, norms, weights, mask, mask_partner,
    rows, rows_partner, qkv, qkv_partner, mixed, mixed_partner, part, keep, send, total,
):
    quarter = mixed.shape[1]
    width = 3 * quarter
    rows[...] = layer_norm(stream[...], norms, 0)
    rows_partner[...] = layer_norm(partner[...].astype(FLOAT), norms, 0)
    for row, heads, mixes, allow in (
        (rows, qkv, mixed, mask), (rows_partner, qkv_partner, mixed_partner, mask_partner)
    ):
        allowed = allow[...] > 0.5
        heads[...] = dot(row[...], weights[:, :width]).astype(BFLOAT)
        for i in range(quarter // HEAD_DIM):
            weight = softmax(head(heads, 3 * i), head(heads, 3 * i + 1), allowed)
            out = dot(weight.astype(BFLOAT), head(heads, 3 * i + 2))
            mixes[:, i * HEAD_DIM : (i + 1) * HEAD_DIM] = out.astype(BFLOAT)
    part[...] = dot_right(mixed[...], weights[:, width : width + quarter]).astype(BFLOAT)
    total[...] = dot_right(mixed_partner[...], weights[:, width : width + quarter])
    take_halves(place, total, keep, send)


def combine_kernel(place, stream, own, other, got, got_core, after):
    put_halves(place, after, got, got_core)
    after[...] += stream[...] + add_parts(own, other)


def ffn_forward_kernel(
    decoder, stream, norms, up_own, up_other, down_own, down_other,
    rows, hidden_own, hidden_other, active_own, active_other, part,
):
    rows[...] = layer_norm(stream[...], norms, 2)

    @pl.when(decoder[0] == 0)
    def _():
        term = None
        for up, down, hidden, active in (
            (up_own, down_own, hidden_own, active_own),
            (up_other, down_other, hidden_other, active_other),
        ):
            raised = dot(rows[...], up[...])
            hidden[...] = raised
            active[...] = gelu_tanh(raised).astype(BFLOAT)
            piece = dot_right(active[...], down[...])
            term = piece if term is None else term + piece
        part[...] = term.astype(BFLOAT)


def ffn_both_kernel(
    decoder, stream, own, other, norms, cotangent, up_own, up_other, down_own, down_other,
    after, rows, active_own, active_other, grad_own, grad_other, part,
):
    @pl.when(decoder[0] == 1)
    def _():
        after[...] = stream[...] + add_parts(own, other)
        rows[...] = layer_norm(after[...], norms, 2)
        term = None
        for up, down, active, grad in (
            (up_own, down_own, active_own, grad_own),
            (up_other, down_other, active_other, grad_other),
        ):
            raised = dot(rows[...], up[...])
            active[...] = gelu_tanh(raised).astype(BFLOAT)
            grad[...] = (dot(cotangent[...], down[...]) * gelu_slope(raised)).astype(BFLOAT)
            piece = dot_right(grad[...], up[...])
            term = piece if term is None else term + piece
        part[...] = term.astype(BFLOAT)


def ffn_down_kernel(decoder, after_this, active_own, active_other, down_own, down_other, part):
    @pl.when(decoder[0] == 1)
    def _():
        term = dot_right(active_own[...], down_own[...]) + dot_right(active_other[...], down_other[...])
        part[...] = term.astype(BFLOAT)


def sort_rows(gathered, ordered, columns):
    depth = ordered.shape[0]
    piece = depth // 32
    first, to = columns
    wide = to.stop - to.start
    for i in range(16):
        for j in range(2):
            start = j * depth // 2 + i * piece
            ordered[start : start + piece, to] = gathered[
                (2 * i + j) * piece : (2 * i + j + 1) * piece, first : first + wide
            ]


def memory_kernel(
    decoder, stream, own, other, norms, late, encoded, memory, keyvals, weights
):
    wide = weights.shape[1] // 2
    half = wide // 2
    base = late.shape[1] - 2 * wide

    @pl.when(decoder[0] == 1)
    def _():
        for side in range(2):
            for part in range(2):
                start = part * wide + side * half
                sort_rows(late, weights, (base + side * wide + part * half, slice(start, start + half)))

    @pl.when(decoder[0] == 0)
    def _():
        sort_rows(late, weights, (base, slice(0, 2 * wide)))
        encoded[...] = stream[...] + add_parts(own, other)
        memory[...] = layer_norm(encoded[...], norms, 1)
        keyvals[...] = dot(memory[...], weights[...]).astype(BFLOAT)


def query_kernel(decoder, stream, norms, weights, rows, queries):
    @pl.when(decoder[0] == 1)
    def _():
        rows[...] = layer_norm(stream[...], norms, 1)
        queries[...] = dot(rows[...], weights[:, : queries.shape[1]]).astype(BFLOAT)


def cross_forward_kernel(decoder, queries, keyvals, mask, weights, mixed, part):
    @pl.when(decoder[0] == 1)
    def _():
        allowed = mask[...] > 0.5
        for i in range(queries.shape[1] // HEAD_DIM):
            weight = softmax(head(queries, i), head(keyvals, 2 * i), allowed)
            out = dot(weight.astype(BFLOAT), head(keyvals, 2 * i + 1))
            mixed[:, i * HEAD_DIM : (i + 1) * HEAD_DIM] = out.astype(BFLOAT)
        part[...] = dot_right(mixed[...], weights[:, queries.shape[1] :]).astype(BFLOAT)


def memory_ffn_backward_kernel(
    decoder, cotangent, own, other, stream, norms, hidden_own, hidden_other, down_own, down_other,
    grad, low, sums, grad_own, grad_other,
):
    @pl.when(decoder[0] == 0)
    def _():
        into, totals = norm_backward(
            cotangent[...].astype(FLOAT) + add_parts(own, other), stream[...], norms[1:2]
        )
        grad[...] = into
        low[...] = into.astype(BFLOAT)
        sums[...] = totals
        for down, hidden, out in ((down_own, hidden_own, grad_own), (down_other, hidden_other, grad_other)):
            out[...] = (dot(low[...], down[...]) * gelu_slope(hidden[...])).astype(BFLOAT)


def ffn_up_kernel(decoder, after_this, grad_own, grad_other, up_own, up_other, part, total):
    step = pl.program_id(0)

    @pl.when(decoder[0] == 0)
    def _():
        term = dot_right(grad_own[...], up_own[...]) + dot_right(grad_other[...], up_other[...])

        @pl.when(step == 0)
        def _():
            total[...] = term

        @pl.when(step > 0)
        def _():
            part[...] = (total[...] + term).astype(BFLOAT)


def cross_backward_kernel(
    decoder, cotangent, own, other, stream, norms, queries, keyvals, mask, weights,
    grad, low, sums, grad_queries, grad_keyvals, part,
):
    @pl.when(decoder[0] == 1)
    def _():
        allowed = mask[...] > 0.5
        into, totals = norm_backward(add_parts(own, other), stream[...], norms[2:3])
        grad[...] = cotangent[...].astype(FLOAT) + into
        low[...] = grad[...].astype(BFLOAT)
        sums[...] = totals
        grad_mixed = dot(low[...], weights[:, queries.shape[1] :]).astype(BFLOAT)
        for i in range(queries.shape[1] // HEAD_DIM):
            one, two, three = head_backward(
                head(queries, i),
                head(keyvals, 2 * i),
                head(keyvals, 2 * i + 1),
                allowed,
                grad_mixed[:, i * HEAD_DIM : (i + 1) * HEAD_DIM],
            )
            grad_queries[:, i * HEAD_DIM : (i + 1) * HEAD_DIM] = one
            grad_keyvals[:, 2 * i * HEAD_DIM : (2 * i + 1) * HEAD_DIM] = two
            grad_keyvals[:, (2 * i + 1) * HEAD_DIM : (2 * i + 2) * HEAD_DIM] = three
        part[...] = dot_right(grad_queries[...], weights[:, : queries.shape[1]]).astype(BFLOAT)


def keyval_backward_kernel(decoder, grad_keyvals, weights, after_this, part):
    @pl.when(decoder[0] == 0)
    def _():
        part[...] = dot_right(grad_keyvals[...], weights[...]).astype(BFLOAT)


def self_gradient_kernel(
    place, grad_enc, own_enc, other_enc, grad_dec, own_dec, other_dec, stream, norms, grad, low, low_half, sums
):
    @pl.when(place[0] == 1)
    def _():
        into, totals = norm_backward(add_parts(own_dec, other_dec), stream[...], norms[1:2])
        grad[...] = grad_dec[...] + into
        sums[...] = totals

    @pl.when(place[0] == 0)
    def _():
        into, totals = norm_backward(add_parts(own_enc, other_enc), stream[...], norms[2:3])
        grad[...] = grad_enc[...] + into
        sums[...] = totals

    low[...] = grad[...].astype(BFLOAT)
    half = low_half.shape[0]
    low_half[...] = low[pl.ds(pl.multiple_of(place[1] * half, half), half), :]


def row_backward(low, qkv, mask, weights, grad_qkv):
    allowed = mask[...] > 0.5
    quarter = qkv.shape[1] // 3
    width = 3 * quarter
    grad_mixed = dot(low[...], weights[:, width : width + quarter]).astype(BFLOAT)
    for i in range(quarter // HEAD_DIM):
        grads = head_backward(
            head(qkv, 3 * i),
            head(qkv, 3 * i + 1),
            head(qkv, 3 * i + 2),
            allowed,
            grad_mixed[:, i * HEAD_DIM : (i + 1) * HEAD_DIM],
        )
        for k in range(3):
            grad_qkv[:, (3 * i + k) * HEAD_DIM : (3 * i + k + 1) * HEAD_DIM] = grads[k]
    return dot_right(grad_qkv[...], weights[:, :width])


def self_backward_kernel(low, qkv, mask, weights, grad_qkv, part):
    part[...] = row_backward(low, qkv, mask, weights, grad_qkv).astype(BFLOAT)


def partner_backward_kernel(
    place, low_got, low_core, qkv, mask, weights, low, grad_qkv, keep, send, total
):
    put_halves(place, low, low_got, low_core)
    total[...] = row_backward(low, qkv, mask, weights, grad_qkv)
    take_halves(place, total, keep, send)


def input_backward_kernel(
    place, grad, own, other, got, got_core, stream, norms, last, one_enc, two_dec, grad_input, sums, total
):
    put_halves(place, total, got, got_core)
    into, zero = norm_backward(total[...] + add_parts(own, other), stream[...], norms[0:1])
    grad_input[...] = grad[...] + into
    is_decoder = place[0] == 1
    one = jnp.where(is_decoder, last[...], one_enc[...])
    two = jnp.where(is_decoder, two_dec[...], last[...])
    sums[...] = jnp.concatenate(
        [zero[0:1], one[0:1], two[0:1], zero[1:2], one[1:2], two[1:2], jnp.zeros((2, zero.shape[1]), FLOAT)]
    )


def early_weights_kernel(
    decoder, rows_enc, rows_dec, low_enc, low_dec, rows_two_low, rows_two_high, low_two_low, low_two_high,
    memory_low, memory_high, hidden_enc_own, hidden_enc_other, hidden_dec_own, hidden_dec_other,
    active_enc_own, active_enc_other, active_dec_own, active_dec_other, queries, mixed, keyvals, whole, token, slots, sems,
):
    token[...] = jnp.zeros_like(token)
    step = pl.program_id(0)
    slot = lax.rem(step, 2)
    out = slots.at[slot]
    rows = slots.shape[1]

    def copy_of(step, slot):
        start = pl.multiple_of(step * rows, rows)
        return pltpu.make_async_copy(slots.at[slot], whole.at[pl.ds(start, rows), :], sems.at[slot])

    @pl.when(step >= 2)
    def _():
        copy_of(step - 2, slot).wait()

    hidden = hidden_enc_own.shape[1]
    half = queries.shape[1]
    piece = rows_two_low.shape[1] // 4

    def put(start, value):
        out[:, start : start + value.shape[1]] = value.astype(BFLOAT)

    def put_cross(start, low, high):
        for i in range(4):
            for j, value in enumerate((low, high)):
                out[
                    (2 * i + j) * piece : (2 * i + j + 1) * piece, start : start + value.shape[1]
                ] = value[i * piece : (i + 1) * piece].astype(BFLOAT)

    @pl.when(decoder[0] == 1)
    def _():
        put(0, dot_left(rows_dec[...], hidden_dec_own[...]))
        put(hidden, dot_left(rows_dec[...], hidden_dec_other[...]))
        put(2 * hidden, dot_left(low_dec[...], active_dec_own[...]))
        put(3 * hidden, dot_left(low_dec[...], active_dec_other[...]))
        put_cross(4 * hidden, dot_left(rows_two_low[...], queries[...]), dot_left(rows_two_high[...], queries[...]))
        put_cross(4 * hidden + half, dot_left(low_two_low[...], mixed[...]), dot_left(low_two_high[...], mixed[...]))

    @pl.when(decoder[0] == 0)
    def _():
        put(0, dot_left(rows_enc[...], hidden_enc_own[...]))
        put(hidden, dot_left(rows_enc[...], hidden_enc_other[...]))
        put(2 * hidden, dot_left(low_enc[...], active_enc_own[...]))
        put(3 * hidden, dot_left(low_enc[...], active_enc_other[...]))
        put_cross(4 * hidden, dot_left(memory_low[...], keyvals[...]), dot_left(memory_high[...], keyvals[...]))

    copy_of(step, slot).start()

    @pl.when(step == pl.num_programs(0) - 1)
    def _():
        copy_of(step - 1, 1 - slot).wait()
        copy_of(step, slot).wait()


def attn_weights_kernel(
    rows, rows_partner, grad_qkv, grad_qkv_partner, low, low_partner, mixed, mixed_partner, out
):
    width = grad_qkv.shape[1]
    out[:, :width] = (
        dot_left(rows[...], grad_qkv[...]) + dot_left(rows_partner[...], grad_qkv_partner[...])
    ).astype(BFLOAT)
    out[:, width:] = (
        dot_left(low[...], mixed[...]) + dot_left(low_partner[...], mixed_partner[...])
    ).astype(BFLOAT)


def gather_plane(block):
    return lax.all_gather(block, PLANE, axis=0, tiled=True)


def scatter_plane(block):
    return lax.psum_scatter(block, PLANE, scatter_dimension=0, tiled=True)


def send_home_kernel(decoder, early, send_h):
    half = send_h.shape[1] // 9
    hidden = 4 * half
    rows = send_h.shape[0] // 2
    send_h[:, :hidden] = early[:, hidden : 2 * hidden]
    send_h[:, hidden : 2 * hidden] = early[:, 3 * hidden : 4 * hidden]
    start = 4 * hidden

    @pl.when(decoder[0] == 1)
    def _():
        send_h[:rows, 2 * hidden :] = early[rows:, start + half : start + 2 * half]
        send_h[rows:, 2 * hidden :] = early[rows:, start + 3 * half : start + 4 * half]

    @pl.when(decoder[0] == 0)
    def _():
        send_h[:rows, 2 * hidden :] = early[:rows, start + 2 * half : start + 3 * half]
        send_h[rows:, 2 * hidden :] = early[:rows, start + 3 * half : start + 4 * half]


def send_section_kernel(decoder, early, after_this, send_s, send_across):
    rows = send_s.shape[0]
    wide = send_s.shape[1]
    half = wide // 2
    start = early.shape[1] - 2 * wide

    @pl.when(decoder[0] == 1)
    def _():
        send_s[:, :half] = early[:rows, start : start + half]
        send_s[:, half:] = early[:rows, start + 2 * half : start + 3 * half]
        send_across[:, :half] = early[:rows, start + half : start + 2 * half]
        send_across[:, half:] = early[:rows, start + 3 * half : start + 4 * half]

    @pl.when(decoder[0] == 0)
    def _():
        send_s[...] = early[rows:, start : start + 2 * half]
        send_across[...] = early[rows:, start + 2 * half :]


def bring_home_kernel(decoder, early, got_h, got_s, got_across, up, down, query, keyval, out):
    rows = got_s.shape[0]
    wide = got_s.shape[1]
    hidden = (early.shape[1] - 2 * wide) // 4
    half = wide // 2
    start = 4 * hidden
    up[0] = early[:, :hidden].astype(FLOAT) + got_h[:, :hidden].astype(FLOAT)
    down[0] = early[:, 2 * hidden : 3 * hidden].astype(FLOAT) + got_h[:, hidden : 2 * hidden].astype(FLOAT)
    far = got_s[...].astype(FLOAT) + got_across[...].astype(FLOAT)
    near_left = got_h[:rows, 2 * hidden :].astype(FLOAT)
    near_right = got_h[rows:, 2 * hidden :].astype(FLOAT)

    @pl.when(decoder[0] == 1)
    def _():
        query[...] = early[rows:, start : start + half].astype(FLOAT) + near_left
        out[...] = early[rows:, start + 2 * half : start + 3 * half].astype(FLOAT) + near_right
        keyval[...] = far

    @pl.when(decoder[0] == 0)
    def _():
        keyval[:, :half] = early[:rows, start : start + half].astype(FLOAT) + near_left
        keyval[:, half:] = early[:rows, start + half : start + 2 * half].astype(FLOAT) + near_right
        query[...] = far[:, :half]
        out[...] = far[:, half:]


def attn_home_kernel(own, norms, qkv, out, gain, offset):
    width = qkv.shape[2]
    qkv[0] = own[:, :width]
    out[0] = own[:, width:]
    sums = norms[...].T
    gain[0] = sums[:3]
    offset[0] = sums[3:6]


VMEM = pl.BlockSpec(memory_space=pltpu.VMEM)
SMEM = pl.BlockSpec(memory_space=pltpu.SMEM)
LIMIT = pltpu.CompilerParams(vmem_limit_bytes=28 * 1024 * 1024)
WIDE_LIMIT = pltpu.CompilerParams(vmem_limit_bytes=56 * 1024 * 1024)


def low_of(*dims):
    return jax.ShapeDtypeStruct(dims, BFLOAT)


def full_of(*dims):
    return jax.ShapeDtypeStruct(dims, FLOAT)


def run(kernel, outs, *operands, flops=0, scratch=(), flag=False, specs=None, limit=LIMIT):
    specs = specs or {}
    whole = lambda o: pl.BlockSpec(o.shape, lambda i: (0,) * len(o.shape)) if specs else VMEM
    in_specs = [specs.get(i, whole(o)) for i, o in enumerate(operands)]
    if flag:
        in_specs[0] = SMEM
    moved = sum(o.size * o.dtype.itemsize for o in (*operands, *outs))
    return pl.pallas_call(
        kernel,
        grid=(1,) if specs else (),
        out_shape=list(outs),
        in_specs=in_specs,
        out_specs=[whole(o) for o in outs],
        scratch_shapes=list(scratch),
        compiler_params=limit,
        cost_estimate=pl.CostEstimate(flops=flops, bytes_accessed=moved, transcendentals=0),
    )(*operands)


def shards(
    embedded,
    cotangent,
    lengths,
    attn_qkv,
    attn_out,
    ffn_up,
    ffn_down,
    norm_gain,
    norm_bias,
    cross_query,
    cross_kv,
    cross_out,
):
    is_decoder = lax.axis_index("s") == 1
    first_half = lax.axis_index("h") == 0
    core = lax.axis_index("c")

    def pick(flag, yes, no):
        return jnp.where(flag, yes, no)

    def own_rows(pairs):
        mine = [pick(first_half, pair[0], pair[1]) for pair in pairs]
        got = swap(jnp.concatenate([pick(first_half, pair[1], pair[0]) for pair in pairs], axis=1), "h")
        mine = jnp.concatenate(mine, axis=1)
        half = jnp.concatenate([pick(first_half, mine, got), pick(first_half, got, mine)])
        got = swap(half, "c")
        whole = jnp.concatenate([pick(core == 0, half, got), pick(core == 0, got, half)])
        return jnp.split(whole, len(pairs), axis=1)

    def to_owners(row):
        half = lax.dynamic_slice_in_dim(row, core * 2 * QUARTER, 2 * QUARTER, 0)
        low, high = half[:QUARTER], half[QUARTER:]
        mine = pick(first_half, low, high)
        got = swap(pick(first_half, high, low), "h")
        return jnp.stack([pick(first_half, mine, got), pick(first_half, got, mine)])

    qkv_width = attn_qkv.shape[2]
    out_width = attn_out.shape[1]
    attn_width = qkv_width + out_width
    ff_width = ffn_up.shape[2]
    cross_width = cross_kv.shape[1]
    half_cross = cross_width // 2
    depth = embedded.shape[-1]

    own_ffn = jnp.concatenate([ffn_up[0], ffn_down[0].T], axis=1)
    query_out = jnp.concatenate([cross_query, cross_out.T], axis=1)
    kept = pick(is_decoder, query_out, cross_kv)
    give = pick(is_decoder, cross_kv, query_out)
    own_ffn, kept, give = together(own_ffn, kept, give)
    other_ffn = swap(own_ffn, "h")
    cross = [
        jnp.concatenate([pick(is_decoder, far, near), pick(is_decoder, near, far)])
        for near, far in ((kept, swap(give, "s")), (swap(kept, "h"), swap_across(give)))
    ]
    late_pack = jnp.concatenate(
        [
            own_ffn[:, :ff_width], other_ffn[:, :ff_width], own_ffn[:, ff_width:], other_ffn[:, ff_width:],
            *cross,
        ],
        axis=1,
    )
    late_pack, attn_qkv, attn_out, norm_gain, norm_bias, embedded, cotangent = together(
        late_pack, attn_qkv, attn_out, norm_gain, norm_bias, embedded, cotangent
    )
    late_whole = gather_plane(late_pack)

    norms = jnp.concatenate([norm_gain[0], norm_bias[0]]).T
    norms = jnp.pad(norms, ((0, 0), (0, NORM_COLUMNS - norms.shape[1])))
    attn_own = gather_ring_plane(
        jnp.concatenate([attn_qkv[0], attn_out[0].T, norms], axis=1), ("z", "x")
    )

    inputs, grads = embedded[0], cotangent[0]
    mine = jnp.concatenate([inputs[0], inputs[1], pick(first_half, grads[0], grads[1])])
    got = swap(jnp.concatenate([inputs[0], inputs[1], pick(first_half, grads[1], grads[0])]), "h")
    mine, got = (block.reshape(3, 1, QUARTER, depth) for block in (mine, got))
    half = jnp.concatenate([pick(first_half, mine, got), pick(first_half, got, mine)], axis=1)
    half = half.reshape(3, 2 * QUARTER, depth)
    got = swap(half, "c")
    whole = jnp.concatenate([pick(core == 0, half, got), pick(core == 0, got, half)], axis=1)
    values = pick(first_half, whole[0], whole[1]).astype(FLOAT)
    partner = pick(first_half, whole[1], whole[0])
    grad_out = whole[2]

    norms = attn_own[:, attn_width : attn_width + 8].T.astype(FLOAT)
    decoder = jnp.stack([lax.axis_index("s"), core]).astype(jnp.int32)

    positions = jnp.asarray(ORDER)
    ordered = (positions[None, :] <= positions[:, None]) | jnp.logical_not(is_decoder)
    masks = []
    for row_lengths in (
        pick(first_half, lengths[:, 0, 0], lengths[:, 1, 0]),
        pick(first_half, lengths[:, 1, 0], lengths[:, 0, 0]),
    ):
        source_pair = segment_ids(row_lengths[0])
        target_pair = segment_ids(row_lengths[1])
        own_pair = pick(is_decoder, target_pair, source_pair)
        masks.append(((own_pair[:, None] == own_pair[None, :]) & ordered).astype(BFLOAT))
        if len(masks) == 1:
            allowed_cross = (target_pair[:, None] == source_pair[None, :]).astype(BFLOAT)
    allowed_self, allowed_partner = masks

    width = values.shape[1]
    steps = 2
    block = ff_width // steps
    row_block = pl.BlockSpec((ROW_LEN, width), lambda i: (0, 0))
    norm_block = pl.BlockSpec((8, width), lambda i: (0, 0))
    weight_blocks = [
        pl.BlockSpec((width, block), functools.partial(lambda start, i: (0, start * steps + i), start))
        for start in range(4)
    ]
    hidden_block = pl.BlockSpec((ROW_LEN, block), lambda i: (0, i))
    ffn_flops = 8 * ROW_LEN * width * ff_width
    hidden_full, hidden_low = full_of(ROW_LEN, ff_width), low_of(ROW_LEN, ff_width)
    row_full, row_low = full_of(ROW_LEN, width), low_of(ROW_LEN, width)
    half_full, half_low = full_of(ROW_LEN // 2, width), low_of(ROW_LEN // 2, width)
    heads_low, mixed_low = low_of(ROW_LEN, qkv_width), low_of(ROW_LEN, out_width)
    row_scratch = [pltpu.VMEM((ROW_LEN, width), FLOAT)]

    def run_ffn(kernel, outs, operands, flops, weights):
        count = len(operands)

        def on_columns(*refs):
            late = refs[count]
            views = [late.at[:, pl.ds(i * ff_width, ff_width)] for i in weights]
            kernel(*refs[:count], *views, *refs[count + 1 :])

        return run(on_columns, outs, *operands, late_whole, flops=flops, flag=True)

    rows_one, rows_partner, qkv, qkv_partner, mixed_one, mixed_partner, part, keep, send = run(
        self_forward_kernel,
        [
            row_low, row_low, heads_low, heads_low, mixed_low, mixed_low, row_low, half_full, half_low,
        ],
        decoder, values, partner, norms, attn_own, allowed_self, allowed_partner,
        flops=10 * ROW_LEN * width * out_width * 2, flag=True, scratch=row_scratch,
    )

    def from_partner(keep, send):
        got = swap((keep + swap(send, "c").astype(FLOAT)).astype(BFLOAT), "h")
        return got, swap(got, "c")

    (after_self,) = run(
        combine_kernel, [row_full],
        decoder, values, part, swap(part, "c"), *from_partner(keep, send), flag=True,
    )

    rows_enc, hidden_own, hidden_other, active_enc_own, active_enc_other, part_enc = run_ffn(
        ffn_forward_kernel,
        [row_low, hidden_full, hidden_full, hidden_low, hidden_low, row_low],
        (decoder, after_self, norms),
        ffn_flops,
        (0, 1, 2, 3),
    )
    encoded, memory, keyvals, cross_whole = run(
        memory_kernel,
        [row_full, row_low, low_of(ROW_LEN, 2 * cross_width), low_of(width, 2 * cross_width)],
        decoder, after_self, part_enc, swap(part_enc, "c"), norms, late_whole,
        flops=4 * ROW_LEN * width * cross_width, flag=True,
    )
    keyvals = lax.ppermute(keyvals, "s", [(0, 1)])


    rows_two, queries = run(
        query_kernel,
        [row_low, low_of(ROW_LEN, cross_width)],
        decoder, after_self, norms, cross_whole,
        flops=2 * ROW_LEN * width * cross_width, flag=True,
    )
    mixed_two, part_two = run(
        cross_forward_kernel,
        [low_of(ROW_LEN, cross_width), low_of(ROW_LEN, width)],
        decoder, queries, keyvals, allowed_cross, cross_whole,
        flops=4 * ROW_LEN * width * cross_width, flag=True,
    )
    after_cross, rows_dec, active_dec_own, active_dec_other, grad_dec_own, grad_dec_other, part = run_ffn(
        ffn_both_kernel,
        [row_full, row_low, hidden_low, hidden_low, hidden_low, hidden_low, row_low],
        (decoder, after_self, part_two, swap(part_two, "c"), norms, grad_out),
        ffn_flops * 3 // 2,
        (0, 1, 2, 3),
    )
    grad_dec, low_two, sums_two_dec, grad_queries, grad_keyvals, part_two = run(
        cross_backward_kernel,
        [
            full_of(ROW_LEN, width),
            low_of(ROW_LEN, width),
            full_of(8, width),
            low_of(ROW_LEN, cross_width),
            low_of(ROW_LEN, 2 * cross_width),
            low_of(ROW_LEN, width),
        ],
        decoder, grad_out, part, swap(part, "c"), after_cross, norms, queries, keyvals, allowed_cross,
        cross_whole,
        flops=8 * ROW_LEN * width * cross_width, flag=True,
    )
    (part_dec,) = run_ffn(
        ffn_down_kernel,
        [row_low],
        (decoder, sums_two_dec, active_dec_own, active_dec_other),
        ffn_flops // 2,
        (2, 3),
    )
    decoded = after_cross + part_dec.astype(FLOAT) + swap(part_dec, "c").astype(FLOAT)
    grad_keyvals = lax.ppermute(grad_keyvals, "s", [(1, 0)])
    got_two = swap(part_two, "c")

    (part,) = run(
        keyval_backward_kernel, [row_low], decoder, grad_keyvals, cross_whole, part_dec,
        flops=4 * ROW_LEN * width * cross_width, flag=True,
    )
    grad_enc, low_enc, sums_one_enc, grad_enc_own, grad_enc_other = run_ffn(
        memory_ffn_backward_kernel,
        [row_full, row_low, full_of(8, width), hidden_low, hidden_low],
        (decoder, grad_out, part, swap(part, "c"), encoded, norms, hidden_own, hidden_other),
        ffn_flops // 2,
        (2, 3),
    )

    early_width = 4 * ff_width + 2 * cross_width
    row_part = pl.BlockSpec((ROW_LEN, width // 4), lambda i: (0, i))
    low_part = pl.BlockSpec((ROW_LEN, width // 8), lambda i: (0, i))
    high_part = pl.BlockSpec((ROW_LEN, width // 8), lambda i: (0, i + 4))
    whole_block = lambda columns: pl.BlockSpec((ROW_LEN, columns), lambda i: (0, 0))
    operands = (
        decoder, rows_enc, rows_dec, low_enc, grad_out, rows_two, rows_two, low_two, low_two, memory, memory,
        grad_enc_own, grad_enc_other, grad_dec_own, grad_dec_other,
        active_enc_own, active_enc_other, active_dec_own, active_dec_other,
        grad_queries, mixed_two, grad_keyvals,
    )
    grad_early, token = pl.pallas_call(
        early_weights_kernel,
        grid=(4,),
        out_shape=[pltpu.HBM((width, early_width), BFLOAT), full_of(8, 128)],
        in_specs=[
            SMEM, *[row_part] * 4, *[low_part, high_part] * 3, *[whole_block(ff_width)] * 8,
            whole_block(cross_width), whole_block(cross_width), whole_block(2 * cross_width),
        ],
        out_specs=[
            pl.BlockSpec(memory_space=pltpu.HBM),
            pl.BlockSpec((8, 128), lambda i: (0, 0)),
        ],
        scratch_shapes=[
            pltpu.VMEM((2, width // 4, early_width), BFLOAT),
            pltpu.SemaphoreType.DMA((2,)),
        ],
        compiler_params=LIMIT,
        cost_estimate=pl.CostEstimate(
            flops=2 * ROW_LEN * width * early_width, bytes_accessed=20 * 1024 * 1024, transcendentals=0
        ),
    )(*operands)
    (part_enc,) = pl.pallas_call(
        ffn_up_kernel,
        grid=(2,),
        out_shape=[row_low],
        in_specs=[
            SMEM, pl.BlockSpec((8, 128), lambda i: (0, 0)), hidden_block, hidden_block,
            weight_blocks[0], weight_blocks[1],
        ],
        out_specs=[row_block],
        scratch_shapes=row_scratch,
        compiler_params=WIDE_LIMIT,
        cost_estimate=pl.CostEstimate(
            flops=ffn_flops // 2, bytes_accessed=6 * 1024 * 1024, transcendentals=0
        ),
    )(decoder, token, grad_enc_own, grad_enc_other, late_whole, late_whole)
    got_enc = swap(part_enc, "c")
    grad_early = scatter_plane(grad_early)

    grad_self, low_self, low_half, sums_last = run(
        self_gradient_kernel,
        [row_full, row_low, half_low, full_of(8, width)],
        decoder, grad_enc, part_enc, got_enc, grad_dec, part_two, got_two, after_self, norms, flag=True,
        limit=WIDE_LIMIT,
    )
    low_got = swap(low_half, "h")
    low_core = swap(low_got, "c")
    grad_qkv, part = run(
        self_backward_kernel,
        [heads_low, row_low],
        low_self, qkv, allowed_self, attn_own,
        flops=10 * ROW_LEN * width * out_width * 2, limit=WIDE_LIMIT,
    )
    part, low_got, low_core = together(part, low_got, low_core)
    low_partner, grad_qkv_partner, keep, send = run(
        partner_backward_kernel,
        [row_low, heads_low, half_full, half_low],
        decoder, low_got, low_core, qkv_partner, allowed_partner, attn_own,
        flops=10 * ROW_LEN * width * out_width * 2, flag=True, limit=WIDE_LIMIT, scratch=row_scratch,
    )
    (attn_grad,) = run(
        attn_weights_kernel,
        [low_of(width, attn_width)],
        rows_one, rows_partner, grad_qkv, grad_qkv_partner, low_self, low_partner, mixed_one, mixed_partner,
        flops=8 * ROW_LEN * width * out_width, limit=WIDE_LIMIT,
    )
    attn_grad = scatter_ring_plane(attn_grad, ("z", "x"))
    grad_input, sums = run(
        input_backward_kernel,
        [row_full, full_of(8, width)],
        decoder, grad_self, part, swap(part, "c"), *from_partner(keep, send), values, norms,
        sums_last, sums_one_enc, sums_two_dec, flag=True, scratch=row_scratch, limit=WIDE_LIMIT,
    )
    sums = jnp.pad(sums.T, ((0, 0), (0, NORM_COLUMNS - sums.shape[0]))).astype(BFLOAT)
    sums = lax.all_to_all(sums, PLANE, split_axis=0, concat_axis=0, tiled=True)
    sums = jnp.sum(sums.reshape(16, -1, NORM_COLUMNS).astype(FLOAT), axis=0)
    sums = sums + swap(sums, "h")
    decoded, memory, grad_input = together(decoded, memory, grad_input)
    outputs = to_owners(pick(is_decoder, decoded.astype(BFLOAT), memory))
    grad_embedded = to_owners(grad_input)

    rows_cross = cross_query.shape[0]
    (send_h,) = run(
        send_home_kernel, [low_of(2 * rows_cross, 2 * ff_width + half_cross)], decoder, grad_early, flag=True
    )
    send_s, send_across = run(
        send_section_kernel,
        [low_of(rows_cross, cross_width), low_of(rows_cross, cross_width)],
        decoder, grad_early, send_h, flag=True,
    )
    total_up, total_down, total_query, total_keyval, total_cross_out = run(
        bring_home_kernel,
        [
            full_of(1, 2 * rows_cross, ff_width),
            full_of(1, 2 * rows_cross, ff_width),
            full_of(rows_cross, half_cross),
            full_of(rows_cross, cross_width),
            full_of(rows_cross, half_cross),
        ],
        decoder, grad_early, swap(send_h, "h"), swap(send_s, "s"), swap_across(send_across), flag=True,
    )
    total_qkv, total_out, total_gain, total_offset = run(
        attn_home_kernel,
        [
            full_of(1, 2 * rows_cross, qkv_width),
            full_of(1, 2 * rows_cross, out_width),
            full_of(1, 3, 2 * rows_cross),
            full_of(1, 3, 2 * rows_cross),
        ],
        attn_grad, sums,
    )
    return (
        outputs[None],
        grad_embedded[None],
        total_qkv,
        total_out.swapaxes(1, 2),
        total_up,
        total_down.swapaxes(1, 2),
        total_gain,
        total_offset,
        total_query,
        total_keyval,
        total_cross_out.T,
    )


def solution(mesh):
    fine = Mesh(mesh.devices.reshape(2, 4, 4, 2, 2), AXES)
    tokens = ("x", "z", "h", "c")
    tensor = ("h", "c")
    whole = ("s", "x", "z")
    return jax.shard_map(
        shards,
        mesh=fine,
        in_specs=(
            P("s", None, tokens, None),
            P("s", None, tokens, None),
            P(None, None, PLANE, None),
            P("s", PLANE, tensor),
            P("s", tensor, PLANE),
            P("s", PLANE, tensor),
            P("s", tensor, PLANE),
            P("s", None, PLANE),
            P("s", None, PLANE),
            P(whole, tensor),
            P(whole, tensor),
            P(tensor, whole),
        ),
        out_specs=(
            P("s", None, tokens, None),
            P("s", None, tokens, None),
            P("s", PLANE, tensor),
            P("s", tensor, PLANE),
            P("s", PLANE, tensor),
            P("s", tensor, PLANE),
            P("s", None, PLANE),
            P("s", None, PLANE),
            P(whole, tensor),
            P(whole, tensor),
            P(tensor, whole),
        ),
        check_vma=False,
    )
```

```python
import functools

import jax
import jax.numpy as jnp
import numpy as np
from jax import lax
from jax.experimental import pallas as pl
from jax.experimental.pallas import tpu as pltpu
from jax.sharding import Mesh
from jax.sharding import PartitionSpec as P

HEAD_DIM = 64
ROW_LEN = 256
QUARTER = 64
NORM_COLUMNS = 128

EPSILON = 1e-05
NEGATIVE = -1000000000.0
SCALING = 0.125
GELU_COEF = 0.7978845608028654
BFLOAT = jnp.bfloat16
FLOAT = jnp.float32
AXES = ("s", "x", "z", "h", "c")
PLANE = ("x", "z")
ORDER = np.concatenate([np.arange(QUARTER) + QUARTER * q for q in (0, 2, 1, 3)]).astype(np.int32)


def swap(block, axis):
    return lax.ppermute(block, axis, [(0, 1), (1, 0)])


def shift(block, axis, distance):
    size = lax.axis_size(axis)
    return lax.ppermute(block, axis, [(i, (i + distance) % size) for i in range(size)])


def place(buffer, block, index, dim):
    return lax.dynamic_update_slice_in_dim(buffer, jnp.expand_dims(block, dim), index, dim)


def take(buffer, index, dim):
    return lax.dynamic_index_in_dim(buffer, index, dim, keepdims=False)


def gather_direct(block, axis):
    here = lax.axis_index(axis)
    blocks = [block, shift(block, axis, -1), shift(block, axis, 2), shift(block, axis, 1)]
    return [((here + k) % 4, block) for k, block in enumerate(blocks)]


def gather_ring(block, axis):
    here = lax.axis_index(axis)
    half = block.shape[0] // 2
    before, after = shift(block, axis, 1), shift(block, axis, -1)
    far = jnp.concatenate([shift(before[:half], axis, 1), shift(after[half:], axis, -1)])
    return [((here + k) % 4, block) for k, block in enumerate([block, after, far, before])]


def gather_ring_plane(block, axes):
    near, far = axes
    rows, columns = block.shape
    first = jnp.zeros((4, rows, columns), block.dtype)
    for index, piece in gather_direct(block, near):
        first = place(first, piece, index, 0)
    whole = jnp.zeros((4, 4, rows, columns), block.dtype)
    dim = PLANE.index(far)
    for index, piece in gather_ring(first, far):
        whole = place(whole, piece, index, dim)
    return whole.reshape(-1, columns)


def together(*arrays):
    return lax.optimization_barrier(arrays)


def scatter_direct(blocks, axis):
    here = lax.axis_index(axis)
    parts = [take(blocks, (here + k) % 4, 0) for k in range(4)]
    total = parts[0].astype(FLOAT)
    for distance in (1, 2, -1):
        total = total + shift(parts[distance % 4].astype(BFLOAT), axis, distance).astype(FLOAT)
    return total


def scatter_ring(blocks, axis, dim):
    here = lax.axis_index(axis)
    own, after, far, before = [take(blocks, (here + k) % 4, dim) for k in range(4)]
    half = own.shape[0] // 2
    far = far.astype(BFLOAT)
    top = shift(far[:half], axis, 1).astype(FLOAT)
    bottom = shift(far[half:], axis, -1).astype(FLOAT)
    after = jnp.concatenate([after[:half].astype(FLOAT) + top, after[half:].astype(FLOAT)])
    before = jnp.concatenate([before[:half].astype(FLOAT), before[half:].astype(FLOAT) + bottom])
    from_before = shift(after.astype(BFLOAT), axis, 1).astype(FLOAT)
    from_after = shift(before.astype(BFLOAT), axis, -1).astype(FLOAT)
    return own.astype(FLOAT) + from_before + from_after


def scatter_ring_plane(block, axes):
    near, far = axes
    rows = block.shape[0] // 16
    blocks = block.reshape(4, 4, rows, -1)
    return scatter_direct(scatter_ring(blocks, far, PLANE.index(far)), near)


def swap_across(block):
    return lax.ppermute(block, ("s", "h"), [(0, 3), (3, 0), (1, 2), (2, 1)])


def gelu_tanh(values):
    return (
        0.5 * values * (1.0 + jnp.tanh(GELU_COEF * (values + 0.044715 * values * values * values)))
    )


def gelu_slope(values):
    squares = values * values
    curve = jnp.tanh(GELU_COEF * (values + 0.044715 * values * squares))
    return 0.5 * (1.0 + curve) + 0.5 * values * (1.0 - curve * curve) * (
        GELU_COEF * (1.0 + 3.0 * 0.044715 * squares)
    )


def segment_ids(lengths_row):
    ends = jnp.cumsum(lengths_row)
    positions = jnp.asarray(ORDER)
    return jnp.sum((positions[:, None] >= ends[None, :]).astype(jnp.int32), axis=1)


def dot(left, right):
    return jnp.dot(left, right, preferred_element_type=FLOAT)


def dot_left(left, right):
    return lax.dot_general(left, right, (((0,), (0,)), ((), ())), preferred_element_type=FLOAT)


def dot_right(left, right):
    return lax.dot_general(left, right, (((1,), (1,)), ((), ())), preferred_element_type=FLOAT)


def normalize(stream):
    centred = stream - jnp.mean(stream, axis=-1, keepdims=True)
    inverse = lax.rsqrt(jnp.mean(centred * centred, axis=-1, keepdims=True) + EPSILON)
    return centred * inverse, inverse


def layer_norm(stream, norms, index):
    unit, _ = normalize(stream)
    return (unit * norms[index : index + 1] + norms[index + 3 : index + 4]).astype(BFLOAT)


def norm_backward(grad_out, stream, gain):
    unit, inverse = normalize(stream)
    scaled = grad_out * gain
    inner = (
        scaled
        - jnp.mean(scaled, axis=-1, keepdims=True)
        - unit * jnp.mean(scaled * unit, axis=-1, keepdims=True)
    )
    sums = jnp.concatenate(
        [
            jnp.sum(grad_out * unit, axis=0, keepdims=True),
            jnp.sum(grad_out, axis=0, keepdims=True),
            jnp.zeros((6, grad_out.shape[1]), FLOAT),
        ]
    )
    return inverse * inner, sums


def add_parts(own_ref, other_ref):
    return own_ref[...].astype(FLOAT) + other_ref[...].astype(FLOAT)


def softmax(query, key, mask):
    scores = jnp.where(mask, dot_right(query, key) * SCALING, NEGATIVE)
    expo_scores = jnp.exp(scores - jnp.max(scores, axis=-1, keepdims=True))
    return expo_scores / jnp.sum(expo_scores, axis=-1, keepdims=True)


def head_backward(query, key, value, mask, grad_mixed):
    weights = softmax(query, key, mask)
    grad_value = dot_left(weights.astype(BFLOAT), grad_mixed)
    grad_weights = dot_right(grad_mixed, value)
    grad_scores = weights * (
        grad_weights - jnp.sum(weights * grad_weights, axis=-1, keepdims=True)
    )
    grad_scores = grad_scores.astype(BFLOAT)
    grad_query = dot(grad_scores, key) * SCALING
    grad_key = dot_left(grad_scores, query) * SCALING
    return grad_query.astype(BFLOAT), grad_key.astype(BFLOAT), grad_value.astype(BFLOAT)


def head(ref, place):
    return ref[:, place * HEAD_DIM : (place + 1) * HEAD_DIM]


def put_halves(place, whole, mine, others):
    length = mine.shape[0]
    whole[pl.ds(pl.multiple_of(place[1] * length, length), length), :] = mine[...].astype(whole.dtype)
    whole[pl.ds(pl.multiple_of((1 - place[1]) * length, length), length), :] = others[...].astype(
        whole.dtype
    )


def take_halves(place, whole, keep, send):
    length = keep.shape[0]
    keep[...] = whole[pl.ds(pl.multiple_of(place[1] * length, length), length), :]
    send[...] = whole[pl.ds(pl.multiple_of((1 - place[1]) * length, length), length), :].astype(BFLOAT)


def self_forward_kernel(
    place, stream, partner, norms, weights, mask, mask_partner,
    rows, rows_partner, qkv, qkv_partner, mixed, mixed_partner, part, keep, send, total,
):
    quarter = mixed.shape[1]
    width = 3 * quarter
    rows[...] = layer_norm(stream[...], norms, 0)
    rows_partner[...] = layer_norm(partner[...].astype(FLOAT), norms, 0)
    for row, heads, mixes, allow in (
        (rows, qkv, mixed, mask), (rows_partner, qkv_partner, mixed_partner, mask_partner)
    ):
        allowed = allow[...] > 0.5
        heads[...] = dot(row[...], weights[:, :width]).astype(BFLOAT)
        for i in range(quarter // HEAD_DIM):
            weight = softmax(head(heads, 3 * i), head(heads, 3 * i + 1), allowed)
            out = dot(weight.astype(BFLOAT), head(heads, 3 * i + 2))
            mixes[:, i * HEAD_DIM : (i + 1) * HEAD_DIM] = out.astype(BFLOAT)
    part[...] = dot_right(mixed[...], weights[:, width : width + quarter]).astype(BFLOAT)
    total[...] = dot_right(mixed_partner[...], weights[:, width : width + quarter])
    take_halves(place, total, keep, send)


def combine_kernel(place, stream, own, other, got, got_core, after):
    put_halves(place, after, got, got_core)
    after[...] += stream[...] + add_parts(own, other)


def ffn_forward_kernel(
    decoder, stream, norms, up_own, up_other, down_own, down_other,
    rows, hidden_own, hidden_other, active_own, active_other, part,
):
    rows[...] = layer_norm(stream[...], norms, 2)

    @pl.when(decoder[0] == 0)
    def _():
        term = None
        for up, down, hidden, active in (
            (up_own, down_own, hidden_own, active_own),
            (up_other, down_other, hidden_other, active_other),
        ):
            raised = dot(rows[...], up[...])
            hidden[...] = raised
            active[...] = gelu_tanh(raised).astype(BFLOAT)
            piece = dot_right(active[...], down[...])
            term = piece if term is None else term + piece
        part[...] = term.astype(BFLOAT)


def ffn_both_kernel(
    decoder, stream, own, other, norms, cotangent, up_own, up_other, down_own, down_other,
    after, rows, active_own, active_other, grad_own, grad_other, part,
):
    @pl.when(decoder[0] == 1)
    def _():
        after[...] = stream[...] + add_parts(own, other)
        rows[...] = layer_norm(after[...], norms, 2)
        term = None
        for up, down, active, grad in (
            (up_own, down_own, active_own, grad_own),
            (up_other, down_other, active_other, grad_other),
        ):
            raised = dot(rows[...], up[...])
            active[...] = gelu_tanh(raised).astype(BFLOAT)
            grad[...] = (dot(cotangent[...], down[...]) * gelu_slope(raised)).astype(BFLOAT)
            piece = dot_right(grad[...], up[...])
            term = piece if term is None else term + piece
        part[...] = term.astype(BFLOAT)


def ffn_down_kernel(decoder, after_this, active_own, active_other, down_own, down_other, part):
    @pl.when(decoder[0] == 1)
    def _():
        term = dot_right(active_own[...], down_own[...]) + dot_right(active_other[...], down_other[...])
        part[...] = term.astype(BFLOAT)


def sort_rows(gathered, ordered, columns):
    depth = ordered.shape[0]
    piece = depth // 32
    first, to = columns
    wide = to.stop - to.start
    for i in range(16):
        for j in range(2):
            start = j * depth // 2 + i * piece
            ordered[start : start + piece, to] = gathered[
                (2 * i + j) * piece : (2 * i + j + 1) * piece, first : first + wide
            ]


def memory_kernel(
    decoder, stream, own, other, norms, late, encoded, memory, keyvals, weights
):
    wide = weights.shape[1] // 2
    half = wide // 2
    base = late.shape[1] - 2 * wide

    @pl.when(decoder[0] == 1)
    def _():
        for side in range(2):
            for part in range(2):
                start = part * wide + side * half
                sort_rows(late, weights, (base + side * wide + part * half, slice(start, start + half)))

    @pl.when(decoder[0] == 0)
    def _():
        sort_rows(late, weights, (base, slice(0, 2 * wide)))
        encoded[...] = stream[...] + add_parts(own, other)
        memory[...] = layer_norm(encoded[...], norms, 1)
        keyvals[...] = dot(memory[...], weights[...]).astype(BFLOAT)


def query_kernel(decoder, stream, norms, weights, rows, queries):
    @pl.when(decoder[0] == 1)
    def _():
        rows[...] = layer_norm(stream[...], norms, 1)
        queries[...] = dot(rows[...], weights[:, : queries.shape[1]]).astype(BFLOAT)


def cross_forward_kernel(decoder, queries, keyvals, mask, weights, mixed, part):
    @pl.when(decoder[0] == 1)
    def _():
        allowed = mask[...] > 0.5
        for i in range(queries.shape[1] // HEAD_DIM):
            weight = softmax(head(queries, i), head(keyvals, 2 * i), allowed)
            out = dot(weight.astype(BFLOAT), head(keyvals, 2 * i + 1))
            mixed[:, i * HEAD_DIM : (i + 1) * HEAD_DIM] = out.astype(BFLOAT)
        part[...] = dot_right(mixed[...], weights[:, queries.shape[1] :]).astype(BFLOAT)


def memory_ffn_backward_kernel(
    decoder, cotangent, own, other, stream, norms, hidden_own, hidden_other, down_own, down_other,
    grad, low, sums, grad_own, grad_other,
):
    @pl.when(decoder[0] == 0)
    def _():
        into, totals = norm_backward(
            cotangent[...].astype(FLOAT) + add_parts(own, other), stream[...], norms[1:2]
        )
        grad[...] = into
        low[...] = into.astype(BFLOAT)
        sums[...] = totals
        for down, hidden, out in ((down_own, hidden_own, grad_own), (down_other, hidden_other, grad_other)):
            out[...] = (dot(low[...], down[...]) * gelu_slope(hidden[...])).astype(BFLOAT)


def ffn_up_kernel(decoder, after_this, grad_own, grad_other, up_own, up_other, part, total):
    step = pl.program_id(0)

    @pl.when(decoder[0] == 0)
    def _():
        term = dot_right(grad_own[...], up_own[...]) + dot_right(grad_other[...], up_other[...])

        @pl.when(step == 0)
        def _():
            total[...] = term

        @pl.when(step > 0)
        def _():
            part[...] = (total[...] + term).astype(BFLOAT)


def cross_backward_kernel(
    decoder, cotangent, own, other, stream, norms, queries, keyvals, mask, weights,
    grad, low, sums, grad_queries, grad_keyvals, part,
):
    @pl.when(decoder[0] == 1)
    def _():
        allowed = mask[...] > 0.5
        into, totals = norm_backward(add_parts(own, other), stream[...], norms[2:3])
        grad[...] = cotangent[...].astype(FLOAT) + into
        low[...] = grad[...].astype(BFLOAT)
        sums[...] = totals
        grad_mixed = dot(low[...], weights[:, queries.shape[1] :]).astype(BFLOAT)
        for i in range(queries.shape[1] // HEAD_DIM):
            one, two, three = head_backward(
                head(queries, i),
                head(keyvals, 2 * i),
                head(keyvals, 2 * i + 1),
                allowed,
                grad_mixed[:, i * HEAD_DIM : (i + 1) * HEAD_DIM],
            )
            grad_queries[:, i * HEAD_DIM : (i + 1) * HEAD_DIM] = one
            grad_keyvals[:, 2 * i * HEAD_DIM : (2 * i + 1) * HEAD_DIM] = two
            grad_keyvals[:, (2 * i + 1) * HEAD_DIM : (2 * i + 2) * HEAD_DIM] = three
        part[...] = dot_right(grad_queries[...], weights[:, : queries.shape[1]]).astype(BFLOAT)


def keyval_backward_kernel(decoder, grad_keyvals, weights, after_this, part):
    @pl.when(decoder[0] == 0)
    def _():
        part[...] = dot_right(grad_keyvals[...], weights[...]).astype(BFLOAT)


def self_gradient_kernel(
    place, grad_enc, own_enc, other_enc, grad_dec, own_dec, other_dec, stream, norms, grad, low, low_half, sums
):
    @pl.when(place[0] == 1)
    def _():
        into, totals = norm_backward(add_parts(own_dec, other_dec), stream[...], norms[1:2])
        grad[...] = grad_dec[...] + into
        sums[...] = totals

    @pl.when(place[0] == 0)
    def _():
        into, totals = norm_backward(add_parts(own_enc, other_enc), stream[...], norms[2:3])
        grad[...] = grad_enc[...] + into
        sums[...] = totals

    low[...] = grad[...].astype(BFLOAT)
    half = low_half.shape[0]
    low_half[...] = low[pl.ds(pl.multiple_of(place[1] * half, half), half), :]


def row_backward(low, qkv, mask, weights, grad_qkv):
    allowed = mask[...] > 0.5
    quarter = qkv.shape[1] // 3
    width = 3 * quarter
    grad_mixed = dot(low[...], weights[:, width : width + quarter]).astype(BFLOAT)
    for i in range(quarter // HEAD_DIM):
        grads = head_backward(
            head(qkv, 3 * i),
            head(qkv, 3 * i + 1),
            head(qkv, 3 * i + 2),
            allowed,
            grad_mixed[:, i * HEAD_DIM : (i + 1) * HEAD_DIM],
        )
        for k in range(3):
            grad_qkv[:, (3 * i + k) * HEAD_DIM : (3 * i + k + 1) * HEAD_DIM] = grads[k]
    return dot_right(grad_qkv[...], weights[:, :width])


def self_backward_kernel(low, qkv, mask, weights, grad_qkv, part):
    part[...] = row_backward(low, qkv, mask, weights, grad_qkv).astype(BFLOAT)


def partner_backward_kernel(
    place, low_got, low_core, qkv, mask, weights, low, grad_qkv, keep, send, total
):
    put_halves(place, low, low_got, low_core)
    total[...] = row_backward(low, qkv, mask, weights, grad_qkv)
    take_halves(place, total, keep, send)


def input_backward_kernel(
    place, grad, own, other, got, got_core, stream, norms, last, one_enc, two_dec, grad_input, sums, total
):
    put_halves(place, total, got, got_core)
    into, zero = norm_backward(total[...] + add_parts(own, other), stream[...], norms[0:1])
    grad_input[...] = grad[...] + into
    is_decoder = place[0] == 1
    one = jnp.where(is_decoder, last[...], one_enc[...])
    two = jnp.where(is_decoder, two_dec[...], last[...])
    sums[...] = jnp.concatenate(
        [zero[0:1], one[0:1], two[0:1], zero[1:2], one[1:2], two[1:2], jnp.zeros((2, zero.shape[1]), FLOAT)]
    )


def early_weights_kernel(
    decoder, rows_enc, rows_dec, low_enc, low_dec, rows_two_low, rows_two_high, low_two_low, low_two_high,
    memory_low, memory_high, hidden_enc_own, hidden_enc_other, hidden_dec_own, hidden_dec_other,
    active_enc_own, active_enc_other, active_dec_own, active_dec_other, queries, mixed, keyvals, whole, token, slots, sems,
):
    token[...] = jnp.zeros_like(token)
    step = pl.program_id(0)
    slot = lax.rem(step, 2)
    out = slots.at[slot]
    rows = slots.shape[1]

    def copy_of(step, slot):
        start = pl.multiple_of(step * rows, rows)
        return pltpu.make_async_copy(slots.at[slot], whole.at[pl.ds(start, rows), :], sems.at[slot])

    @pl.when(step >= 2)
    def _():
        copy_of(step - 2, slot).wait()

    hidden = hidden_enc_own.shape[1]
    half = queries.shape[1]
    piece = rows_two_low.shape[1] // 4

    def put(start, value):
        out[:, start : start + value.shape[1]] = value.astype(BFLOAT)

    def put_cross(start, low, high):
        for i in range(4):
            for j, value in enumerate((low, high)):
                out[
                    (2 * i + j) * piece : (2 * i + j + 1) * piece, start : start + value.shape[1]
                ] = value[i * piece : (i + 1) * piece].astype(BFLOAT)

    @pl.when(decoder[0] == 1)
    def _():
        put(0, dot_left(rows_dec[...], hidden_dec_own[...]))
        put(hidden, dot_left(rows_dec[...], hidden_dec_other[...]))
        put(2 * hidden, dot_left(low_dec[...], active_dec_own[...]))
        put(3 * hidden, dot_left(low_dec[...], active_dec_other[...]))
        put_cross(4 * hidden, dot_left(rows_two_low[...], queries[...]), dot_left(rows_two_high[...], queries[...]))
        put_cross(4 * hidden + half, dot_left(low_two_low[...], mixed[...]), dot_left(low_two_high[...], mixed[...]))

    @pl.when(decoder[0] == 0)
    def _():
        put(0, dot_left(rows_enc[...], hidden_enc_own[...]))
        put(hidden, dot_left(rows_enc[...], hidden_enc_other[...]))
        put(2 * hidden, dot_left(low_enc[...], active_enc_own[...]))
        put(3 * hidden, dot_left(low_enc[...], active_enc_other[...]))
        put_cross(4 * hidden, dot_left(memory_low[...], keyvals[...]), dot_left(memory_high[...], keyvals[...]))

    copy_of(step, slot).start()

    @pl.when(step == pl.num_programs(0) - 1)
    def _():
        copy_of(step - 1, 1 - slot).wait()
        copy_of(step, slot).wait()


def attn_weights_kernel(
    rows, rows_partner, grad_qkv, grad_qkv_partner, low, low_partner, mixed, mixed_partner, out
):
    width = grad_qkv.shape[1]
    out[:, :width] = (
        dot_left(rows[...], grad_qkv[...]) + dot_left(rows_partner[...], grad_qkv_partner[...])
    ).astype(BFLOAT)
    out[:, width:] = (
        dot_left(low[...], mixed[...]) + dot_left(low_partner[...], mixed_partner[...])
    ).astype(BFLOAT)


def gather_plane(block):
    return lax.all_gather(block, PLANE, axis=0, tiled=True)


def scatter_plane(block):
    return lax.psum_scatter(block, PLANE, scatter_dimension=0, tiled=True)


def send_home_kernel(decoder, early, send_h):
    half = send_h.shape[1] // 9
    hidden = 4 * half
    rows = send_h.shape[0] // 2
    send_h[:, :hidden] = early[:, hidden : 2 * hidden]
    send_h[:, hidden : 2 * hidden] = early[:, 3 * hidden : 4 * hidden]
    start = 4 * hidden

    @pl.when(decoder[0] == 1)
    def _():
        send_h[:rows, 2 * hidden :] = early[rows:, start + half : start + 2 * half]
        send_h[rows:, 2 * hidden :] = early[rows:, start + 3 * half : start + 4 * half]

    @pl.when(decoder[0] == 0)
    def _():
        send_h[:rows, 2 * hidden :] = early[:rows, start + 2 * half : start + 3 * half]
        send_h[rows:, 2 * hidden :] = early[:rows, start + 3 * half : start + 4 * half]


def send_section_kernel(decoder, early, after_this, send_s, send_across):
    rows = send_s.shape[0]
    wide = send_s.shape[1]
    half = wide // 2
    start = early.shape[1] - 2 * wide

    @pl.when(decoder[0] == 1)
    def _():
        send_s[:, :half] = early[:rows, start : start + half]
        send_s[:, half:] = early[:rows, start + 2 * half : start + 3 * half]
        send_across[:, :half] = early[:rows, start + half : start + 2 * half]
        send_across[:, half:] = early[:rows, start + 3 * half : start + 4 * half]

    @pl.when(decoder[0] == 0)
    def _():
        send_s[...] = early[rows:, start : start + 2 * half]
        send_across[...] = early[rows:, start + 2 * half :]


def bring_home_kernel(decoder, early, got_h, got_s, got_across, up, down, query, keyval, out):
    rows = got_s.shape[0]
    wide = got_s.shape[1]
    hidden = (early.shape[1] - 2 * wide) // 4
    half = wide // 2
    start = 4 * hidden
    up[0] = early[:, :hidden].astype(FLOAT) + got_h[:, :hidden].astype(FLOAT)
    down[0] = early[:, 2 * hidden : 3 * hidden].astype(FLOAT) + got_h[:, hidden : 2 * hidden].astype(FLOAT)
    far = got_s[...].astype(FLOAT) + got_across[...].astype(FLOAT)
    near_left = got_h[:rows, 2 * hidden :].astype(FLOAT)
    near_right = got_h[rows:, 2 * hidden :].astype(FLOAT)

    @pl.when(decoder[0] == 1)
    def _():
        query[...] = early[rows:, start : start + half].astype(FLOAT) + near_left
        out[...] = early[rows:, start + 2 * half : start + 3 * half].astype(FLOAT) + near_right
        keyval[...] = far

    @pl.when(decoder[0] == 0)
    def _():
        keyval[:, :half] = early[:rows, start : start + half].astype(FLOAT) + near_left
        keyval[:, half:] = early[:rows, start + half : start + 2 * half].astype(FLOAT) + near_right
        query[...] = far[:, :half]
        out[...] = far[:, half:]


def attn_home_kernel(own, norms, qkv, out, gain, offset):
    width = qkv.shape[2]
    qkv[0] = own[:, :width]
    out[0] = own[:, width:]
    sums = norms[...].T
    gain[0] = sums[:3]
    offset[0] = sums[3:6]


VMEM = pl.BlockSpec(memory_space=pltpu.VMEM)
SMEM = pl.BlockSpec(memory_space=pltpu.SMEM)
LIMIT = pltpu.CompilerParams(vmem_limit_bytes=20 * 1024 * 1024)
WIDE_LIMIT = pltpu.CompilerParams(vmem_limit_bytes=56 * 1024 * 1024)


def low_of(*dims):
    return jax.ShapeDtypeStruct(dims, BFLOAT)


def full_of(*dims):
    return jax.ShapeDtypeStruct(dims, FLOAT)


def run(kernel, outs, *operands, flops=0, scratch=(), flag=False, specs=None, limit=LIMIT):
    specs = specs or {}
    whole = lambda o: pl.BlockSpec(o.shape, lambda i: (0,) * len(o.shape)) if specs else VMEM
    in_specs = [specs.get(i, whole(o)) for i, o in enumerate(operands)]
    if flag:
        in_specs[0] = SMEM
    moved = sum(o.size * o.dtype.itemsize for o in (*operands, *outs))
    return pl.pallas_call(
        kernel,
        grid=(1,) if specs else (),
        out_shape=list(outs),
        in_specs=in_specs,
        out_specs=[whole(o) for o in outs],
        scratch_shapes=list(scratch),
        compiler_params=limit,
        cost_estimate=pl.CostEstimate(flops=flops, bytes_accessed=moved, transcendentals=0),
    )(*operands)


def shards(
    embedded,
    cotangent,
    lengths,
    attn_qkv,
    attn_out,
    ffn_up,
    ffn_down,
    norm_gain,
    norm_bias,
    cross_query,
    cross_kv,
    cross_out,
):
    is_decoder = lax.axis_index("s") == 1
    first_half = lax.axis_index("h") == 0
    core = lax.axis_index("c")

    def pick(flag, yes, no):
        return jnp.where(flag, yes, no)

    def own_rows(pairs):
        mine = [pick(first_half, pair[0], pair[1]) for pair in pairs]
        got = swap(jnp.concatenate([pick(first_half, pair[1], pair[0]) for pair in pairs], axis=1), "h")
        mine = jnp.concatenate(mine, axis=1)
        half = jnp.concatenate([pick(first_half, mine, got), pick(first_half, got, mine)])
        got = swap(half, "c")
        whole = jnp.concatenate([pick(core == 0, half, got), pick(core == 0, got, half)])
        return jnp.split(whole, len(pairs), axis=1)

    def to_owners(row):
        half = lax.dynamic_slice_in_dim(row, core * 2 * QUARTER, 2 * QUARTER, 0)
        low, high = half[:QUARTER], half[QUARTER:]
        mine = pick(first_half, low, high)
        got = swap(pick(first_half, high, low), "h")
        return jnp.stack([pick(first_half, mine, got), pick(first_half, got, mine)])

    qkv_width = attn_qkv.shape[2]
    out_width = attn_out.shape[1]
    attn_width = qkv_width + out_width
    ff_width = ffn_up.shape[2]
    cross_width = cross_kv.shape[1]
    half_cross = cross_width // 2
    depth = embedded.shape[-1]

    own_ffn = jnp.concatenate([ffn_up[0], ffn_down[0].T], axis=1)
    query_out = jnp.concatenate([cross_query, cross_out.T], axis=1)
    kept = pick(is_decoder, query_out, cross_kv)
    give = pick(is_decoder, cross_kv, query_out)
    own_ffn, kept, give = together(own_ffn, kept, give)
    other_ffn = swap(own_ffn, "h")
    cross = [
        jnp.concatenate([pick(is_decoder, far, near), pick(is_decoder, near, far)])
        for near, far in ((kept, swap(give, "s")), (swap(kept, "h"), swap_across(give)))
    ]
    late_pack = jnp.concatenate(
        [
            own_ffn[:, :ff_width], other_ffn[:, :ff_width], own_ffn[:, ff_width:], other_ffn[:, ff_width:],
            *cross,
        ],
        axis=1,
    )
    late_pack, attn_qkv, attn_out, norm_gain, norm_bias, embedded, cotangent = together(
        late_pack, attn_qkv, attn_out, norm_gain, norm_bias, embedded, cotangent
    )
    late_whole = gather_plane(late_pack)

    norms = jnp.concatenate([norm_gain[0], norm_bias[0]]).T
    norms = jnp.pad(norms, ((0, 0), (0, NORM_COLUMNS - norms.shape[1])))
    attn_own = gather_ring_plane(
        jnp.concatenate([attn_qkv[0], attn_out[0].T, norms], axis=1), ("z", "x")
    )

    inputs, grads = embedded[0], cotangent[0]
    mine = jnp.concatenate([inputs[0], inputs[1], pick(first_half, grads[0], grads[1])])
    got = swap(jnp.concatenate([inputs[0], inputs[1], pick(first_half, grads[1], grads[0])]), "h")
    mine, got = (block.reshape(3, 1, QUARTER, depth) for block in (mine, got))
    half = jnp.concatenate([pick(first_half, mine, got), pick(first_half, got, mine)], axis=1)
    half = half.reshape(3, 2 * QUARTER, depth)
    got = swap(half, "c")
    whole = jnp.concatenate([pick(core == 0, half, got), pick(core == 0, got, half)], axis=1)
    values = pick(first_half, whole[0], whole[1]).astype(FLOAT)
    partner = pick(first_half, whole[1], whole[0])
    grad_out = whole[2]

    norms = attn_own[:, attn_width : attn_width + 8].T.astype(FLOAT)
    decoder = jnp.stack([lax.axis_index("s"), core]).astype(jnp.int32)

    positions = jnp.asarray(ORDER)
    ordered = (positions[None, :] <= positions[:, None]) | jnp.logical_not(is_decoder)
    masks = []
    for row_lengths in (
        pick(first_half, lengths[:, 0, 0], lengths[:, 1, 0]),
        pick(first_half, lengths[:, 1, 0], lengths[:, 0, 0]),
    ):
        source_pair = segment_ids(row_lengths[0])
        target_pair = segment_ids(row_lengths[1])
        own_pair = pick(is_decoder, target_pair, source_pair)
        masks.append(((own_pair[:, None] == own_pair[None, :]) & ordered).astype(BFLOAT))
        if len(masks) == 1:
            allowed_cross = (target_pair[:, None] == source_pair[None, :]).astype(BFLOAT)
    allowed_self, allowed_partner = masks

    width = values.shape[1]
    steps = 2
    block = ff_width // steps
    row_block = pl.BlockSpec((ROW_LEN, width), lambda i: (0, 0))
    norm_block = pl.BlockSpec((8, width), lambda i: (0, 0))
    weight_blocks = [
        pl.BlockSpec((width, block), functools.partial(lambda start, i: (0, start * steps + i), start))
        for start in range(4)
    ]
    hidden_block = pl.BlockSpec((ROW_LEN, block), lambda i: (0, i))
    ffn_flops = 8 * ROW_LEN * width * ff_width
    hidden_full, hidden_low = full_of(ROW_LEN, ff_width), low_of(ROW_LEN, ff_width)
    row_full, row_low = full_of(ROW_LEN, width), low_of(ROW_LEN, width)
    half_full, half_low = full_of(ROW_LEN // 2, width), low_of(ROW_LEN // 2, width)
    heads_low, mixed_low = low_of(ROW_LEN, qkv_width), low_of(ROW_LEN, out_width)
    row_scratch = [pltpu.VMEM((ROW_LEN, width), FLOAT)]

    def run_ffn(kernel, outs, operands, flops, weights):
        count = len(operands)

        def on_columns(*refs):
            late = refs[count]
            views = [late.at[:, pl.ds(i * ff_width, ff_width)] for i in weights]
            kernel(*refs[:count], *views, *refs[count + 1 :])

        return run(on_columns, outs, *operands, late_whole, flops=flops, flag=True)

    rows_one, rows_partner, qkv, qkv_partner, mixed_one, mixed_partner, part, keep, send = run(
        self_forward_kernel,
        [
            row_low, row_low, heads_low, heads_low, mixed_low, mixed_low, row_low, half_full, half_low,
        ],
        decoder, values, partner, norms, attn_own, allowed_self, allowed_partner,
        flops=10 * ROW_LEN * width * out_width * 2, flag=True, scratch=row_scratch,
    )

    def from_partner(keep, send):
        got = swap((keep + swap(send, "c").astype(FLOAT)).astype(BFLOAT), "h")
        return got, swap(got, "c")

    (after_self,) = run(
        combine_kernel, [row_full],
        decoder, values, part, swap(part, "c"), *from_partner(keep, send), flag=True,
    )

    rows_enc, hidden_own, hidden_other, active_enc_own, active_enc_other, part_enc = run_ffn(
        ffn_forward_kernel,
        [row_low, hidden_full, hidden_full, hidden_low, hidden_low, row_low],
        (decoder, after_self, norms),
        ffn_flops,
        (0, 1, 2, 3),
    )
    encoded, memory, keyvals, cross_whole = run(
        memory_kernel,
        [row_full, row_low, low_of(ROW_LEN, 2 * cross_width), low_of(width, 2 * cross_width)],
        decoder, after_self, part_enc, swap(part_enc, "c"), norms, late_whole,
        flops=4 * ROW_LEN * width * cross_width, flag=True,
    )
    keyvals = lax.ppermute(keyvals, "s", [(0, 1)])


    rows_two, queries = run(
        query_kernel,
        [row_low, low_of(ROW_LEN, cross_width)],
        decoder, after_self, norms, cross_whole,
        flops=2 * ROW_LEN * width * cross_width, flag=True,
    )
    mixed_two, part_two = run(
        cross_forward_kernel,
        [low_of(ROW_LEN, cross_width), low_of(ROW_LEN, width)],
        decoder, queries, keyvals, allowed_cross, cross_whole,
        flops=4 * ROW_LEN * width * cross_width, flag=True,
    )
    after_cross, rows_dec, active_dec_own, active_dec_other, grad_dec_own, grad_dec_other, part = run_ffn(
        ffn_both_kernel,
        [row_full, row_low, hidden_low, hidden_low, hidden_low, hidden_low, row_low],
        (decoder, after_self, part_two, swap(part_two, "c"), norms, grad_out),
        ffn_flops * 3 // 2,
        (0, 1, 2, 3),
    )
    grad_dec, low_two, sums_two_dec, grad_queries, grad_keyvals, part_two = run(
        cross_backward_kernel,
        [
            full_of(ROW_LEN, width),
            low_of(ROW_LEN, width),
            full_of(8, width),
            low_of(ROW_LEN, cross_width),
            low_of(ROW_LEN, 2 * cross_width),
            low_of(ROW_LEN, width),
        ],
        decoder, grad_out, part, swap(part, "c"), after_cross, norms, queries, keyvals, allowed_cross,
        cross_whole,
        flops=8 * ROW_LEN * width * cross_width, flag=True,
    )
    (part_dec,) = run_ffn(
        ffn_down_kernel,
        [row_low],
        (decoder, sums_two_dec, active_dec_own, active_dec_other),
        ffn_flops // 2,
        (2, 3),
    )
    decoded = after_cross + part_dec.astype(FLOAT) + swap(part_dec, "c").astype(FLOAT)
    grad_keyvals = lax.ppermute(grad_keyvals, "s", [(1, 0)])
    got_two = swap(part_two, "c")

    (part,) = run(
        keyval_backward_kernel, [row_low], decoder, grad_keyvals, cross_whole, part_dec,
        flops=4 * ROW_LEN * width * cross_width, flag=True,
    )
    grad_enc, low_enc, sums_one_enc, grad_enc_own, grad_enc_other = run_ffn(
        memory_ffn_backward_kernel,
        [row_full, row_low, full_of(8, width), hidden_low, hidden_low],
        (decoder, grad_out, part, swap(part, "c"), encoded, norms, hidden_own, hidden_other),
        ffn_flops // 2,
        (2, 3),
    )

    early_width = 4 * ff_width + 2 * cross_width
    row_part = pl.BlockSpec((ROW_LEN, width // 4), lambda i: (0, i))
    low_part = pl.BlockSpec((ROW_LEN, width // 8), lambda i: (0, i))
    high_part = pl.BlockSpec((ROW_LEN, width // 8), lambda i: (0, i + 4))
    whole_block = lambda columns: pl.BlockSpec((ROW_LEN, columns), lambda i: (0, 0))
    operands = (
        decoder, rows_enc, rows_dec, low_enc, grad_out, rows_two, rows_two, low_two, low_two, memory, memory,
        grad_enc_own, grad_enc_other, grad_dec_own, grad_dec_other,
        active_enc_own, active_enc_other, active_dec_own, active_dec_other,
        grad_queries, mixed_two, grad_keyvals,
    )
    grad_early, token = pl.pallas_call(
        early_weights_kernel,
        grid=(4,),
        out_shape=[pltpu.HBM((width, early_width), BFLOAT), full_of(8, 128)],
        in_specs=[
            SMEM, *[row_part] * 4, *[low_part, high_part] * 3, *[whole_block(ff_width)] * 8,
            whole_block(cross_width), whole_block(cross_width), whole_block(2 * cross_width),
        ],
        out_specs=[
            pl.BlockSpec(memory_space=pltpu.HBM),
            pl.BlockSpec((8, 128), lambda i: (0, 0)),
        ],
        scratch_shapes=[
            pltpu.VMEM((2, width // 4, early_width), BFLOAT),
            pltpu.SemaphoreType.DMA((2,)),
        ],
        compiler_params=LIMIT,
        cost_estimate=pl.CostEstimate(
            flops=2 * ROW_LEN * width * early_width, bytes_accessed=20 * 1024 * 1024, transcendentals=0
        ),
    )(*operands)
    (part_enc,) = pl.pallas_call(
        ffn_up_kernel,
        grid=(2,),
        out_shape=[row_low],
        in_specs=[
            SMEM, pl.BlockSpec((8, 128), lambda i: (0, 0)), hidden_block, hidden_block,
            weight_blocks[0], weight_blocks[1],
        ],
        out_specs=[row_block],
        scratch_shapes=row_scratch,
        compiler_params=WIDE_LIMIT,
        cost_estimate=pl.CostEstimate(
            flops=ffn_flops // 2, bytes_accessed=6 * 1024 * 1024, transcendentals=0
        ),
    )(decoder, token, grad_enc_own, grad_enc_other, late_whole, late_whole)
    got_enc = swap(part_enc, "c")
    grad_early = scatter_plane(grad_early)

    grad_self, low_self, low_half, sums_last = run(
        self_gradient_kernel,
        [row_full, row_low, half_low, full_of(8, width)],
        decoder, grad_enc, part_enc, got_enc, grad_dec, part_two, got_two, after_self, norms, flag=True,
        limit=WIDE_LIMIT,
    )
    low_got = swap(low_half, "h")
    low_core = swap(low_got, "c")
    grad_qkv, part = run(
        self_backward_kernel,
        [heads_low, row_low],
        low_self, qkv, allowed_self, attn_own,
        flops=10 * ROW_LEN * width * out_width * 2, limit=WIDE_LIMIT,
    )
    part, low_got, low_core = together(part, low_got, low_core)
    low_partner, grad_qkv_partner, keep, send = run(
        partner_backward_kernel,
        [row_low, heads_low, half_full, half_low],
        decoder, low_got, low_core, qkv_partner, allowed_partner, attn_own,
        flops=10 * ROW_LEN * width * out_width * 2, flag=True, limit=WIDE_LIMIT, scratch=row_scratch,
    )
    (attn_grad,) = run(
        attn_weights_kernel,
        [low_of(width, attn_width)],
        rows_one, rows_partner, grad_qkv, grad_qkv_partner, low_self, low_partner, mixed_one, mixed_partner,
        flops=8 * ROW_LEN * width * out_width, limit=WIDE_LIMIT,
    )
    attn_grad = scatter_ring_plane(attn_grad, ("z", "x"))
    grad_input, sums = run(
        input_backward_kernel,
        [row_full, full_of(8, width)],
        decoder, grad_self, part, swap(part, "c"), *from_partner(keep, send), values, norms,
        sums_last, sums_one_enc, sums_two_dec, flag=True, scratch=row_scratch, limit=WIDE_LIMIT,
    )
    sums = jnp.pad(sums.T, ((0, 0), (0, NORM_COLUMNS - sums.shape[0]))).astype(BFLOAT)
    sums = lax.all_to_all(sums, PLANE, split_axis=0, concat_axis=0, tiled=True)
    sums = jnp.sum(sums.reshape(16, -1, NORM_COLUMNS).astype(FLOAT), axis=0)
    sums = sums + swap(sums, "h")
    decoded, memory, grad_input = together(decoded, memory, grad_input)
    outputs = to_owners(pick(is_decoder, decoded.astype(BFLOAT), memory))
    grad_embedded = to_owners(grad_input)

    rows_cross = cross_query.shape[0]
    (send_h,) = run(
        send_home_kernel, [low_of(2 * rows_cross, 2 * ff_width + half_cross)], decoder, grad_early, flag=True
    )
    send_s, send_across = run(
        send_section_kernel,
        [low_of(rows_cross, cross_width), low_of(rows_cross, cross_width)],
        decoder, grad_early, send_h, flag=True,
    )
    total_up, total_down, total_query, total_keyval, total_cross_out = run(
        bring_home_kernel,
        [
            full_of(1, 2 * rows_cross, ff_width),
            full_of(1, 2 * rows_cross, ff_width),
            full_of(rows_cross, half_cross),
            full_of(rows_cross, cross_width),
            full_of(rows_cross, half_cross),
        ],
        decoder, grad_early, swap(send_h, "h"), swap(send_s, "s"), swap_across(send_across), flag=True,
    )
    total_qkv, total_out, total_gain, total_offset = run(
        attn_home_kernel,
        [
            full_of(1, 2 * rows_cross, qkv_width),
            full_of(1, 2 * rows_cross, out_width),
            full_of(1, 3, 2 * rows_cross),
            full_of(1, 3, 2 * rows_cross),
        ],
        attn_grad, sums,
    )
    return (
        outputs[None],
        grad_embedded[None],
        total_qkv,
        total_out.swapaxes(1, 2),
        total_up,
        total_down.swapaxes(1, 2),
        total_gain,
        total_offset,
        total_query,
        total_keyval,
        total_cross_out.T,
    )


def solution(mesh):
    fine = Mesh(mesh.devices.reshape(2, 4, 4, 2, 2), AXES)
    tokens = ("x", "z", "h", "c")
    tensor = ("h", "c")
    whole = ("s", "x", "z")
    return jax.shard_map(
        shards,
        mesh=fine,
        in_specs=(
            P("s", None, tokens, None),
            P("s", None, tokens, None),
            P(None, None, PLANE, None),
            P("s", PLANE, tensor),
            P("s", tensor, PLANE),
            P("s", PLANE, tensor),
            P("s", tensor, PLANE),
            P("s", None, PLANE),
            P("s", None, PLANE),
            P(whole, tensor),
            P(whole, tensor),
            P(tensor, whole),
        ),
        out_specs=(
            P("s", None, tokens, None),
            P("s", None, tokens, None),
            P("s", PLANE, tensor),
            P("s", tensor, PLANE),
            P("s", PLANE, tensor),
            P("s", tensor, PLANE),
            P("s", None, PLANE),
            P("s", None, PLANE),
            P(whole, tensor),
            P(whole, tensor),
            P(tensor, whole),
        ),
        check_vma=False,
    )
```
